32 devices in a mesh: img: 8 (over z, y), row: 4 (over x, core).
Axes of the slice: x: 2, y: 2, z: 4, core: 2. Of those that a mesh axis runs over, the one named last changes fastest.
Arguments:
- activations: bfloat16 [24, 16, 192, 512], P('img', 'row'), may hold values from -4 to 4
- cotangent: bfloat16 [24, 16, 192, 512], P('img', 'row'), may hold values from -6 to 6
- weights: bfloat16 [3147776], P(('img', 'row')), may hold values from -2 to 2
Outputs:
- block_out: bfloat16 [24, 16, 192, 512], P('img', 'row')
- input_grad: float32 [24, 16, 192, 512], P('img', 'row')
- weight_grad: float32 [3147776], P(('img', 'row'))
- summary_mean: float32 [512], replicated
- summary_var: float32 [512], replicated
The draws below stay inside these ranges and needn't reach their ends.
All inputs are finite; a program needn't handle non-finite values.
Results may differ from the reference program's by a relative error of at most 0.0102.
Values may be sent and summed in bfloat16 or wider, within the bound.
No kernel may reach another device: no remote copies, remote signals or barrier semaphores. Data moves between devices by JAX's collectives and lax.ppermute only.
A program may use at most 256 MiB of HBM per device.

```python
import math
import jax
import jax.numpy as jnp
from jax import lax

D = 512
FF = 2048
HEADS = 8
W = 192
H = 16
IMAGES = 24


def draw_activations(key, part):
    key = jax.random.fold_in(key, 11)
    first_key, second_key, third_key = jax.random.split(key, 3)
    row_pos = jnp.arange(H, dtype=jnp.float32) / max(H - 1, 1)
    image_pos = jnp.arange(IMAGES, dtype=jnp.float32) / max(IMAGES - 1, 1)
    level_sum = image_pos[:, None] + row_pos[None, :]
    row_level = jnp.exp(0.5 * math.log(3.0) * level_sum)
    common = jnp.clip(0.5 * jax.random.normal(first_key, (D,), jnp.float32), -1.0, 1.0)
    row_part = 0.02 * jnp.clip(jax.random.normal(second_key, (IMAGES, H, 1, D), jnp.float32), -2.0, 2.0)
    noise_draw = 0.5 * jnp.clip(jax.random.normal(third_key, (IMAGES, H, W, D), jnp.float32), -4.0, 4.0)
    values = common + row_level[:, :, None, None] * row_part + noise_draw
    return values.astype(jnp.bfloat16)


def draw_weights(key, part):
    key = jax.random.fold_in(key, 23)
    first_key, second_key = jax.random.split(key)
    length_all = 4 * D * D + 2 * D * FF + 4 * D
    position = jnp.arange(length_all, dtype=jnp.int32)
    matrix_start = 4 * D
    random_part = jnp.clip(jax.random.normal(first_key, (length_all,), jnp.float32), -4.0, 4.0)
    gain_draw = jax.random.uniform(second_key, (length_all,), jnp.float32, 0.6, 1.4)
    spread = jnp.where(position < matrix_start + 3 * D * D, 1.0 / math.sqrt(D), jnp.where(position < matrix_start + 4 * D * D, 3.0 / math.sqrt(D), jnp.where(position < matrix_start + 4 * D * D + D * FF, 1.0 / math.sqrt(D), 2.0 / math.sqrt(FF))))
    bias_draw = 0.5 * random_part
    is_bias = (position >= 2 * D) & (position < 3 * D)
    is_vector = position < matrix_start
    values = jnp.where(is_vector, jnp.where(is_bias, bias_draw, gain_draw), random_part * spread)
    return values.astype(jnp.bfloat16)


def block_levels(stream_key, extent, cuts, low, high):
    def one(axis_at, blocks):
        heights = jax.random.uniform(jax.random.fold_in(jax.random.fold_in(stream_key, 6), axis_at), (blocks,), jnp.float32, low / len(cuts), high / len(cuts))
        return jnp.repeat(jnp.exp(heights), extent[axis_at] // blocks).reshape((-1,) + (1,) * (len(extent) - axis_at - 1))

    level = one(*cuts[0])
    for cut in cuts[1:]:
        level = level * one(*cut)
    return level


def bell_draw(rng, shape, width, most, cuts=(), kind=jnp.bfloat16):
    values = jax.random.normal(rng, shape, jnp.float32) * width
    if len(cuts) > 0:
        values = block_levels(rng, shape, cuts, -0.22, 0.18) * values
    return jnp.clip(values, min=-most, max=most).astype(kind)


def setup_inputs(seed: int = 0) -> dict:
    seeds = jax.random.split(jax.random.key(seed), 4)
    activations = draw_activations(jax.random.fold_in(seeds[3], 71), 0)
    cotangent = bell_draw(seeds[1], (IMAGES, H, W, D), 1.0, 6.0, ((0, 8), (1, 4)))
    weights = draw_weights(jax.random.fold_in(seeds[3], 71), 0)
    return {"activations": activations, "cotangent": cotangent, "weights": weights}


@jax.custom_vjp
def low(v):
    return lax.optimization_barrier(v.astype(jnp.bfloat16)).astype(jnp.float32)

@jax.custom_vjp
def low_back(v):
    return v

def low_keep(v):
    return (low(v), None)

def low_pass(kept, grad):
    return (grad,)

def back_keep(v):
    return (v, None)

def back_low(kept, grad):
    return (low(grad),)
low.defvjp(low_keep, low_pass)
low_back.defvjp(back_keep, back_low)
EPS = 1e-05
NEGATIVE = -1e+30

def dense(left, right):
    return jnp.dot(left, right, precision=lax.Precision.HIGHEST)

def unpack(flat_weights, model_width, ff_width):
    lengths = [model_width] * 4 + [model_width * model_width] * 4 + [model_width * ff_width, ff_width * model_width]
    segments = []
    offset = 0
    for length in lengths:
        segments.append(flat_weights[offset:offset + length])
        offset = offset + length
    layouts = [(model_width, model_width)] * 4 + [(model_width, ff_width), (ff_width, model_width)]
    matrices = [segment.reshape(layout) for segment, layout in zip(segments[4:], layouts)]
    return tuple(segments[:4]) + tuple(matrices)

def normalize(values):
    centred = values - lax.optimization_barrier(jnp.mean(values, axis=-1, keepdims=True))
    inverse = lax.rsqrt(lax.optimization_barrier(jnp.mean(centred * centred, axis=-1, keepdims=True)) + EPS)
    return centred * inverse

def image_block(parts, block_in, key_far, value_far):
    gain_one, gain_sum, bias_sum, gain_two, w_query, w_key, w_value, w_out, w_inner, w_outer = parts
    total_rows, columns, model_width = block_in.shape
    head_width = model_width // HEADS
    scaling = 1.0 / math.sqrt(head_width)
    attn_in = low(normalize(block_in) * gain_one)
    query_four = low(low_back(dense(attn_in, w_query))).reshape(total_rows, columns, HEADS, head_width)
    key_four = low(low_back(dense(attn_in, w_key))).reshape(total_rows, columns, HEADS, head_width)
    value_four = low(low_back(dense(attn_in, w_value))).reshape(total_rows, columns, HEADS, head_width)
    key_heads = key_far.reshape(total_rows, HEADS, head_width)
    value_heads = value_far.reshape(total_rows, HEADS, head_width)
    own_scores = jnp.einsum('rqhd,rkhd->rhqk', query_four, key_four, precision=lax.Precision.HIGHEST) * scaling
    far_scores = jnp.einsum('rqhd,shd->rhqs', query_four, key_heads, precision=lax.Precision.HIGHEST) * scaling
    scores = low_back(jnp.concatenate([own_scores, far_scores], axis=-1))
    position = jnp.arange(columns, dtype=jnp.int32)
    row_mask = position[None, :] <= position[:, None]
    row_index = jnp.arange(total_rows, dtype=jnp.int32)
    far_mask = row_index[None, :] < row_index[:, None]
    full_mask = jnp.concatenate([jnp.broadcast_to(row_mask[None, None], (total_rows, 1, columns, columns)), jnp.broadcast_to(far_mask[:, None, None, :], (total_rows, 1, columns, total_rows))], axis=-1)
    scores = jnp.where(full_mask, scores, NEGATIVE)
    top_score = lax.optimization_barrier(jnp.max(scores, axis=-1, keepdims=True))
    exp_scores = jnp.exp(scores - top_score)
    probs_low = low(exp_scores / lax.optimization_barrier(jnp.sum(exp_scores, axis=-1, keepdims=True)))
    mixed_heads = jnp.einsum('rhqk,rkhd->rqhd', probs_low[..., :columns], value_four, precision=lax.Precision.HIGHEST)
    mixed_heads = mixed_heads + jnp.einsum('rhqs,shd->rqhd', probs_low[..., columns:], value_heads, precision=lax.Precision.HIGHEST)
    mixed_low = low(low_back(mixed_heads.reshape(total_rows, columns, model_width)))
    branch = low_back(dense(mixed_low, w_out))
    middle = block_in + branch
    ff_in = low(normalize(middle) * gain_two)
    inner_pre = low_back(dense(ff_in, w_inner))
    activated = low(jax.nn.gelu(inner_pre))
    return middle + dense(activated, w_outer)

def forward(inputs, flat_weights):
    parts = unpack(flat_weights, D, FF)
    gain_sum, bias_sum = (parts[1], parts[2])
    w_key, w_value = (parts[5], parts[6])
    row_means = lax.optimization_barrier(jnp.mean(inputs, axis=2))
    mean_value = lax.optimization_barrier(jnp.mean(row_means, axis=(0, 1)))
    var_value = lax.optimization_barrier(jnp.mean(row_means * row_means, axis=(0, 1))) - mean_value * mean_value
    standard = (row_means - mean_value) * lax.rsqrt(var_value + EPS)
    summary_low = low(standard * gain_sum + bias_sum)
    key_far = low(low_back(dense(summary_low, w_key)))
    value_far = low(low_back(dense(summary_low, w_value)))
    checked = jax.checkpoint(image_block)

    def per_image(carry, item):
        return (carry, checked(parts, item[0], item[1], item[2]))
    carry_out, result = lax.scan(per_image, jnp.zeros((), jnp.float32), (inputs, key_far, value_far))
    return (result, (mean_value, var_value))

def reference(activations, cotangent, weights):
    inputs = activations.astype(jnp.float32)
    flat_weights = weights.astype(jnp.float32)
    result, backward, stats = jax.vjp(forward, inputs, flat_weights, has_aux=True)
    input_grad, weight_grad = backward(cotangent.astype(jnp.float32))
    return (result.astype(jnp.bfloat16), input_grad, weight_grad, stats[0], stats[1])
```

```python
import math

import jax
import jax.numpy as jnp
from jax import lax
from jax.sharding import PartitionSpec as P

FF = 2048
HEADS = 8


EPS = 1e-05
NEGATIVE = -1e30
HALF = jnp.bfloat16
SINGLE = jnp.float32


TAIL = 16


def swap(value, axis, distance):
    size = lax.axis_size(axis)
    return lax.ppermute(value, axis, [(i, i ^ distance) for i in range(size)])


def hops():
    rows, images = lax.axis_size("row"), lax.axis_size("img")
    inner = ("row", 1, 1)
    across = ("row", 2, 2)
    along = ("img", 1, rows)
    outer = []
    distance = images // 2
    while distance > 1:
        outer.append(("img", distance, distance * rows))
        distance //= 2
    distance = rows // 2
    while distance > 2:
        outer.append(("row", distance, distance))
        distance //= 2
    return inner, across, along, outer


def piece_order():
    inner, across, along, outer = hops()
    masks = [0]
    for _, _, mask in outer:
        masks = masks + [m ^ mask for m in masks]
    near = (
        masks
        + [m ^ across[2] for m in masks]
        + [m ^ along[2] for m in masks]
        + [m ^ across[2] ^ along[2] for m in masks]
    )
    return near + [m ^ inner[2] for m in near]


def device_index():
    return lax.axis_index("img") * lax.axis_size("row") + lax.axis_index("row")


def gather_pieces(own):
    inner, across, along, outer = hops()
    held = own[None]
    for axis, distance, _ in outer:
        held = jnp.concatenate([held, swap(held, axis, distance)])
    half = held.shape[0] // 2
    held_x = swap(held, across[0], across[1])
    held_y = swap(held, along[0], along[1])
    corner_first = swap(held_x[:half], along[0], along[1])
    corner_second = swap(held_y[half:], across[0], across[1])
    near = [held, held_x, held_y, corner_first, corner_second]
    far = [swap(part, inner[0], inner[1]) for part in near]
    return jnp.concatenate(near + far)


def scatter_pieces(pieces):
    inner, across, along, outer = hops()

    def add(kept, sent, axis, distance):
        return kept + swap(sent.astype(HALF), axis, distance).astype(SINGLE)

    count = pieces.shape[0] // 2
    near = add(pieces[:count], pieces[count:], inner[0], inner[1])
    quarter = count // 4
    half = quarter // 2
    held, held_x, held_y, corner = (near[i * quarter : (i + 1) * quarter] for i in range(4))
    first = add(
        jnp.concatenate([held[:half], held_x[:half]]),
        jnp.concatenate([held_y[:half], corner[:half]]),
        along[0],
        along[1],
    )
    second = add(
        jnp.concatenate([held[half:], held_y[half:]]),
        jnp.concatenate([held_x[half:], corner[half:]]),
        across[0],
        across[1],
    )
    first = add(first[:half], first[half:], across[0], across[1])
    second = add(second[:half], second[half:], along[0], along[1])
    held = jnp.concatenate([first, second])
    for axis, distance, _ in reversed(outer):
        half = held.shape[0] // 2
        held = add(held[:half], held[half:], axis, distance)
    return held[0]


def sum_everywhere(value):
    inner, across, along, outer = hops()
    for axis, distance, _ in [inner, across, along] + outer[::-1]:
        value = value + swap(value, axis, distance)
    return value


def gather_weights(weights, model_width):
    length = weights.shape[0]
    me = device_index()
    devices = lax.axis_size("img") * lax.axis_size("row")
    block = length // model_width
    rest = length % model_width
    start = TAIL * model_width + rest * me - 4 * model_width
    own = lax.dynamic_update_slice(jnp.zeros(((block + TAIL) * model_width,), HALF), weights, (start,))
    own = own.reshape(block + TAIL, model_width)
    pieces = gather_pieces(own)
    place = [0] * devices
    for at, mask in enumerate(piece_order()):
        place[mask] = at
    order = jnp.asarray(place, jnp.int32)[jnp.arange(devices) ^ me]
    pieces = jnp.take(pieces, order, axis=0, mode="clip")
    tails = jnp.concatenate([pieces[1:, :TAIL], jnp.zeros((1, TAIL, model_width), HALF)])
    body = jnp.concatenate([pieces[:, TAIL:block], pieces[:, block:] + tails], axis=1)
    return pieces[0, TAIL - 4 : TAIL], body.reshape(devices * block, model_width)


def scatter_grads(vectors, rows, length):
    model_width = rows.shape[1]
    me = device_index()
    devices = lax.axis_size("img") * lax.axis_size("row")
    block = length // model_width
    rest = length % model_width
    whole = jnp.concatenate([jnp.zeros((TAIL - 4, model_width), SINGLE), vectors, rows])
    place = jnp.asarray(piece_order(), jnp.int32)
    pieces = jnp.stack([whole[block * s : block * s + block + TAIL] for s in range(devices)])
    pieces = jnp.take(pieces, place ^ me, axis=0, mode="clip")
    mine = scatter_pieces(pieces)
    start = TAIL * model_width + rest * me - 4 * model_width
    return lax.dynamic_slice(mine.reshape(-1), (start,), (length,))


def unpack(vectors, rows, model_width, ff_width):
    matrices = [rows[i * model_width : (i + 1) * model_width] for i in range(4)]
    matrices.append(rows[4 * model_width : 4 * model_width + ff_width].reshape(model_width, ff_width))
    matrices.append(rows[4 * model_width + ff_width :])
    return ([vectors[i].astype(SINGLE) for i in range(4)], matrices)


def normalize(values):
    centred = values - jnp.mean(values, axis=-1, keepdims=True)
    inverse = lax.rsqrt(jnp.mean(centred * centred, axis=-1, keepdims=True) + EPS)
    return (centred * inverse, inverse)


def norm_back(grad_norm, normed, inverse):
    return inverse * (
        grad_norm
        - jnp.mean(grad_norm, axis=-1, keepdims=True)
        - normed * jnp.mean(grad_norm * normed, axis=-1, keepdims=True)
    )


def forward_dot(left, right):
    return jnp.einsum("rwd,de->rwe", left, right, preferred_element_type=SINGLE)


def backward_dot(left, right):
    return jnp.einsum("rwe,de->rwd", left, right, preferred_element_type=SINGLE)


def outer_dot(left, right):
    return jnp.einsum("rwd,rwe->de", left, right, preferred_element_type=SINGLE)


def attention_probs(query_four, key_four, key_heads, row_mask, far_mask, scaling):
    own_scores = (
        jnp.einsum("rqhd,rkhd->rhqk", query_four, key_four, preferred_element_type=SINGLE) * scaling
    )
    far_scores = (
        jnp.einsum("rqhd,shd->rhqs", query_four, key_heads, preferred_element_type=SINGLE) * scaling
    )
    own_scores = jnp.where(row_mask[None, None], own_scores, NEGATIVE)
    far_scores = jnp.where(far_mask[:, None, None, :], far_scores, NEGATIVE)
    top_score = jnp.maximum(
        jnp.max(own_scores, axis=-1, keepdims=True), jnp.max(far_scores, axis=-1, keepdims=True)
    )
    own_exp = jnp.exp(own_scores - top_score)
    far_exp = jnp.exp(far_scores - top_score)
    exp_total = jnp.sum(own_exp, axis=-1, keepdims=True) + jnp.sum(far_exp, axis=-1, keepdims=True)
    return (own_exp / exp_total, far_exp / exp_total)


def per_device(activations, cotangent, weights):
    images, local_rows, columns, model_width = activations.shape
    head_width = model_width // HEADS
    scaling = 1.0 / math.sqrt(head_width)
    total_rows = local_rows * lax.axis_size("row")
    first_row = lax.axis_index("row") * local_rows
    summary_count = float(images * lax.axis_size("img") * total_rows)
    vectors, matrices = unpack(*gather_weights(weights, model_width), model_width, FF)
    gain_one, gain_sum, bias_sum, gain_two = vectors
    w_query, w_key, w_value, w_out, w_inner, w_outer = matrices
    row_means = jnp.mean(activations.astype(SINGLE), axis=2)
    local_first = jnp.sum(row_means, axis=(0, 1))
    local_second = jnp.sum(row_means * row_means, axis=(0, 1))
    total_first, total_second = sum_everywhere(jnp.stack([local_first, local_second]))
    summary_mean = total_first / summary_count
    summary_var = total_second / summary_count - summary_mean * summary_mean
    summary_inv = lax.rsqrt(summary_var + EPS)
    standard = (row_means - summary_mean) * summary_inv
    summary_low = (standard * gain_sum + bias_sum).astype(HALF)
    key_local = forward_dot(summary_low, w_key).astype(HALF)
    value_local = forward_dot(summary_low, w_value).astype(HALF)
    key_all, value_all = (
        lax.all_gather(key_local, "row", axis=1, tiled=True),
        lax.all_gather(value_local, "row", axis=1, tiled=True),
    )
    position = lax.broadcasted_iota(jnp.int32, (columns, columns), 0)
    key_position = lax.broadcasted_iota(jnp.int32, (columns, columns), 1)
    row_mask = key_position <= position
    global_rows = first_row + jnp.arange(local_rows, dtype=jnp.int32)
    far_mask = jnp.arange(total_rows, dtype=jnp.int32)[None, :] < global_rows[:, None]
    kept_values = []
    outputs = []
    for image_index in range(images):
        block_in = activations[image_index].astype(SINGLE)
        normed_one, inverse_one = normalize(block_in)
        attn_in = (normed_one * gain_one).astype(HALF)
        four_shape = (local_rows, columns, HEADS, head_width)
        query_four = forward_dot(attn_in, w_query).astype(HALF).reshape(four_shape)
        key_four = forward_dot(attn_in, w_key).astype(HALF).reshape(four_shape)
        value_four = forward_dot(attn_in, w_value).astype(HALF).reshape(four_shape)
        key_heads = key_all[image_index].reshape(total_rows, HEADS, head_width)
        value_heads = value_all[image_index].reshape(total_rows, HEADS, head_width)
        own_prob, far_prob = attention_probs(
            query_four, key_four, key_heads, row_mask, far_mask, scaling
        )
        own_low = own_prob.astype(HALF)
        far_low = far_prob.astype(HALF)
        mixed_heads = jnp.einsum(
            "rhqk,rkhd->rqhd", own_low, value_four, preferred_element_type=SINGLE
        )
        mixed_heads = mixed_heads + jnp.einsum(
            "rhqs,shd->rqhd", far_low, value_heads, preferred_element_type=SINGLE
        )
        mixed_low = mixed_heads.reshape(local_rows, columns, model_width).astype(HALF)
        middle = block_in + forward_dot(mixed_low, w_out)
        normed_two, inverse_two = normalize(middle)
        ff_in = (normed_two * gain_two).astype(HALF)
        inner_pre = forward_dot(ff_in, w_inner)
        activated = jax.nn.gelu(inner_pre).astype(HALF)
        outputs.append((middle + forward_dot(activated, w_outer)).astype(HALF))
        kept_values.append(
            (
                normed_one,
                inverse_one,
                attn_in,
                query_four,
                key_four,
                value_four,
                own_prob,
                far_prob,
                mixed_low,
                normed_two,
                inverse_two,
                ff_in,
                inner_pre,
                activated,
            )
        )
    grad_gain_one = jnp.zeros((model_width,), SINGLE)
    grad_gain_two = jnp.zeros((model_width,), SINGLE)
    grad_query_w = jnp.zeros((model_width, model_width), SINGLE)
    grad_key_w = jnp.zeros((model_width, model_width), SINGLE)
    grad_value_w = jnp.zeros((model_width, model_width), SINGLE)
    grad_out_w = jnp.zeros((model_width, model_width), SINGLE)
    grad_inner_w = jnp.zeros((model_width, FF), SINGLE)
    grad_outer_w = jnp.zeros((FF, model_width), SINGLE)
    key_far_grads = []
    value_far_grads = []
    partial_inputs = []
    for image_index in range(images):
        (
            normed_one,
            inverse_one,
            attn_in,
            query_four,
            key_four,
            value_four,
            own_prob,
            far_prob,
            mixed_low,
            normed_two,
            inverse_two,
            ff_in,
            inner_pre,
            activated,
        ) = kept_values[image_index]
        key_heads = key_all[image_index].reshape(total_rows, HEADS, head_width)
        value_heads = value_all[image_index].reshape(total_rows, HEADS, head_width)
        out_grad = cotangent[image_index]
        grad_outer_w = grad_outer_w + outer_dot(activated, out_grad)
        act_grad = backward_dot(out_grad, w_outer)
        gelu_value, gelu_back = jax.vjp(jax.nn.gelu, inner_pre)
        inner_grad = gelu_back(act_grad)[0].astype(HALF)
        grad_inner_w = grad_inner_w + outer_dot(ff_in, inner_grad)
        ff_grad = backward_dot(inner_grad, w_inner)
        grad_gain_two = grad_gain_two + jnp.sum(ff_grad * normed_two, axis=(0, 1))
        middle_grad = out_grad.astype(SINGLE) + norm_back(
            ff_grad * gain_two, normed_two, inverse_two
        )
        branch_grad = middle_grad.astype(HALF)
        grad_out_w = grad_out_w + outer_dot(mixed_low, branch_grad)
        mixed_grad = (
            backward_dot(branch_grad, w_out)
            .astype(HALF)
            .reshape(local_rows, columns, HEADS, head_width)
        )
        own_dp = jnp.einsum(
            "rqhd,rkhd->rhqk", mixed_grad, value_four, preferred_element_type=SINGLE
        )
        far_dp = jnp.einsum(
            "rqhd,shd->rhqs", mixed_grad, value_heads, preferred_element_type=SINGLE
        )
        inner_sum = jnp.sum(own_dp * own_prob, axis=-1, keepdims=True) + jnp.sum(
            far_dp * far_prob, axis=-1, keepdims=True
        )
        own_dz = (own_prob * (own_dp - inner_sum)).astype(HALF)
        far_dz = (far_prob * (far_dp - inner_sum)).astype(HALF)
        query_grad = (
            jnp.einsum("rhqk,rkhd->rqhd", own_dz, key_four, preferred_element_type=SINGLE)
            + jnp.einsum("rhqs,shd->rqhd", far_dz, key_heads, preferred_element_type=SINGLE)
        ) * scaling
        key_grad = (
            jnp.einsum("rhqk,rqhd->rkhd", own_dz, query_four, preferred_element_type=SINGLE)
            * scaling
        )
        value_grad = jnp.einsum(
            "rhqk,rqhd->rkhd", own_prob.astype(HALF), mixed_grad, preferred_element_type=SINGLE
        )
        key_far_grads.append(
            (
                jnp.einsum("rhqs,rqhd->shd", far_dz, query_four, preferred_element_type=SINGLE)
                * scaling
            ).reshape(total_rows, model_width)
        )
        value_far_grads.append(
            jnp.einsum(
                "rhqs,rqhd->shd", far_prob.astype(HALF), mixed_grad, preferred_element_type=SINGLE
            ).reshape(total_rows, model_width)
        )
        flat_shape = (local_rows, columns, model_width)
        query_low = query_grad.astype(HALF).reshape(flat_shape)
        key_low = key_grad.astype(HALF).reshape(flat_shape)
        value_low = value_grad.astype(HALF).reshape(flat_shape)
        grad_query_w = grad_query_w + outer_dot(attn_in, query_low)
        grad_key_w = grad_key_w + outer_dot(attn_in, key_low)
        grad_value_w = grad_value_w + outer_dot(attn_in, value_low)
        attn_grad = (
            backward_dot(query_low, w_query)
            + backward_dot(key_low, w_key)
            + backward_dot(value_low, w_value)
        )
        grad_gain_one = grad_gain_one + jnp.sum(attn_grad * normed_one, axis=(0, 1))
        partial_inputs.append(
            middle_grad + norm_back(attn_grad * gain_one, normed_one, inverse_one)
        )
    key_far_total, value_far_total = (
        lax.psum_scatter(
            jnp.stack(key_far_grads).astype(jnp.bfloat16), "row", scatter_dimension=1, tiled=True
        ).astype(jnp.float32),
        lax.psum_scatter(
            jnp.stack(value_far_grads).astype(jnp.bfloat16), "row", scatter_dimension=1, tiled=True
        ).astype(jnp.float32),
    )
    key_far_low = key_far_total.astype(HALF)
    value_far_low = value_far_total.astype(HALF)
    grad_key_w = grad_key_w + outer_dot(summary_low, key_far_low)
    grad_value_w = grad_value_w + outer_dot(summary_low, value_far_low)
    summary_grad = backward_dot(key_far_low, w_key) + backward_dot(value_far_low, w_value)
    grad_gain_sum = jnp.sum(summary_grad * standard, axis=(0, 1))
    grad_bias_sum = jnp.sum(summary_grad, axis=(0, 1))
    standard_grad = summary_grad * gain_sum
    plain_total, cross_total = sum_everywhere(
        jnp.stack([jnp.sum(standard_grad, axis=(0, 1)), jnp.sum(standard_grad * standard, axis=(0, 1))])
    )
    mean_grad = summary_inv * (
        standard_grad - plain_total / summary_count - standard * (cross_total / summary_count)
    )
    input_grad = jnp.stack(partial_inputs) + mean_grad[:, :, None, :] / columns
    vectors = jnp.stack([grad_gain_one, grad_gain_sum, grad_bias_sum, grad_gain_two])
    rows = jnp.concatenate(
        [
            grad_query_w,
            grad_key_w,
            grad_value_w,
            grad_out_w,
            grad_inner_w.reshape(-1, model_width),
            grad_outer_w,
        ]
    )
    weight_grad = scatter_grads(vectors, rows, weights.shape[0])
    return (jnp.stack(outputs), input_grad, weight_grad, summary_mean, summary_var)


def solution(mesh):
    placed = (P("img", "row", None, None), P("img", "row", None, None), P(("img", "row")))
    return jax.shard_map(
        per_device,
        mesh=mesh,
        in_specs=placed,
        out_specs=(
            P("img", "row", None, None),
            P("img", "row", None, None),
            P(("img", "row")),
            P(),
            P(),
        ),
        check_vma=False,
    )
```

```python
import functools
import math

import jax
import jax.numpy as jnp
from jax import lax
from jax.experimental import pallas as pl
from jax.experimental.pallas import tpu as pltpu
from jax.sharding import PartitionSpec as P

FF = 2048
HEADS = 8
LANES = 128


EPS = 1e-05
NEGATIVE = -1e30
HALF = jnp.bfloat16
SINGLE = jnp.float32
VMEM_BYTES = 56 * 1024 * 1024

TAIL = 16


def swap(value, axis, distance):
    size = lax.axis_size(axis)
    return lax.ppermute(value, axis, [(i, i ^ distance) for i in range(size)])


def hops():
    rows, images = lax.axis_size("row"), lax.axis_size("img")
    inner = ("row", 1, 1)
    across = ("row", 2, 2)
    along = ("img", 1, rows)
    outer = []
    distance = images // 2
    while distance > 1:
        outer.append(("img", distance, distance * rows))
        distance //= 2
    distance = rows // 2
    while distance > 2:
        outer.append(("row", distance, distance))
        distance //= 2
    return inner, across, along, outer


def piece_order():
    inner, across, along, outer = hops()
    masks = [0]
    for _, _, mask in outer:
        masks = masks + [m ^ mask for m in masks]
    near = (
        masks
        + [m ^ across[2] for m in masks]
        + [m ^ along[2] for m in masks]
        + [m ^ across[2] ^ along[2] for m in masks]
    )
    return near + [m ^ inner[2] for m in near]


def device_index():
    return lax.axis_index("img") * lax.axis_size("row") + lax.axis_index("row")


def gather_pieces(own):
    inner, across, along, outer = hops()
    held = own[None]
    for axis, distance, _ in outer:
        held = jnp.concatenate([held, swap(held, axis, distance)])
    half = held.shape[0] // 2
    held_x = swap(held, across[0], across[1])
    held_y = swap(held, along[0], along[1])
    corner_first = swap(held_x[:half], along[0], along[1])
    corner_second = swap(held_y[half:], across[0], across[1])
    near = [held, held_x, held_y, corner_first, corner_second]
    far = [swap(part, inner[0], inner[1]) for part in near]
    return jnp.concatenate(near + far)


def scatter_pieces(pieces):
    inner, across, along, outer = hops()

    def add(kept, sent, axis, distance):
        return kept + swap(sent.astype(HALF), axis, distance).astype(SINGLE)

    count = pieces.shape[0] // 2
    near = add(pieces[:count], pieces[count:], inner[0], inner[1])
    quarter = count // 4
    half = quarter // 2
    held, held_x, held_y, corner = (near[i * quarter : (i + 1) * quarter] for i in range(4))
    first = add(
        jnp.concatenate([held[:half], held_x[:half]]),
        jnp.concatenate([held_y[:half], corner[:half]]),
        along[0],
        along[1],
    )
    second = add(
        jnp.concatenate([held[half:], held_y[half:]]),
        jnp.concatenate([held_x[half:], corner[half:]]),
        across[0],
        across[1],
    )
    first = add(first[:half], first[half:], across[0], across[1])
    second = add(second[:half], second[half:], along[0], along[1])
    held = jnp.concatenate([first, second])
    for axis, distance, _ in reversed(outer):
        half = held.shape[0] // 2
        held = add(held[:half], held[half:], axis, distance)
    return held[0]


def row_hops():
    inner, across, _, outer = hops()
    return [inner, across] + [hop for hop in outer if hop[0] == "row"]


def image_hops():
    _, _, along, outer = hops()
    return [along] + [hop for hop in outer if hop[0] == "img"]


def gather_rows(own, shown):
    width = own.shape[-1]
    count = shown.shape[0]
    held, masks = own[None], [0]
    for axis, distance, mask in row_hops():
        got = swap(jnp.concatenate([held.reshape(-1, width), shown]), axis, distance)
        held = jnp.concatenate([held, got[:-count].reshape(held.shape)])
        shown = shown + got[-count:]
        masks = masks + [m ^ mask for m in masks]
    place = [0] * len(masks)
    for at, mask in enumerate(masks):
        place[mask] = at
    order = jnp.asarray(place, jnp.int32)[jnp.arange(len(masks)) ^ lax.axis_index("row")]
    held = jnp.moveaxis(jnp.take(held, order, axis=0, mode="clip"), 0, 1)
    return held.reshape(own.shape[0], -1, width), shown


def gather_weights(weights, model_width):
    length = weights.shape[0]
    me = device_index()
    devices = lax.axis_size("img") * lax.axis_size("row")
    block = length // model_width
    rest = length % model_width
    start = TAIL * model_width + rest * me - 4 * model_width
    own = lax.dynamic_update_slice(jnp.zeros(((block + TAIL) * model_width,), HALF), weights, (start,))
    own = own.reshape(block + TAIL, model_width)
    pieces = gather_pieces(own)
    place = [0] * devices
    for at, mask in enumerate(piece_order()):
        place[mask] = at
    order = jnp.asarray(place, jnp.int32)[jnp.arange(devices) ^ me]
    pieces = jnp.take(pieces, order, axis=0, mode="clip")
    tails = jnp.concatenate([pieces[1:, :TAIL], jnp.zeros((1, TAIL, model_width), HALF)])
    body = jnp.concatenate([pieces[:, TAIL:block], pieces[:, block:] + tails], axis=1)
    return pieces[0, TAIL - 4 : TAIL], body.reshape(devices * block, model_width)


def scatter_grads(vectors, rows, length):
    model_width = rows.shape[1]
    me = device_index()
    devices = lax.axis_size("img") * lax.axis_size("row")
    block = length // model_width
    rest = length % model_width
    whole = jnp.concatenate([jnp.zeros((TAIL - 4, model_width), SINGLE), vectors, rows])
    place = jnp.asarray(piece_order(), jnp.int32)
    pieces = jnp.stack([whole[block * s : block * s + block + TAIL] for s in range(devices)])
    pieces = jnp.take(pieces, place ^ me, axis=0, mode="clip")
    mine = scatter_pieces(pieces)
    start = TAIL * model_width + rest * me - 4 * model_width
    return lax.dynamic_slice(mine.reshape(-1), (start,), (length,))


def unpack(rows, model_width, ff_width):
    w_qkv = jnp.concatenate([rows[i * model_width : (i + 1) * model_width] for i in range(3)], axis=1)
    w_out = rows[3 * model_width : 4 * model_width]
    w_inner = rows[4 * model_width : 4 * model_width + ff_width].reshape(model_width, ff_width)
    w_outer = rows[4 * model_width + ff_width :]
    return (w_qkv, w_out, w_inner, w_outer)


def dot(left, right):
    return jnp.dot(left, right, preferred_element_type=SINGLE)


def dot_rows(left, right):
    return lax.dot_general(left, right, (((1,), (1,)), ((), ())), preferred_element_type=SINGLE)


def dot_outer(left, right):
    return lax.dot_general(left, right, (((0,), (0,)), ((), ())), preferred_element_type=SINGLE)


def normalize(values):
    centred = values - jnp.mean(values, axis=-1, keepdims=True)
    inverse = lax.rsqrt(jnp.mean(centred * centred, axis=-1, keepdims=True) + EPS)
    return (centred * inverse, inverse)


def norm_back(grad_norm, normed, inverse):
    return inverse * (
        grad_norm
        - jnp.mean(grad_norm, axis=-1, keepdims=True)
        - normed * jnp.mean(grad_norm * normed, axis=-1, keepdims=True)
    )


def whole_block(shape):
    return pl.BlockSpec(shape, lambda *_: (0,) * len(shape), pipeline_mode=pl.Buffered(1))


def head_keys(rows_per_step, model_width):
    return [
        (row, pair, half)
        for row in range(rows_per_step)
        for pair in range(model_width // LANES)
        for half in range(2)
    ]


def attention_forward_kernel(
    scaling,
    rows_per_step,
    local_rows,
    first_row_ref,
    block_ref,
    gain_ref,
    w_ref,
    key_far_ref,
    value_far_ref,
    causal_ref,
    query_ref,
    key_ref,
    value_ref,
    mixed_ref,
    probs_ref,
):
    columns = causal_ref.shape[0]
    far = key_far_ref.shape[0]
    width = block_ref.shape[1]
    head_width = width // HEADS
    step = pl.program_id(0)
    normed, _ = normalize(block_ref[...].astype(SINGLE))
    attn_in = (normed * gain_ref[...]).astype(HALF)
    for i, ref in enumerate((query_ref, key_ref, value_ref)):
        ref[...] = dot(attn_in, w_ref[:, i * width : (i + 1) * width]).astype(HALF)
    first_half = lax.broadcasted_iota(jnp.int32, (columns + far, LANES), 1) < head_width
    far_index = lax.broadcasted_iota(jnp.int32, (far, columns), 0)
    keys = head_keys(rows_per_step, width)
    for start in range(0, len(keys), HEADS):
        group = keys[start : start + HEADS]
        scores, low, mixed = {}, {}, {}
        for row, pair, half in group:
            global_row = first_row_ref[0] + lax.rem(step * rows_per_step + row, local_rows)
            far_bias = jnp.where(far_index < global_row, 0.0, NEGATIVE)
            tokens = slice(row * columns, (row + 1) * columns)
            lanes = slice(pair * LANES, (pair + 1) * LANES)
            all_keys = jnp.concatenate([key_ref[tokens, lanes], key_far_ref[:, lanes]], axis=0)
            one_head = jnp.where(
                first_half if half == 0 else ~first_half, all_keys, jnp.zeros_like(all_keys)
            )
            found = dot_rows(one_head, query_ref[tokens, lanes])
            scores[row, pair, half] = jnp.concatenate(
                [found[:columns] + causal_ref[...], found[columns:] + far_bias], axis=0
            )
        for row, pair, half in group:
            found = scores.pop((row, pair, half))
            top = jnp.max(found, axis=0, keepdims=True)
            powers = jnp.exp((found - top) * scaling)
            inverse = 1.0 / jnp.sum(powers, axis=0, keepdims=True)
            low[row, pair, half] = (powers * inverse).astype(HALF)
            probs_ref[row, 2 * pair + half] = low[row, pair, half]
        for row, pair, half in group:
            tokens = slice(row * columns, (row + 1) * columns)
            lanes = slice(pair * LANES, (pair + 1) * LANES)
            all_values = jnp.concatenate([value_ref[tokens, lanes], value_far_ref[:, lanes]], axis=0)
            turned = all_values.T[half * head_width : (half + 1) * head_width]
            mixed[row, pair, half] = dot(turned, low[row, pair, half])
        for row, pair, half in group:
            if half == 0:
                tokens = slice(row * columns, (row + 1) * columns)
                lanes = slice(pair * LANES, (pair + 1) * LANES)
                both = jnp.concatenate([mixed[row, pair, 0], mixed[row, pair, 1]], axis=0)
                mixed_ref[tokens, lanes] = both.T.astype(HALF)


def chain_call(kernel, image, previous, scalars, inputs, in_specs, out_specs, out_shape, steps, cost, name):
    count = len(out_shape)
    aliases = {}
    if previous is not None:
        aliases = {len(scalars) + len(inputs) + i: i for i in range(count)}
        inputs = inputs + list(previous)
        in_specs = in_specs + [pl.BlockSpec(memory_space=pl.ANY)] * count

    def body(*refs):
        kept = len(scalars) + len(in_specs)
        fixed = kept - (count if previous is not None else 0)
        kernel(*refs[:fixed], *refs[kept:])

    return pl.pallas_call(
        body,
        grid_spec=pltpu.PrefetchScalarGridSpec(
            num_scalar_prefetch=len(scalars), grid=(steps,), in_specs=in_specs, out_specs=out_specs
        ),
        out_shape=out_shape,
        input_output_aliases=aliases,
        compiler_params=pltpu.CompilerParams(vmem_limit_bytes=VMEM_BYTES),
        cost_estimate=cost,
        name=name,
    )(*scalars, *inputs)


def attention_forward(
    image, previous, block_in, gain, w_qkv, key_far, value_far, first_row, local_rows, columns
):
    tokens, width = block_in.shape
    images, far, _ = key_far.shape
    rows_per_step = math.gcd(local_rows, 2)
    steps = local_rows // rows_per_step
    size = rows_per_step * columns
    position = jnp.arange(columns)
    causal = jnp.where(position[:, None] <= position[None, :], 0.0, NEGATIVE).astype(SINGLE)
    block = pl.BlockSpec((size, width), lambda i, _: (image * steps + i, 0))
    far_block = pl.BlockSpec((None, far, width), lambda i, _: (image, 0, 0))
    probs_block = pl.BlockSpec(
        (rows_per_step, HEADS, columns + far, columns), lambda i, _: (image * steps + i, 0, 0, 0)
    )
    low = jax.ShapeDtypeStruct((tokens, width), HALF)
    part = tokens // images
    return chain_call(
        functools.partial(
            attention_forward_kernel, 1.0 / math.sqrt(width // HEADS), rows_per_step, local_rows
        ),
        image,
        previous,
        [first_row],
        [block_in, gain, w_qkv, key_far, value_far, causal],
        [
            block,
            whole_block((1, width)),
            whole_block((width, 3 * width)),
            far_block,
            far_block,
            whole_block((columns, columns)),
        ],
        [block] * 4 + [probs_block],
        [low] * 4 + [jax.ShapeDtypeStruct((images * local_rows, HEADS, columns + far, columns), HALF)],
        steps,
        pl.CostEstimate(
            flops=part * width * (6 * width + 8 * (columns + far)),
            bytes_accessed=part * width * 12 + part * HEADS * (columns + far) * 2,
            transcendentals=part * HEADS * (columns + far),
        ),
        "attention_forward",
    )


GELU_OUTER = math.sqrt(2.0 / math.pi)
GELU_CUBE = 0.044715


def gelu_and_slope(value):
    square = value * value
    gate = 0.5 * jnp.tanh(value * (GELU_OUTER * GELU_CUBE * square + GELU_OUTER)) + 0.5
    activated = value * gate
    slope = gate + activated * (1.0 - gate) * (6.0 * GELU_OUTER * GELU_CUBE * square + 2.0 * GELU_OUTER)
    return (activated, slope)


def start_pieces(plan, flat_ref, outs, sems, index):
    copies = []
    for i, (out, place, offset, rows) in enumerate(plan):
        source = flat_ref.at[pl.ds(pl.multiple_of(offset(index), TAIL), rows)]
        target = outs[out].at[place] if place else outs[out]
        copies.append(pltpu.make_async_copy(source, target, sems.at[i]))
    for copy in copies:
        copy.start()
    return copies


def feed_forward_kernel(
    chunk,
    plan,
    index_ref,
    block_ref,
    mixed_ref,
    cotangent_ref,
    gain_ref,
    w_out_ref,
    w_inner_ref,
    w_outer_ref,
    out_ref,
    middle_grad_ref,
    mixed_grad_ref,
    grad_gain_ref,
    *rest,
):
    *pieces, grad_out_ref, grad_inner_ref, grad_outer_ref, flat_ref, sems = rest

    @pl.when(pl.program_id(0) == 0)
    def _():
        for ref in (grad_out_ref, grad_inner_ref, grad_outer_ref, grad_gain_ref):
            ref[...] = jnp.zeros_like(ref)

    mixed = mixed_ref[...]
    cotangent = cotangent_ref[...]
    middle = block_ref[...].astype(SINGLE) + dot(mixed, w_out_ref[...])
    normed, inverse = normalize(middle)
    ff_in = (normed * gain_ref[...]).astype(HALF)
    out = middle
    ff_grad = jnp.zeros_like(middle)
    cotangent_turned = cotangent.T
    ff_turned = ff_in.T
    width, hidden = w_inner_ref.shape
    count = hidden // chunk
    spans = [slice(j * chunk, (j + 1) * chunk) for j in range(count)]

    def products(j):
        return (dot(ff_in, w_inner_ref[:, spans[j]]), dot_rows(cotangent, w_outer_ref[spans[j], :]))

    ready = products(0)
    for j in range(count):
        inner, act_grad = ready
        if j + 1 < count:
            ready = products(j + 1)
        activated, slope = gelu_and_slope(inner)
        activated = activated.astype(HALF)
        inner_grad = (slope * act_grad).astype(HALF)
        out = out + dot(activated, w_outer_ref[spans[j], :])
        ff_grad = ff_grad + dot_rows(inner_grad, w_inner_ref[:, spans[j]])
        grad_inner_ref[:, spans[j]] += dot(ff_turned, inner_grad)
        grad_outer_ref[:, spans[j]] += dot(cotangent_turned, activated)
    out_ref[...] = out.astype(HALF)
    grad_gain_ref[...] += jnp.sum(ff_grad * normed, axis=0, keepdims=True)
    middle_grad = cotangent.astype(SINGLE) + norm_back(ff_grad * gain_ref[...], normed, inverse)
    middle_grad_ref[...] = middle_grad
    branch_grad = middle_grad.astype(HALF)
    mixed_grad_ref[...] = dot_rows(branch_grad, w_out_ref[...]).astype(HALF)
    grad_out_ref[...] += dot_outer(mixed, branch_grad)

    @pl.when(pl.program_id(0) == pl.num_programs(0) - 1)
    def _():
        groups = hidden // width
        flat_ref[:TAIL] = jnp.zeros((TAIL, width), HALF)
        flat_ref[TAIL : TAIL + width] = grad_out_ref[...].astype(HALF)
        per = 256 // groups
        mix = weave(groups, per)
        for c in range(width // per):
            parts = [
                grad_inner_ref[c * per : (c + 1) * per, g * width : (g + 1) * width].astype(HALF)
                for g in range(groups)
            ]
            start = TAIL + width + c * groups * per
            woven = dot(mix, jnp.concatenate(parts, axis=0))
            flat_ref[start : start + groups * per] = woven.astype(HALF)
        start = TAIL + width + hidden
        for j in range(hidden // width):
            turned = grad_outer_ref[:, j * width : (j + 1) * width].astype(HALF).T
            flat_ref[start + j * width : start + (j + 1) * width] = turned
        for copy in start_pieces(plan, flat_ref, pieces, sems, index_ref[0]):
            copy.wait()


def weave(groups, per):
    size = groups * per
    row = lax.broadcasted_iota(jnp.int32, (size, size), 0)
    column = lax.broadcasted_iota(jnp.int32, (size, size), 1)
    wanted = lax.rem(row, groups) * per + lax.div(row, groups)
    return (wanted == column).astype(SINGLE).astype(HALF)


def piece_outputs(shapes):
    return (
        [pl.BlockSpec(memory_space=pl.ANY)] * len(shapes),
        [jax.ShapeDtypeStruct(shape, HALF) for shape in shapes],
    )


def feed_forward(index, block_in, mixed, cotangent, gain, w_out, w_inner, w_outer, size, plan, shapes):
    tokens, width = block_in.shape
    hidden = w_inner.shape[1]
    block = pl.BlockSpec((size, width), lambda i, _: (i, 0))
    piece_specs, piece_shapes = piece_outputs(shapes)
    return pl.pallas_call(
        functools.partial(feed_forward_kernel, 512, plan),
        grid_spec=pltpu.PrefetchScalarGridSpec(
            num_scalar_prefetch=1,
            grid=(tokens // size,),
            in_specs=[
                block,
                block,
                block,
                whole_block((1, width)),
                whole_block((width, width)),
                whole_block((width, hidden)),
                whole_block((hidden, width)),
            ],
            out_specs=[block, block, block, whole_block((1, width))] + piece_specs,
            scratch_shapes=[
                pltpu.VMEM((width, width), SINGLE),
                pltpu.VMEM((width, hidden), SINGLE),
                pltpu.VMEM((width, hidden), SINGLE),
                pltpu.VMEM((TAIL + width + 2 * hidden, width), HALF),
                pltpu.SemaphoreType.DMA((len(plan),)),
            ],
        ),
        out_shape=[
            jax.ShapeDtypeStruct((tokens, width), HALF),
            jax.ShapeDtypeStruct((tokens, width), SINGLE),
            jax.ShapeDtypeStruct((tokens, width), HALF),
            jax.ShapeDtypeStruct((1, width), SINGLE),
        ]
        + piece_shapes,
        compiler_params=pltpu.CompilerParams(vmem_limit_bytes=VMEM_BYTES),
        cost_estimate=pl.CostEstimate(
            flops=tokens * width * (6 * width + 12 * hidden),
            bytes_accessed=tokens * width * 14 + width * hidden * 8,
            transcendentals=tokens * hidden,
        ),
        name="feed_forward",
    )(index, block_in, mixed, cotangent, gain, w_out, w_inner, w_outer)


def attention_backward_kernel(
    scaling,
    rows_per_step,
    query_ref,
    key_ref,
    value_ref,
    key_far_ref,
    value_far_ref,
    probs_ref,
    mixed_grad_ref,
    query_grad_ref,
    key_grad_ref,
    value_grad_ref,
    key_far_grad_ref,
    value_far_grad_ref,
):
    width = query_ref.shape[1]
    head_width = width // HEADS
    far = key_far_ref.shape[0]
    columns = query_ref.shape[0] // rows_per_step

    @pl.when(pl.program_id(0) == 0)
    def _():
        key_far_grad_ref[...] = jnp.zeros_like(key_far_grad_ref)
        value_far_grad_ref[...] = jnp.zeros_like(value_far_grad_ref)

    first_half = lax.broadcasted_iota(jnp.int32, (columns + far, LANES), 1) < head_width
    keys = head_keys(rows_per_step, width)
    for start in range(0, len(keys), HEADS):
        group = keys[start : start + HEADS]
        prob_grad, score_grad, value_grad, key_grad, query_grad = {}, {}, {}, {}, {}
        for row, pair, half in group:
            tokens = slice(row * columns, (row + 1) * columns)
            lanes = slice(pair * LANES, (pair + 1) * LANES)
            all_values = jnp.concatenate([value_ref[tokens, lanes], value_far_ref[:, lanes]], axis=0)
            one_head = jnp.where(
                first_half if half == 0 else ~first_half, all_values, jnp.zeros_like(all_values)
            )
            prob_grad[row, pair, half] = dot_rows(one_head, mixed_grad_ref[tokens, lanes])
        for row, pair, half in group:
            tokens = slice(row * columns, (row + 1) * columns)
            lanes = slice(pair * LANES, (pair + 1) * LANES)
            value_grad[row, pair, half] = dot(
                probs_ref[row, 2 * pair + half], mixed_grad_ref[tokens, lanes]
            )
        for row, pair, half in group:
            probs = probs_ref[row, 2 * pair + half].astype(SINGLE)
            grad = prob_grad.pop((row, pair, half))
            total = jnp.sum(probs * grad, axis=0, keepdims=True)
            score_grad[row, pair, half] = (probs * (grad - total)).astype(HALF)
        for row, pair, half in group:
            tokens = slice(row * columns, (row + 1) * columns)
            lanes = slice(pair * LANES, (pair + 1) * LANES)
            key_grad[row, pair, half] = dot(score_grad[row, pair, half], query_ref[tokens, lanes])
            all_keys = jnp.concatenate([key_ref[tokens, lanes], key_far_ref[:, lanes]], axis=0)
            turned = all_keys.T[half * head_width : (half + 1) * head_width]
            query_grad[row, pair, half] = dot(turned, score_grad[row, pair, half])
        for row, pair, half in group:
            if half == 0:
                tokens = slice(row * columns, (row + 1) * columns)
                lanes = slice(pair * LANES, (pair + 1) * LANES)
                first, second = (row, pair, 0), (row, pair, 1)
                value_both = jnp.where(first_half, value_grad[first], value_grad[second])
                key_both = jnp.where(first_half, key_grad[first], key_grad[second]) * scaling
                value_grad_ref[tokens, lanes] = value_both[:columns].astype(HALF)
                key_grad_ref[tokens, lanes] = key_both[:columns].astype(HALF)
                value_far_grad_ref[:, lanes] += value_both[columns:]
                key_far_grad_ref[:, lanes] += key_both[columns:]
                query_both = jnp.concatenate([query_grad[first], query_grad[second]], axis=0) * scaling
                query_grad_ref[tokens, lanes] = query_both.T.astype(HALF)


def attention_backward(
    image, previous, query, key, value, key_far, value_far, probs, mixed_grad, local_rows, columns
):
    tokens, width = query.shape
    images, far, _ = key_far.shape
    rows_per_step = math.gcd(local_rows, 2)
    steps = local_rows // rows_per_step
    size = rows_per_step * columns
    part = tokens // images
    block = pl.BlockSpec((size, width), lambda i: (image * steps + i, 0))
    far_block = pl.BlockSpec((None, far, width), lambda i: (image, 0, 0))
    probs_block = pl.BlockSpec(
        (rows_per_step, HEADS, columns + far, columns), lambda i: (image * steps + i, 0, 0, 0)
    )
    return chain_call(
        functools.partial(
            attention_backward_kernel, 1.0 / math.sqrt(width // HEADS), rows_per_step
        ),
        image,
        previous,
        [],
        [query, key, value, key_far, value_far, probs, mixed_grad],
        [block] * 3 + [far_block] * 2 + [probs_block, block],
        [block] * 3 + [far_block] * 2,
        [jax.ShapeDtypeStruct((tokens, width), HALF)] * 3
        + [jax.ShapeDtypeStruct((images, far, width), SINGLE)] * 2,
        steps,
        pl.CostEstimate(
            flops=part * width * 16 * (columns + far),
            bytes_accessed=part * width * 14 + part * HEADS * (columns + far) * 2,
            transcendentals=0,
        ),
        "attention_backward",
    )


def projection_grad_kernel(
    plan,
    index_ref,
    block_ref,
    query_grad_ref,
    key_grad_ref,
    value_grad_ref,
    gain_ref,
    gain_two_grad_ref,
    w_ref,
    summary_ref,
    standard_ref,
    gain_sum_ref,
    key_far_grad_ref,
    value_far_grad_ref,
    standard_grad_ref,
    small_ref,
    *rest,
):
    *pieces, total_ref, flat_ref, sems = rest
    width = block_ref.shape[1]

    @pl.when(pl.program_id(0) == 0)
    def _():
        total_ref[...] = jnp.zeros_like(total_ref)

    normed, _ = normalize(block_ref[...].astype(SINGLE))
    turned = normed.astype(HALF).T
    for i, ref in enumerate((query_grad_ref, key_grad_ref, value_grad_ref)):
        total_ref[:, i * width : (i + 1) * width] += dot(turned, ref[...])

    @pl.when(pl.program_id(0) == pl.num_programs(0) - 1)
    def _():
        key_low = key_far_grad_ref[...].astype(HALF)
        value_low = value_far_grad_ref[...].astype(HALF)
        gain = gain_ref[...]
        matched = jnp.zeros((width, width), SINGLE)
        flat_ref[:TAIL] = jnp.zeros((TAIL, width), HALF)
        for i in range(3):
            total = total_ref[:, i * width : (i + 1) * width]
            matched = matched + total * w_ref[:, i * width : (i + 1) * width].astype(SINGLE)
            grad = total * gain
            if i > 0:
                grad = grad + dot_outer(summary_ref[...], key_low if i == 1 else value_low)
            flat_ref[TAIL + i * width : TAIL + (i + 1) * width] = grad.astype(HALF)
            if i == 2:
                small_ref[8:] = grad[width - TAIL :]
        copies = start_pieces(plan, flat_ref, pieces, sems, index_ref[0])
        summary_grad = dot_rows(key_low, w_ref[:, width : 2 * width]) + dot_rows(
            value_low, w_ref[:, 2 * width :]
        )
        standard = standard_ref[...]
        standard_grad = summary_grad * gain_sum_ref[...]
        standard_grad_ref[...] = standard_grad

        def fold(value):
            return jnp.sum(value, axis=0, keepdims=True)

        small_ref[0:1] = fold(standard_grad)
        small_ref[1:2] = fold(standard_grad * standard)
        small_ref[2:3] = fold(matched.T)
        small_ref[3:4] = fold(summary_grad * standard)
        small_ref[4:5] = fold(summary_grad)
        small_ref[5:6] = gain_two_grad_ref[...]
        small_ref[6:8] = jnp.zeros((2, width), SINGLE)
        for copy in copies:
            copy.wait()


def projection_grads(
    index,
    block_in,
    query_grad,
    key_grad,
    value_grad,
    gain,
    gain_two_grad,
    w_qkv,
    summary_low,
    standard,
    gain_sum,
    key_far_grad,
    value_far_grad,
    size,
    plan,
    shapes,
):
    tokens, width = block_in.shape
    far = summary_low.shape[0]
    block = pl.BlockSpec((size, width), lambda i, _: (i, 0))
    piece_specs, piece_shapes = piece_outputs(shapes)
    return pl.pallas_call(
        functools.partial(projection_grad_kernel, plan),
        grid_spec=pltpu.PrefetchScalarGridSpec(
            num_scalar_prefetch=1,
            grid=(tokens // size,),
            in_specs=[block] * 4
            + [whole_block((width, 1)), whole_block((1, width)), whole_block((width, 3 * width))]
            + [whole_block((far, width))] * 2
            + [whole_block((1, width))]
            + [whole_block((far, width))] * 2,
            out_specs=[whole_block((far, width)), whole_block((8 + TAIL, width))] + piece_specs,
            scratch_shapes=[
                pltpu.VMEM((width, 3 * width), SINGLE),
                pltpu.VMEM((TAIL + 3 * width, width), HALF),
                pltpu.SemaphoreType.DMA((len(plan),)),
            ],
        ),
        out_shape=[
            jax.ShapeDtypeStruct((far, width), SINGLE),
            jax.ShapeDtypeStruct((8 + TAIL, width), SINGLE),
        ]
        + piece_shapes,
        compiler_params=pltpu.CompilerParams(vmem_limit_bytes=VMEM_BYTES),
        cost_estimate=pl.CostEstimate(
            flops=tokens * width * 6 * width, bytes_accessed=tokens * width * 8, transcendentals=0
        ),
        name="projection_grads",
    )(
        index,
        block_in,
        query_grad,
        key_grad,
        value_grad,
        gain.reshape(width, 1),
        gain_two_grad,
        w_qkv,
        summary_low,
        standard,
        gain_sum,
        key_far_grad,
        value_far_grad,
    )


def input_grad_kernel(
    rows_per_step,
    block_ref,
    gain_ref,
    query_grad_ref,
    key_grad_ref,
    value_grad_ref,
    w_ref,
    middle_grad_ref,
    mean_grad_ref,
    out_ref,
):
    width = block_ref.shape[1]
    columns = block_ref.shape[0] // rows_per_step

    attn_grad = (
        dot_rows(query_grad_ref[...], w_ref[:, :width])
        + dot_rows(key_grad_ref[...], w_ref[:, width : 2 * width])
        + dot_rows(value_grad_ref[...], w_ref[:, 2 * width :])
    )
    normed, inverse = normalize(block_ref[...].astype(SINGLE))
    total = middle_grad_ref[...] + norm_back(attn_grad * gain_ref[...], normed, inverse)
    for row in range(rows_per_step):
        tokens = slice(row * columns, (row + 1) * columns)
        out_ref[tokens] = total[tokens] + mean_grad_ref[row : row + 1]


def input_grads(
    block_in, gain, query_grad, key_grad, value_grad, w_qkv, middle_grad, mean_grad, local_rows, columns
):
    tokens, width = block_in.shape
    rows_per_step = math.gcd(local_rows, 4)
    size = rows_per_step * columns
    block = pl.BlockSpec((size, width), lambda i: (i, 0))
    return pl.pallas_call(
        functools.partial(input_grad_kernel, rows_per_step),
        grid=(tokens // size,),
        in_specs=[block, whole_block((1, width))]
        + [block] * 3
        + [whole_block((width, 3 * width)), block]
        + [pl.BlockSpec((None, rows_per_step, width), lambda i: (i, 0, 0))],
        out_specs=block,
        out_shape=jax.ShapeDtypeStruct((tokens, width), SINGLE),
        compiler_params=pltpu.CompilerParams(vmem_limit_bytes=VMEM_BYTES),
        cost_estimate=pl.CostEstimate(
            flops=tokens * width * 6 * width, bytes_accessed=tokens * width * 16, transcendentals=0
        ),
        name="input_grads",
    )(
        block_in,
        gain,
        query_grad,
        key_grad,
        value_grad,
        w_qkv,
        middle_grad,
        mean_grad.reshape(tokens // size, rows_per_step, width),
    )


def assemble(flat_ref, pieces, index, block, count):
    plane = 8 * block
    width = flat_ref.shape[1]
    for at in range(0, count * plane + 1, block):
        flat_ref[at : at + TAIL] = jnp.zeros((TAIL, width), HALF)
    for ref, mask, first in pieces:
        spot = pl.multiple_of((index ^ mask) * block, TAIL)
        for slot in range(count):
            part = ref.at[slot] if len(ref.shape) == 3 else ref
            last = first + part.shape[0]
            for low, high in ((0, TAIL), (TAIL, block), (block, block + TAIL)):
                low, high = max(low, first), min(high, last)
                if low >= high:
                    continue
                rows = pl.ds(spot + (slot * plane + low), high - low)
                value = part[low - first : high - first]
                if low < TAIL or low >= block:
                    value = flat_ref[rows] + value
                flat_ref[rows] = value


def projection_weights_kernel(masks, block, index_ref, tail_ref, summary_ref, *refs):
    *piece_refs, w_ref, key_far_ref, value_far_ref, flat_ref = refs
    width = flat_ref.shape[1]
    pieces = [(ref, mask, first) for ref, (mask, first) in zip(piece_refs, masks)]
    assemble(flat_ref, pieces, lax.rem(index_ref[0], 8), block, 1)
    flat_ref[3 * width :] += tail_ref[...]
    for i in range(3):
        w_ref[:, i * width : (i + 1) * width] = flat_ref[TAIL + i * width : TAIL + (i + 1) * width]
    key_far_ref[...] = dot(summary_ref[...], w_ref[:, width : 2 * width]).astype(HALF)
    value_far_ref[...] = dot(summary_ref[...], w_ref[:, 2 * width :]).astype(HALF)


def vmem_specs(count):
    return [pl.BlockSpec(memory_space=pltpu.VMEM)] * count


def projection_weights(index, tail, summary_low, pieces, block):
    width = tail.shape[1]
    arrays, masks = [p[0] for p in pieces], [p[1:] for p in pieces]
    far = summary_low.shape[0]
    return pl.pallas_call(
        functools.partial(projection_weights_kernel, masks, block),
        in_specs=[pl.BlockSpec(memory_space=pltpu.SMEM)] + vmem_specs(2 + len(arrays)),
        out_specs=vmem_specs(3),
        out_shape=[
            jax.ShapeDtypeStruct((width, 3 * width), HALF),
            jax.ShapeDtypeStruct((far, width), HALF),
            jax.ShapeDtypeStruct((far, width), HALF),
        ],
        scratch_shapes=[pltpu.VMEM((TAIL + 3 * width, width), HALF)],
        compiler_params=pltpu.CompilerParams(vmem_limit_bytes=VMEM_BYTES),
        name="projection_weights",
    )(index, tail, summary_low, *arrays)


def hidden_weights_kernel(masks, block, index_ref, *refs):
    *piece_refs, w_out_ref, w_inner_ref, w_outer_ref, flat_ref = refs
    width, hidden = w_inner_ref.shape
    pieces = [(ref, mask, first) for ref, (mask, first) in zip(piece_refs, masks)]
    assemble(flat_ref, pieces, lax.rem(index_ref[0], 8), block, 3)
    groups = hidden // width
    per = 256 // groups
    w_out_ref[...] = flat_ref[TAIL : TAIL + width]
    mix = weave(groups, per)
    for c in range(width // per):
        start = TAIL + width + c * groups * per
        parted = dot_outer(mix, flat_ref[start : start + groups * per]).astype(HALF)
        for g in range(groups):
            w_inner_ref[c * per : (c + 1) * per, g * width : (g + 1) * width] = parted[
                g * per : (g + 1) * per
            ]
    w_outer_ref[...] = flat_ref[TAIL + width + hidden :]


def hidden_weights(index, pieces, block, width, hidden):
    arrays, masks = [p[0] for p in pieces], [p[1:] for p in pieces]
    return pl.pallas_call(
        functools.partial(hidden_weights_kernel, masks, block),
        in_specs=[pl.BlockSpec(memory_space=pltpu.SMEM)] + vmem_specs(len(arrays)),
        out_specs=vmem_specs(3),
        out_shape=[
            jax.ShapeDtypeStruct((width, width), HALF),
            jax.ShapeDtypeStruct((width, hidden), HALF),
            jax.ShapeDtypeStruct((hidden, width), HALF),
        ],
        scratch_shapes=[pltpu.VMEM((TAIL + width + 2 * hidden, width), HALF)],
        compiler_params=pltpu.CompilerParams(vmem_limit_bytes=VMEM_BYTES),
        name="hidden_weights",
    )(index, *arrays)


def swap_core(value):
    return swap(value, "row", 1)


def swap_x(value):
    return swap(value, "row", 2)


def swap_y(value):
    return swap(value, "img", 1)


def swap_near(value):
    return swap(value, "img", 2)


def swap_far(value):
    return swap(value, "img", 4)


def send_down(value, distance):
    size = lax.axis_size("img")
    senders = [i for i in range(size) if i & distance and not i & (distance - 1) & ~1]
    return lax.ppermute(value, "img", [(i, i ^ distance) for i in senders])


def spread_plane(value, split):
    rows = value.ndim - 2

    def cut(array, low, high):
        return lax.slice_in_dim(array, low, high, axis=rows)

    over_x, over_y = swap_x(value), swap_y(value)
    corner_first = swap_y(cut(over_x, 0, split))
    corner_second = swap_x(cut(over_y, split, value.shape[rows]))
    near = [(value, 0, 0), (over_x, 2, 0), (over_y, 4, 0), (corner_first, 6, 0), (corner_second, 6, split)]
    return near + [(swap_core(array), mask | 1, first) for array, mask, first in near]


def sum_plane(kept, sent, split):
    near = kept.astype(SINGLE) + swap_core(sent).astype(SINGLE)
    first, second = near[..., :split, :], near[..., split:, :]

    def pick(array, i):
        return lax.index_in_dim(array, i, array.ndim - 3, keepdims=False)

    def both(array, i, j):
        return jnp.stack([pick(array, i), pick(array, j)], axis=array.ndim - 3)

    first_in = swap_y(both(first, 2, 3).astype(HALF))
    second_in = swap_x(both(second, 1, 3).astype(HALF))
    first = both(first, 0, 1) + first_in.astype(SINGLE)
    second = both(second, 0, 2) + second_in.astype(SINGLE)
    first = pick(first, 0) + swap_x(pick(first, 1).astype(HALF)).astype(SINGLE)
    second = pick(second, 0) + swap_y(pick(second, 1).astype(HALF)).astype(SINGLE)
    return jnp.concatenate([first, second], axis=-2)


def fits_planes(width, block):
    return lax.axis_size("row") == 4 and lax.axis_size("img") == 8 and 8 * block == 3 * width


def own_rows(weights, width):
    length = weights.shape[0]
    block, rest = length // width, length % width
    start = TAIL * width + rest * device_index() - 4 * width
    own = lax.dynamic_update_slice(jnp.zeros(((block + TAIL) * width,), HALF), weights, (start,))
    return own.reshape(block + TAIL, width), start


def per_device(activations, cotangent, weights):
    images, local_rows, columns, width = activations.shape
    tokens = images * local_rows * columns
    size = tokens // images
    rows_all = local_rows * lax.axis_size("row")
    far = images * rows_all
    first_row = lax.axis_index("row") * local_rows
    summary_count = float(images * lax.axis_size("img") * rows_all)
    block = weights.shape[0] // width
    planes = fits_planes(width, block)
    split = block // 2 // TAIL * TAIL
    me = device_index()
    index = me[None]
    z = lax.axis_index("img") // 2
    block_in = activations.reshape(tokens, width)

    if planes:
        own, start = own_rows(weights, width)
        over_far = swap_far(own)
        over_near = swap_near(jnp.stack([own, over_far]))
        held = jnp.stack([own, over_near[0], over_far, over_near[1]])
        first_slot = lax.dynamic_index_in_dim(held, z, 0, keepdims=False)
        other_slots = jnp.stack(
            [lax.dynamic_index_in_dim(held, z ^ i, 0, keepdims=False) for i in (1, 2, 3)]
        )
        first_pieces = spread_plane(first_slot, split)
        other_pieces = spread_plane(other_slots, split)
        shown = jnp.concatenate(
            [
                jnp.where(me == 0, own[TAIL - 4 : TAIL].astype(SINGLE), 0.0),
                jnp.where(me == 8, own[:TAIL].astype(SINGLE), 0.0),
            ]
        )
    else:
        gathered, matrix_rows = gather_weights(weights, width)
        shown = jnp.zeros((4 + TAIL, width), SINGLE)

    row_means = jnp.mean(activations.astype(SINGLE), axis=2)
    all_means, shown = gather_rows(row_means, shown)
    sums = jnp.stack([jnp.sum(all_means, axis=(0, 1)), jnp.sum(all_means * all_means, axis=(0, 1))])
    sums = jnp.concatenate([sums, shown])
    for axis, distance, _ in image_hops():
        sums = sums + swap(sums, axis, distance)
    summary_mean = sums[0] / summary_count
    summary_var = sums[1] / summary_count - summary_mean * summary_mean
    summary_inv = lax.rsqrt(summary_var + EPS)
    standard = (all_means - summary_mean) * summary_inv
    vectors = sums[2:6] if planes else gathered.astype(SINGLE)
    gain_one, gain_sum, bias_sum, gain_two = (vectors[i : i + 1] for i in range(4))
    summary_low = (standard * gain_sum + bias_sum).astype(HALF).reshape(far, width)

    if planes:
        w_qkv, key_far, value_far = projection_weights(
            index, sums[6:].astype(HALF), summary_low, first_pieces, block
        )
    else:
        w_qkv, w_out, w_inner, w_outer = unpack(matrix_rows, width, FF)
        key_far = dot(summary_low, w_qkv[:, width : 2 * width]).astype(HALF)
        value_far = dot(summary_low, w_qkv[:, 2 * width :]).astype(HALF)
    key_far = key_far.reshape(images, rows_all, width)
    value_far = value_far.reshape(images, rows_all, width)

    forward = None
    for image in range(images):
        forward = attention_forward(
            image,
            forward,
            block_in,
            gain_one,
            w_qkv,
            key_far,
            value_far,
            first_row[None],
            local_rows,
            columns,
        )
    query, key, value, mixed, probs = forward

    if planes:
        w_out, w_inner, w_outer = hidden_weights(index, other_pieces, block, width, FF)
        late_plan, early_plan = [], []
        for side in range(2):
            for place, mask in enumerate((0, 2, 4, 6)):

                def offset(i, mask=mask | side):
                    return lax.rem(i, 8) ^ mask

                late_plan.append((side, (place,), lambda i, at=offset: at(i) * block, block + TAIL))
                for slot in range(3):
                    early_plan.append(
                        (
                            side,
                            (slot, place),
                            lambda i, at=offset, slot=slot: (slot * 8 + at(i)) * block,
                            block + TAIL,
                        )
                    )
        early_shapes = [(3, 4, block + TAIL, width)] * 2
        late_shapes = [(4, block + TAIL, width)] * 2
    else:
        early_shapes = [(TAIL + width + 2 * FF, width)]
        late_shapes = [(TAIL + 3 * width, width)]
        early_plan = [(0, (), lambda i: i * 0, early_shapes[0][0])]
        late_plan = [(0, (), lambda i: i * 0, late_shapes[0][0])]

    out, middle_grad, mixed_grad, gain_two_grad, *early = feed_forward(
        index,
        block_in,
        mixed,
        cotangent.reshape(tokens, width),
        gain_two,
        w_out,
        w_inner,
        w_outer,
        size,
        early_plan,
        early_shapes,
    )
    backward = None
    for image in range(images):
        backward = attention_backward(
            image, backward, query, key, value, key_far, value_far, probs, mixed_grad, local_rows, columns
        )
    query_grad, key_grad, value_grad, key_far_grad, value_far_grad = backward
    standard_flat = standard.reshape(far, width)
    standard_grad, small, *late = projection_grads(
        index,
        block_in,
        query_grad,
        key_grad,
        value_grad,
        gain_one,
        gain_two_grad,
        w_qkv,
        summary_low,
        standard_flat,
        gain_sum,
        key_far_grad.reshape(far, width),
        value_far_grad.reshape(far, width),
        size,
        late_plan,
        late_shapes,
    )
    shared = jnp.concatenate([standard_grad, small])
    for axis, distance, _ in row_hops():
        shared = shared + swap(shared, axis, distance)
    own_grad = lax.dynamic_slice_in_dim(
        shared[:far].reshape(images, rows_all, width), first_row, local_rows, axis=1
    )
    own_standard = lax.dynamic_slice_in_dim(standard, first_row, local_rows, axis=1)
    small = shared[far:]
    for axis, distance, _ in image_hops():
        small = small + swap(small, axis, distance)
    mean_grad = summary_inv * (
        own_grad - small[0] / summary_count - own_standard * (small[1] / summary_count)
    )
    input_grad = input_grads(
        block_in,
        gain_one,
        query_grad,
        key_grad,
        value_grad,
        w_qkv,
        middle_grad,
        mean_grad / columns,
        local_rows,
        columns,
    )
    if planes:
        early_sum = sum_plane(*early, split)
        padded = jnp.concatenate([jnp.zeros_like(early_sum[:1]), early_sum])
        by_mask = [lax.dynamic_index_in_dim(padded, z ^ i, 0, keepdims=False) for i in range(4)]
        got = swap_near(jnp.stack([by_mask[1], by_mask[3]]).astype(HALF)).astype(SINGLE)
        early_own = by_mask[0] + got[0]
        early_own = early_own + swap_far((by_mask[2] + got[1]).astype(HALF)).astype(SINGLE)
        late_own = sum_plane(*late, split)
        late_own = late_own + send_down(late_own.astype(HALF), 2).astype(SINGLE)
        late_own = late_own + send_down(late_own.astype(HALF), 4).astype(SINGLE)
        head = jnp.where(
            me == 0,
            jnp.concatenate([jnp.zeros((TAIL - 4, width), SINGLE), small[2:6]]),
            jnp.where(me == 8, small[8:], 0.0),
        )
        mine = jnp.where(z == 0, late_own, early_own)
        mine = jnp.concatenate([mine[:TAIL] + head, mine[TAIL:]])
        weight_grad = lax.dynamic_slice(mine.reshape(-1), (start,), weights.shape)
    else:
        grad_rows = jnp.concatenate([late[0][TAIL:], early[0][TAIL:]]).astype(SINGLE)
        weight_grad = scatter_grads(small[2:6], grad_rows, weights.shape[0])
    return (
        out.reshape(activations.shape),
        input_grad.reshape(activations.shape),
        weight_grad,
        summary_mean,
        summary_var,
    )


def solution(mesh):
    placed = (P("img", "row", None, None), P("img", "row", None, None), P(("img", "row")))
    return jax.shard_map(
        per_device,
        mesh=mesh,
        in_specs=placed,
        out_specs=(
            P("img", "row", None, None),
            P("img", "row", None, None),
            P(("img", "row")),
            P(),
            P(),
        ),
        check_vma=False,
    )
```

```python
import functools
import math

import jax
import jax.numpy as jnp
from jax import lax
from jax.experimental import pallas as pl
from jax.experimental.pallas import tpu as pltpu
from jax.sharding import PartitionSpec as P

FF = 2048
HEADS = 8
LANES = 128


EPS = 1e-05
NEGATIVE = -1e30
HALF = jnp.bfloat16
SINGLE = jnp.float32
VMEM_BYTES = 56 * 1024 * 1024

TAIL = 16


def swap(value, axis, distance):
    size = lax.axis_size(axis)
    return lax.ppermute(value, axis, [(i, i ^ distance) for i in range(size)])


def hops():
    rows, images = lax.axis_size("row"), lax.axis_size("img")
    inner = ("row", 1, 1)
    across = ("row", 2, 2)
    along = ("img", 1, rows)
    outer = []
    distance = images // 2
    while distance > 1:
        outer.append(("img", distance, distance * rows))
        distance //= 2
    distance = rows // 2
    while distance > 2:
        outer.append(("row", distance, distance))
        distance //= 2
    return inner, across, along, outer


def piece_order():
    inner, across, along, outer = hops()
    masks = [0]
    for _, _, mask in outer:
        masks = masks + [m ^ mask for m in masks]
    near = (
        masks
        + [m ^ across[2] for m in masks]
        + [m ^ along[2] for m in masks]
        + [m ^ across[2] ^ along[2] for m in masks]
    )
    return near + [m ^ inner[2] for m in near]


def device_index():
    return lax.axis_index("img") * lax.axis_size("row") + lax.axis_index("row")


def gather_pieces(own):
    inner, across, along, outer = hops()
    held = own[None]
    for axis, distance, _ in outer:
        held = jnp.concatenate([held, swap(held, axis, distance)])
    half = held.shape[0] // 2
    held_x = swap(held, across[0], across[1])
    held_y = swap(held, along[0], along[1])
    corner_first = swap(held_x[:half], along[0], along[1])
    corner_second = swap(held_y[half:], across[0], across[1])
    near = [held, held_x, held_y, corner_first, corner_second]
    far = [swap(part, inner[0], inner[1]) for part in near]
    return jnp.concatenate(near + far)


def scatter_pieces(pieces):
    inner, across, along, outer = hops()

    def add(kept, sent, axis, distance):
        return kept + swap(sent.astype(HALF), axis, distance).astype(SINGLE)

    count = pieces.shape[0] // 2
    near = add(pieces[:count], pieces[count:], inner[0], inner[1])
    quarter = count // 4
    half = quarter // 2
    held, held_x, held_y, corner = (near[i * quarter : (i + 1) * quarter] for i in range(4))
    first = add(
        jnp.concatenate([held[:half], held_x[:half]]),
        jnp.concatenate([held_y[:half], corner[:half]]),
        along[0],
        along[1],
    )
    second = add(
        jnp.concatenate([held[half:], held_y[half:]]),
        jnp.concatenate([held_x[half:], corner[half:]]),
        across[0],
        across[1],
    )
    first = add(first[:half], first[half:], across[0], across[1])
    second = add(second[:half], second[half:], along[0], along[1])
    held = jnp.concatenate([first, second])
    for axis, distance, _ in reversed(outer):
        half = held.shape[0] // 2
        held = add(held[:half], held[half:], axis, distance)
    return held[0]


def row_hops():
    inner, across, _, outer = hops()
    return [inner, across] + [hop for hop in outer if hop[0] == "row"]


def image_hops():
    _, _, along, outer = hops()
    return [along] + [hop for hop in outer if hop[0] == "img"]


def gather_rows(own, shown):
    width = own.shape[-1]
    count = shown.shape[0]
    held, masks = own[None], [0]
    for axis, distance, mask in row_hops():
        got = swap(jnp.concatenate([held.reshape(-1, width), shown]), axis, distance)
        held = jnp.concatenate([held, got[:-count].reshape(held.shape)])
        shown = shown + got[-count:]
        masks = masks + [m ^ mask for m in masks]
    place = [0] * len(masks)
    for at, mask in enumerate(masks):
        place[mask] = at
    order = jnp.asarray(place, jnp.int32)[jnp.arange(len(masks)) ^ lax.axis_index("row")]
    held = jnp.moveaxis(jnp.take(held, order, axis=0, mode="clip"), 0, 1)
    return held.reshape(own.shape[0], -1, width), shown


def gather_weights(weights, model_width):
    length = weights.shape[0]
    me = device_index()
    devices = lax.axis_size("img") * lax.axis_size("row")
    block = length // model_width
    rest = length % model_width
    start = TAIL * model_width + rest * me - 4 * model_width
    own = lax.dynamic_update_slice(jnp.zeros(((block + TAIL) * model_width,), HALF), weights, (start,))
    own = own.reshape(block + TAIL, model_width)
    pieces = gather_pieces(own)
    place = [0] * devices
    for at, mask in enumerate(piece_order()):
        place[mask] = at
    order = jnp.asarray(place, jnp.int32)[jnp.arange(devices) ^ me]
    pieces = jnp.take(pieces, order, axis=0, mode="clip")
    tails = jnp.concatenate([pieces[1:, :TAIL], jnp.zeros((1, TAIL, model_width), HALF)])
    body = jnp.concatenate([pieces[:, TAIL:block], pieces[:, block:] + tails], axis=1)
    return pieces[0, TAIL - 4 : TAIL], body.reshape(devices * block, model_width)


def scatter_grads(vectors, rows, length):
    model_width = rows.shape[1]
    me = device_index()
    devices = lax.axis_size("img") * lax.axis_size("row")
    block = length // model_width
    rest = length % model_width
    whole = jnp.concatenate([jnp.zeros((TAIL - 4, model_width), SINGLE), vectors, rows])
    place = jnp.asarray(piece_order(), jnp.int32)
    pieces = jnp.stack([whole[block * s : block * s + block + TAIL] for s in range(devices)])
    pieces = jnp.take(pieces, place ^ me, axis=0, mode="clip")
    mine = scatter_pieces(pieces)
    start = TAIL * model_width + rest * me - 4 * model_width
    return lax.dynamic_slice(mine.reshape(-1), (start,), (length,))


def unpack(rows, model_width, ff_width):
    w_qkv = jnp.concatenate([rows[i * model_width : (i + 1) * model_width] for i in range(3)], axis=1)
    w_out = rows[3 * model_width : 4 * model_width]
    w_inner = rows[4 * model_width : 4 * model_width + ff_width].reshape(model_width, ff_width)
    w_outer = rows[4 * model_width + ff_width :]
    return (w_qkv, w_out, w_inner, w_outer)


def dot(left, right):
    return jnp.dot(left, right, preferred_element_type=SINGLE)


def dot_rows(left, right):
    return lax.dot_general(left, right, (((1,), (1,)), ((), ())), preferred_element_type=SINGLE)


def dot_outer(left, right):
    return lax.dot_general(left, right, (((0,), (0,)), ((), ())), preferred_element_type=SINGLE)


def normalize(values):
    centred = values - jnp.mean(values, axis=-1, keepdims=True)
    inverse = lax.rsqrt(jnp.mean(centred * centred, axis=-1, keepdims=True) + EPS)
    return (centred * inverse, inverse)


def norm_back(grad_norm, normed, inverse):
    return inverse * (
        grad_norm
        - jnp.mean(grad_norm, axis=-1, keepdims=True)
        - normed * jnp.mean(grad_norm * normed, axis=-1, keepdims=True)
    )


def whole_block(shape):
    return pl.BlockSpec(shape, lambda *_: (0,) * len(shape), pipeline_mode=pl.Buffered(1))


def head_keys(rows_per_step, model_width):
    return [
        (row, pair, half)
        for row in range(rows_per_step)
        for pair in range(model_width // LANES)
        for half in range(2)
    ]


def attention_forward_kernel(
    scaling,
    rows_per_step,
    local_rows,
    first_row_ref,
    block_ref,
    gain_ref,
    w_ref,
    key_far_ref,
    value_far_ref,
    causal_ref,
    query_ref,
    key_ref,
    value_ref,
    mixed_ref,
    probs_ref,
):
    columns = causal_ref.shape[0]
    far = key_far_ref.shape[0]
    width = block_ref.shape[1]
    head_width = width // HEADS
    step = pl.program_id(0)
    normed, _ = normalize(block_ref[...].astype(SINGLE))
    attn_in = (normed * gain_ref[...]).astype(HALF)
    for i, ref in enumerate((query_ref, key_ref, value_ref)):
        ref[...] = dot(attn_in, w_ref[:, i * width : (i + 1) * width]).astype(HALF)
    first_half = lax.broadcasted_iota(jnp.int32, (columns + far, LANES), 1) < head_width
    far_index = lax.broadcasted_iota(jnp.int32, (far, columns), 0)
    keys = head_keys(rows_per_step, width)
    for start in range(0, len(keys), HEADS):
        group = keys[start : start + HEADS]
        scores, low, mixed = {}, {}, {}
        for row, pair, half in group:
            global_row = first_row_ref[0] + lax.rem(step * rows_per_step + row, local_rows)
            far_bias = jnp.where(far_index < global_row, 0.0, NEGATIVE)
            tokens = slice(row * columns, (row + 1) * columns)
            lanes = slice(pair * LANES, (pair + 1) * LANES)
            all_keys = jnp.concatenate([key_ref[tokens, lanes], key_far_ref[:, lanes]], axis=0)
            one_head = jnp.where(
                first_half if half == 0 else ~first_half, all_keys, jnp.zeros_like(all_keys)
            )
            found = dot_rows(one_head, query_ref[tokens, lanes])
            scores[row, pair, half] = jnp.concatenate(
                [found[:columns] + causal_ref[...], found[columns:] + far_bias], axis=0
            )
        for row, pair, half in group:
            found = scores.pop((row, pair, half))
            top = jnp.max(found, axis=0, keepdims=True)
            powers = jnp.exp((found - top) * scaling)
            inverse = 1.0 / jnp.sum(powers, axis=0, keepdims=True)
            low[row, pair, half] = (powers * inverse).astype(HALF)
            probs_ref[row, 2 * pair + half] = low[row, pair, half]
        for row, pair, half in group:
            tokens = slice(row * columns, (row + 1) * columns)
            lanes = slice(pair * LANES, (pair + 1) * LANES)
            all_values = jnp.concatenate([value_ref[tokens, lanes], value_far_ref[:, lanes]], axis=0)
            turned = all_values.T[half * head_width : (half + 1) * head_width]
            mixed[row, pair, half] = dot(turned, low[row, pair, half])
        for row, pair, half in group:
            if half == 0:
                tokens = slice(row * columns, (row + 1) * columns)
                lanes = slice(pair * LANES, (pair + 1) * LANES)
                both = jnp.concatenate([mixed[row, pair, 0], mixed[row, pair, 1]], axis=0)
                mixed_ref[tokens, lanes] = both.T.astype(HALF)


def image_groups(images):
    return [(0, 1), (1, images - 1)] if images > 1 else [(0, images)]


def kept_arrays(previous, start):
    if previous is None:
        return ([], [], {})
    specs = [pl.BlockSpec(memory_space=pl.ANY)] * len(previous)
    return (list(previous), specs, {start + i: i for i in range(len(previous))})


def attention_forward(
    group, previous, block_in, gain, w_qkv, key_far, value_far, first_row, local_rows, columns
):
    tokens, width = block_in.shape
    images, far, _ = key_far.shape
    first_image, count = group
    rows_per_step = math.gcd(local_rows, 2)
    steps = local_rows // rows_per_step
    first_step = first_image * steps
    size = rows_per_step * columns
    position = jnp.arange(columns)
    causal = jnp.where(position[:, None] <= position[None, :], 0.0, NEGATIVE).astype(SINGLE)
    block = pl.BlockSpec((size, width), lambda i, _: (first_step + i, 0))
    far_block = pl.BlockSpec((None, far, width), lambda i, _: (first_image + i // steps, 0, 0))
    probs_block = pl.BlockSpec(
        (rows_per_step, HEADS, columns + far, columns), lambda i, _: (first_step + i, 0, 0, 0)
    )
    inputs = [block_in, gain, w_qkv, key_far, value_far, causal]
    kept, kept_specs, aliases = kept_arrays(previous, 1 + len(inputs))
    low = jax.ShapeDtypeStruct((tokens, width), HALF)
    part = count * tokens // images
    kernel = functools.partial(
        attention_forward_kernel, 1.0 / math.sqrt(width // HEADS), rows_per_step, local_rows
    )

    def body(*refs):
        kernel(*refs[: 1 + len(inputs)], *refs[1 + len(inputs) + len(kept) :])

    return pl.pallas_call(
        body,
        grid_spec=pltpu.PrefetchScalarGridSpec(
            num_scalar_prefetch=1,
            grid=(count * steps,),
            in_specs=[
                block,
                whole_block((1, width)),
                whole_block((width, 3 * width)),
                far_block,
                far_block,
                whole_block((columns, columns)),
            ]
            + kept_specs,
            out_specs=[block] * 4 + [probs_block],
        ),
        out_shape=[low] * 4
        + [jax.ShapeDtypeStruct((images * local_rows, HEADS, columns + far, columns), HALF)],
        input_output_aliases=aliases,
        compiler_params=pltpu.CompilerParams(vmem_limit_bytes=VMEM_BYTES),
        cost_estimate=pl.CostEstimate(
            flops=part * width * (6 * width + 8 * (columns + far)),
            bytes_accessed=part * width * 12 + part * HEADS * (columns + far) * 2,
            transcendentals=part * HEADS * (columns + far),
        ),
        name="attention_forward",
    )(first_row, *inputs, *kept)


GELU_OUTER = math.sqrt(2.0 / math.pi)
GELU_CUBE = 0.044715


def gelu_and_slope(value):
    square = value * value
    gate = 0.5 * jnp.tanh(value * (GELU_OUTER * GELU_CUBE * square + GELU_OUTER)) + 0.5
    activated = value * gate
    slope = gate + activated * (1.0 - gate) * (6.0 * GELU_OUTER * GELU_CUBE * square + 2.0 * GELU_OUTER)
    return (activated, slope)


def start_pieces(plan, flat_ref, outs, sems, index):
    copies = []
    for i, (out, place, offset, rows) in enumerate(plan):
        source = flat_ref.at[pl.ds(pl.multiple_of(offset(index), TAIL), rows)]
        target = outs[out].at[place] if place else outs[out]
        copies.append(pltpu.make_async_copy(source, target, sems.at[i]))
    for copy in copies:
        copy.start()
    return copies


def feed_forward_kernel(
    chunk,
    plan,
    index_ref,
    block_ref,
    mixed_ref,
    cotangent_ref,
    gain_ref,
    w_out_ref,
    w_inner_ref,
    w_outer_ref,
    out_ref,
    middle_grad_ref,
    mixed_grad_ref,
    grad_gain_ref,
    *rest,
):
    *pieces, grad_out_ref, grad_inner_ref, grad_outer_ref, flat_ref, sems = rest

    @pl.when(pl.program_id(0) == 0)
    def _():
        for ref in (grad_out_ref, grad_inner_ref, grad_outer_ref, grad_gain_ref):
            ref[...] = jnp.zeros_like(ref)

    mixed = mixed_ref[...]
    cotangent = cotangent_ref[...]
    middle = block_ref[...].astype(SINGLE) + dot(mixed, w_out_ref[...])
    normed, inverse = normalize(middle)
    ff_in = (normed * gain_ref[...]).astype(HALF)
    out = middle
    ff_grad = jnp.zeros_like(middle)
    cotangent_turned = cotangent.T
    ff_turned = ff_in.T
    width, hidden = w_inner_ref.shape
    count = hidden // chunk
    spans = [slice(j * chunk, (j + 1) * chunk) for j in range(count)]

    def products(j):
        return (dot(ff_in, w_inner_ref[:, spans[j]]), dot_rows(cotangent, w_outer_ref[spans[j], :]))

    ready = products(0)
    for j in range(count):
        inner, act_grad = ready
        if j + 1 < count:
            ready = products(j + 1)
        activated, slope = gelu_and_slope(inner)
        activated = activated.astype(HALF)
        inner_grad = (slope * act_grad).astype(HALF)
        out = out + dot(activated, w_outer_ref[spans[j], :])
        ff_grad = ff_grad + dot_rows(inner_grad, w_inner_ref[:, spans[j]])
        grad_inner_ref[:, spans[j]] += dot(ff_turned, inner_grad)
        grad_outer_ref[:, spans[j]] += dot(cotangent_turned, activated)
    out_ref[...] = out.astype(HALF)
    grad_gain_ref[...] += jnp.sum(ff_grad * normed, axis=0, keepdims=True)
    middle_grad = cotangent.astype(SINGLE) + norm_back(ff_grad * gain_ref[...], normed, inverse)
    middle_grad_ref[...] = middle_grad
    branch_grad = middle_grad.astype(HALF)
    mixed_grad_ref[...] = dot_rows(branch_grad, w_out_ref[...]).astype(HALF)
    grad_out_ref[...] += dot_outer(mixed, branch_grad)

    @pl.when(pl.program_id(0) == pl.num_programs(0) - 1)
    def _():
        groups = hidden // width
        flat_ref[:TAIL] = jnp.zeros((TAIL, width), HALF)
        flat_ref[TAIL : TAIL + width] = grad_out_ref[...].astype(HALF)
        per = 256 // groups
        mix = weave(groups, per)
        for c in range(width // per):
            parts = [
                grad_inner_ref[c * per : (c + 1) * per, g * width : (g + 1) * width].astype(HALF)
                for g in range(groups)
            ]
            start = TAIL + width + c * groups * per
            woven = dot(mix, jnp.concatenate(parts, axis=0))
            flat_ref[start : start + groups * per] = woven.astype(HALF)
        start = TAIL + width + hidden
        for j in range(hidden // width):
            turned = grad_outer_ref[:, j * width : (j + 1) * width].astype(HALF).T
            flat_ref[start + j * width : start + (j + 1) * width] = turned
        for copy in start_pieces(plan, flat_ref, pieces, sems, index_ref[0]):
            copy.wait()


def weave(groups, per):
    size = groups * per
    row = lax.broadcasted_iota(jnp.int32, (size, size), 0)
    column = lax.broadcasted_iota(jnp.int32, (size, size), 1)
    wanted = lax.rem(row, groups) * per + lax.div(row, groups)
    return (wanted == column).astype(SINGLE).astype(HALF)


def piece_outputs(shapes):
    return (
        [pl.BlockSpec(memory_space=pl.ANY)] * len(shapes),
        [jax.ShapeDtypeStruct(shape, HALF) for shape in shapes],
    )


def feed_forward(index, block_in, mixed, cotangent, gain, w_out, w_inner, w_outer, size, plan, shapes):
    tokens, width = block_in.shape
    hidden = w_inner.shape[1]
    block = pl.BlockSpec((size, width), lambda i, _: (i, 0))
    piece_specs, piece_shapes = piece_outputs(shapes)
    return pl.pallas_call(
        functools.partial(feed_forward_kernel, 512, plan),
        grid_spec=pltpu.PrefetchScalarGridSpec(
            num_scalar_prefetch=1,
            grid=(tokens // size,),
            in_specs=[
                block,
                block,
                block,
                whole_block((1, width)),
                whole_block((width, width)),
                whole_block((width, hidden)),
                whole_block((hidden, width)),
            ],
            out_specs=[block, block, block, whole_block((1, width))] + piece_specs,
            scratch_shapes=[
                pltpu.VMEM((width, width), SINGLE),
                pltpu.VMEM((width, hidden), SINGLE),
                pltpu.VMEM((width, hidden), SINGLE),
                pltpu.VMEM((TAIL + width + 2 * hidden, width), HALF),
                pltpu.SemaphoreType.DMA((len(plan),)),
            ],
        ),
        out_shape=[
            jax.ShapeDtypeStruct((tokens, width), HALF),
            jax.ShapeDtypeStruct((tokens, width), SINGLE),
            jax.ShapeDtypeStruct((tokens, width), HALF),
            jax.ShapeDtypeStruct((1, width), SINGLE),
        ]
        + piece_shapes,
        compiler_params=pltpu.CompilerParams(vmem_limit_bytes=VMEM_BYTES),
        cost_estimate=pl.CostEstimate(
            flops=tokens * width * (6 * width + 12 * hidden),
            bytes_accessed=tokens * width * 14 + width * hidden * 8,
            transcendentals=tokens * hidden,
        ),
        name="feed_forward",
    )(index, block_in, mixed, cotangent, gain, w_out, w_inner, w_outer)


def attention_backward_kernel(
    scaling,
    rows_per_step,
    per_image,
    plan,
    begins,
    ends,
    index_ref,
    block_ref,
    query_ref,
    key_ref,
    value_ref,
    key_far_ref,
    value_far_ref,
    probs_ref,
    mixed_grad_ref,
    *rest,
):
    rest = list(rest)
    earlier = None
    if not begins:
        earlier, rest = rest[:3], rest[6:]
    if ends:
        fixed, rest = rest[:6], rest[6:]
    query_grad_ref, key_grad_ref, value_grad_ref, *rest = rest
    if ends:
        standard_grad_ref, small_ref, *rest = rest
        *pieces, total_ref, key_far_grad_ref, value_far_grad_ref, flat_ref, sems = rest
    else:
        total_ref, key_far_grad_ref, value_far_grad_ref = rest
    width = query_ref.shape[1]
    head_width = width // HEADS
    far = key_far_ref.shape[0]
    columns = query_ref.shape[0] // rows_per_step
    image = lax.div(pl.program_id(0), per_image)

    @pl.when(pl.program_id(0) == 0)
    def _():
        if earlier is None:
            total_ref[...] = jnp.zeros_like(total_ref)
        else:
            total_ref[...] = earlier[0][...]
        key_far_grad_ref[...] = jnp.zeros_like(key_far_grad_ref)
        value_far_grad_ref[...] = jnp.zeros_like(value_far_grad_ref)

    first_half = lax.broadcasted_iota(jnp.int32, (columns + far, LANES), 1) < head_width
    keys = head_keys(rows_per_step, width)
    for start in range(0, len(keys), HEADS):
        group = keys[start : start + HEADS]
        prob_grad, score_grad, value_grad, key_grad, query_grad = {}, {}, {}, {}, {}
        for row, pair, half in group:
            tokens = slice(row * columns, (row + 1) * columns)
            lanes = slice(pair * LANES, (pair + 1) * LANES)
            all_values = jnp.concatenate([value_ref[tokens, lanes], value_far_ref[:, lanes]], axis=0)
            one_head = jnp.where(
                first_half if half == 0 else ~first_half, all_values, jnp.zeros_like(all_values)
            )
            prob_grad[row, pair, half] = dot_rows(one_head, mixed_grad_ref[tokens, lanes])
        for row, pair, half in group:
            tokens = slice(row * columns, (row + 1) * columns)
            lanes = slice(pair * LANES, (pair + 1) * LANES)
            value_grad[row, pair, half] = dot(
                probs_ref[row, 2 * pair + half], mixed_grad_ref[tokens, lanes]
            )
        for row, pair, half in group:
            probs = probs_ref[row, 2 * pair + half].astype(SINGLE)
            grad = prob_grad.pop((row, pair, half))
            total = jnp.sum(probs * grad, axis=0, keepdims=True)
            score_grad[row, pair, half] = (probs * (grad - total)).astype(HALF)
        for row, pair, half in group:
            tokens = slice(row * columns, (row + 1) * columns)
            lanes = slice(pair * LANES, (pair + 1) * LANES)
            key_grad[row, pair, half] = dot(score_grad[row, pair, half], query_ref[tokens, lanes])
            all_keys = jnp.concatenate([key_ref[tokens, lanes], key_far_ref[:, lanes]], axis=0)
            turned = all_keys.T[half * head_width : (half + 1) * head_width]
            query_grad[row, pair, half] = dot(turned, score_grad[row, pair, half])
        for row, pair, half in group:
            if half == 0:
                tokens = slice(row * columns, (row + 1) * columns)
                lanes = slice(pair * LANES, (pair + 1) * LANES)
                first, second = (row, pair, 0), (row, pair, 1)
                value_both = jnp.where(first_half, value_grad[first], value_grad[second])
                key_both = jnp.where(first_half, key_grad[first], key_grad[second]) * scaling
                value_grad_ref[tokens, lanes] = value_both[:columns].astype(HALF)
                key_grad_ref[tokens, lanes] = key_both[:columns].astype(HALF)
                value_far_grad_ref[image, :, lanes] += value_both[columns:]
                key_far_grad_ref[image, :, lanes] += key_both[columns:]
                query_both = jnp.concatenate([query_grad[first], query_grad[second]], axis=0) * scaling
                query_grad_ref[tokens, lanes] = query_both.T.astype(HALF)
    normed, _ = normalize(block_ref[...].astype(SINGLE))
    turned = normed.astype(HALF).T
    for i, ref in enumerate((query_grad_ref, key_grad_ref, value_grad_ref)):
        total_ref[:, i * width : (i + 1) * width] += dot(turned, ref[...])
    if not ends:
        return

    @pl.when(pl.program_id(0) == pl.num_programs(0) - 1)
    def _():
        gain_ref, gain_two_grad_ref, w_ref, summary_ref, standard_ref, gain_sum_ref = fixed

        def all_far(here, before):
            here = here[...].reshape(-1, width)
            if before is not None:
                here = jnp.concatenate([before[...].reshape(-1, width), here], axis=0)
            return here.astype(HALF)

        key_low = all_far(key_far_grad_ref, earlier and earlier[1])
        value_low = all_far(value_far_grad_ref, earlier and earlier[2])
        gain = gain_ref[...]
        matched = jnp.zeros((width, width), SINGLE)
        flat_ref[:TAIL] = jnp.zeros((TAIL, width), HALF)
        for i in range(3):
            total = total_ref[:, i * width : (i + 1) * width]
            matched = matched + total * w_ref[:, i * width : (i + 1) * width].astype(SINGLE)
            grad = total * gain
            if i > 0:
                grad = grad + dot_outer(summary_ref[...], key_low if i == 1 else value_low)
            flat_ref[TAIL + i * width : TAIL + (i + 1) * width] = grad.astype(HALF)
            if i == 2:
                small_ref[8:] = grad[width - TAIL :]
        copies = start_pieces(plan, flat_ref, pieces, sems, index_ref[0])
        summary_grad = dot_rows(key_low, w_ref[:, width : 2 * width]) + dot_rows(
            value_low, w_ref[:, 2 * width :]
        )
        standard = standard_ref[...]
        standard_grad = summary_grad * gain_sum_ref[...]
        standard_grad_ref[...] = standard_grad

        def fold(value):
            return jnp.sum(value, axis=0, keepdims=True)

        small_ref[0:1] = fold(standard_grad)
        small_ref[1:2] = fold(standard_grad * standard)
        small_ref[2:3] = fold(matched.T)
        small_ref[3:4] = fold(summary_grad * standard)
        small_ref[4:5] = fold(summary_grad)
        small_ref[5:6] = gain_two_grad_ref[...]
        small_ref[6:8] = jnp.zeros((2, width), SINGLE)
        for copy in copies:
            copy.wait()


def attention_backward(
    group,
    previous,
    index,
    block_in,
    query,
    key,
    value,
    key_far,
    value_far,
    probs,
    mixed_grad,
    last,
    local_rows,
    columns,
    plan,
    shapes,
):
    tokens, width = query.shape
    images, far, _ = key_far.shape
    first_image, count = group
    begins, ends = first_image == 0, first_image + count == images
    rows_per_step = math.gcd(local_rows, 2)
    per_image = local_rows // rows_per_step
    first_step = first_image * per_image
    size = rows_per_step * columns
    part = count * tokens // images
    block = pl.BlockSpec((size, width), lambda i, _: (first_step + i, 0))
    far_block = pl.BlockSpec((None, far, width), lambda i, _: (first_image + i // per_image, 0, 0))
    probs_block = pl.BlockSpec(
        (rows_per_step, HEADS, columns + far, columns), lambda i, _: (first_step + i, 0, 0, 0)
    )
    inputs = [block_in, query, key, value, key_far, value_far, probs, mixed_grad]
    in_specs = [block] * 4 + [far_block] * 2 + [probs_block, block]
    aliases = {}
    total_shape = (width, 3 * width)
    far_shape = (count, far, width)
    if previous is not None:
        sums = list(previous[3:])
        inputs = inputs + sums
        in_specs = in_specs + [whole_block(array.shape) for array in sums]
        kept, kept_specs, aliases = kept_arrays(previous[:3], 1 + len(inputs))
        inputs, in_specs = inputs + kept, in_specs + kept_specs
    out_specs = [block] * 3
    out_shape = [jax.ShapeDtypeStruct((tokens, width), HALF)] * 3
    scratch = []
    if ends:
        inputs = inputs + list(last)
        in_specs = in_specs + [whole_block(array.shape) for array in last]
        piece_specs, piece_shapes = piece_outputs(shapes)
        summaries = images * far
        out_specs += [whole_block((summaries, width)), whole_block((8 + TAIL, width))] + piece_specs
        out_shape += [
            jax.ShapeDtypeStruct((summaries, width), SINGLE),
            jax.ShapeDtypeStruct((8 + TAIL, width), SINGLE),
        ] + piece_shapes
        scratch = [
            pltpu.VMEM(total_shape, SINGLE),
            pltpu.VMEM(far_shape, SINGLE),
            pltpu.VMEM(far_shape, SINGLE),
            pltpu.VMEM((TAIL + 3 * width, width), HALF),
            pltpu.SemaphoreType.DMA((len(plan),)),
        ]
    else:
        out_specs += [whole_block(total_shape), whole_block(far_shape), whole_block(far_shape)]
        out_shape += [
            jax.ShapeDtypeStruct(total_shape, SINGLE),
            jax.ShapeDtypeStruct(far_shape, SINGLE),
            jax.ShapeDtypeStruct(far_shape, SINGLE),
        ]
    return pl.pallas_call(
        functools.partial(
            attention_backward_kernel,
            1.0 / math.sqrt(width // HEADS),
            rows_per_step,
            per_image,
            plan,
            begins,
            ends,
        ),
        grid_spec=pltpu.PrefetchScalarGridSpec(
            num_scalar_prefetch=1,
            grid=(count * per_image,),
            in_specs=in_specs,
            out_specs=out_specs,
            scratch_shapes=scratch,
        ),
        out_shape=out_shape,
        input_output_aliases=aliases,
        compiler_params=pltpu.CompilerParams(vmem_limit_bytes=VMEM_BYTES),
        cost_estimate=pl.CostEstimate(
            flops=part * width * (6 * width + 16 * (columns + far)),
            bytes_accessed=part * width * 16 + part * HEADS * (columns + far) * 2,
            transcendentals=0,
        ),
        name="attention_backward",
    )(index, *inputs)


def input_grad_kernel(
    rows_per_step,
    block_ref,
    gain_ref,
    query_grad_ref,
    key_grad_ref,
    value_grad_ref,
    w_ref,
    middle_grad_ref,
    mean_grad_ref,
    out_ref,
):
    width = block_ref.shape[1]
    columns = block_ref.shape[0] // rows_per_step

    attn_grad = (
        dot_rows(query_grad_ref[...], w_ref[:, :width])
        + dot_rows(key_grad_ref[...], w_ref[:, width : 2 * width])
        + dot_rows(value_grad_ref[...], w_ref[:, 2 * width :])
    )
    normed, inverse = normalize(block_ref[...].astype(SINGLE))
    total = middle_grad_ref[...] + norm_back(attn_grad * gain_ref[...], normed, inverse)
    for row in range(rows_per_step):
        tokens = slice(row * columns, (row + 1) * columns)
        out_ref[tokens] = total[tokens] + mean_grad_ref[row : row + 1]


def input_grads(
    group,
    previous,
    block_in,
    gain,
    query_grad,
    key_grad,
    value_grad,
    w_qkv,
    middle_grad,
    mean_grad,
    local_rows,
    columns,
):
    tokens, width = block_in.shape
    images = mean_grad.shape[0]
    first_image, count = group
    rows_per_step = math.gcd(local_rows, 2)
    per_image = local_rows // rows_per_step
    first_step = first_image * per_image
    size = rows_per_step * columns
    part = count * tokens // images
    block = pl.BlockSpec((size, width), lambda i: (first_step + i, 0))
    inputs = [block_in, gain, query_grad, key_grad, value_grad, w_qkv, middle_grad]
    inputs = inputs + [mean_grad.reshape(tokens // size, rows_per_step, width)]
    kept, kept_specs, aliases = kept_arrays(None if previous is None else [previous], len(inputs))
    kernel = functools.partial(input_grad_kernel, rows_per_step)

    def body(*refs):
        kernel(*refs[: len(inputs)], *refs[len(inputs) + len(kept) :])

    return pl.pallas_call(
        body,
        grid=(count * per_image,),
        in_specs=[block, whole_block((1, width))]
        + [block] * 3
        + [whole_block((width, 3 * width)), block]
        + [pl.BlockSpec((None, rows_per_step, width), lambda i: (first_step + i, 0, 0))]
        + kept_specs,
        out_specs=block,
        out_shape=jax.ShapeDtypeStruct((tokens, width), SINGLE),
        input_output_aliases=aliases,
        compiler_params=pltpu.CompilerParams(vmem_limit_bytes=VMEM_BYTES),
        cost_estimate=pl.CostEstimate(
            flops=part * width * 6 * width, bytes_accessed=part * width * 16, transcendentals=0
        ),
        name="input_grads",
    )(*inputs, *kept)


def assemble(flat_ref, pieces, index, block, count):
    plane = 8 * block
    width = flat_ref.shape[1]
    for at in range(0, count * plane + 1, block):
        flat_ref[at : at + TAIL] = jnp.zeros((TAIL, width), HALF)
    for ref, mask, first in pieces:
        spot = pl.multiple_of((index ^ mask) * block, TAIL)
        for slot in range(count):
            part = ref.at[slot] if len(ref.shape) == 3 else ref
            last = first + part.shape[0]
            for low, high in ((0, TAIL), (TAIL, block), (block, block + TAIL)):
                low, high = max(low, first), min(high, last)
                if low >= high:
                    continue
                rows = pl.ds(spot + (slot * plane + low), high - low)
                value = part[low - first : high - first]
                if low < TAIL or low >= block:
                    value = flat_ref[rows] + value
                flat_ref[rows] = value


def projection_weights_kernel(masks, block, index_ref, tail_ref, summary_ref, *refs):
    *piece_refs, w_ref, key_far_ref, value_far_ref, flat_ref = refs
    width = flat_ref.shape[1]
    pieces = [(ref, mask, first) for ref, (mask, first) in zip(piece_refs, masks)]
    assemble(flat_ref, pieces, lax.rem(index_ref[0], 8), block, 1)
    flat_ref[3 * width :] += tail_ref[...]
    for i in range(3):
        w_ref[:, i * width : (i + 1) * width] = flat_ref[TAIL + i * width : TAIL + (i + 1) * width]
    key_far_ref[...] = dot(summary_ref[...], w_ref[:, width : 2 * width]).astype(HALF)
    value_far_ref[...] = dot(summary_ref[...], w_ref[:, 2 * width :]).astype(HALF)


def vmem_specs(count):
    return [pl.BlockSpec(memory_space=pltpu.VMEM)] * count


def projection_weights(index, tail, summary_low, pieces, block):
    width = tail.shape[1]
    arrays, masks = [p[0] for p in pieces], [p[1:] for p in pieces]
    far = summary_low.shape[0]
    return pl.pallas_call(
        functools.partial(projection_weights_kernel, masks, block),
        in_specs=[pl.BlockSpec(memory_space=pltpu.SMEM)] + vmem_specs(2 + len(arrays)),
        out_specs=vmem_specs(3),
        out_shape=[
            jax.ShapeDtypeStruct((width, 3 * width), HALF),
            jax.ShapeDtypeStruct((far, width), HALF),
            jax.ShapeDtypeStruct((far, width), HALF),
        ],
        scratch_shapes=[pltpu.VMEM((TAIL + 3 * width, width), HALF)],
        compiler_params=pltpu.CompilerParams(vmem_limit_bytes=VMEM_BYTES),
        name="projection_weights",
    )(index, tail, summary_low, *arrays)


def hidden_weights_kernel(masks, block, index_ref, *refs):
    *piece_refs, w_out_ref, w_inner_ref, w_outer_ref, flat_ref = refs
    width, hidden = w_inner_ref.shape
    pieces = [(ref, mask, first) for ref, (mask, first) in zip(piece_refs, masks)]
    assemble(flat_ref, pieces, lax.rem(index_ref[0], 8), block, 3)
    groups = hidden // width
    per = 256 // groups
    w_out_ref[...] = flat_ref[TAIL : TAIL + width]
    mix = weave(groups, per)
    for c in range(width // per):
        start = TAIL + width + c * groups * per
        parted = dot_outer(mix, flat_ref[start : start + groups * per]).astype(HALF)
        for g in range(groups):
            w_inner_ref[c * per : (c + 1) * per, g * width : (g + 1) * width] = parted[
                g * per : (g + 1) * per
            ]
    w_outer_ref[...] = flat_ref[TAIL + width + hidden :]


def hidden_weights(index, pieces, block, width, hidden):
    arrays, masks = [p[0] for p in pieces], [p[1:] for p in pieces]
    return pl.pallas_call(
        functools.partial(hidden_weights_kernel, masks, block),
        in_specs=[pl.BlockSpec(memory_space=pltpu.SMEM)] + vmem_specs(len(arrays)),
        out_specs=vmem_specs(3),
        out_shape=[
            jax.ShapeDtypeStruct((width, width), HALF),
            jax.ShapeDtypeStruct((width, hidden), HALF),
            jax.ShapeDtypeStruct((hidden, width), HALF),
        ],
        scratch_shapes=[pltpu.VMEM((TAIL + width + 2 * hidden, width), HALF)],
        compiler_params=pltpu.CompilerParams(vmem_limit_bytes=VMEM_BYTES),
        name="hidden_weights",
    )(index, *arrays)


def swap_core(value):
    return swap(value, "row", 1)


def swap_x(value):
    return swap(value, "row", 2)


def swap_y(value):
    return swap(value, "img", 1)


def swap_near(value):
    return swap(value, "img", 2)


def swap_far(value):
    return swap(value, "img", 4)


def send_down(value, distance):
    size = lax.axis_size("img")
    senders = [i for i in range(size) if i & distance and not i & (distance - 1) & ~1]
    return lax.ppermute(value, "img", [(i, i ^ distance) for i in senders])


def corners(over_x, over_y, split):
    rows = over_x.ndim - 2
    first = lax.slice_in_dim(over_x, 0, split, axis=rows)
    second = lax.slice_in_dim(over_y, split, over_y.shape[rows], axis=rows)
    return (swap_y(first), swap_x(second))


def with_cores(value, over_x, over_y, corner_first, corner_second, split):
    near = [(value, 0, 0), (over_x, 2, 0), (over_y, 4, 0), (corner_first, 6, 0), (corner_second, 6, split)]
    return near + [(swap_core(array), mask | 1, first) for array, mask, first in near]


def sum_planes(value):
    far = lax.ppermute(value, "img", [(i, i ^ 6) for i in range(lax.axis_size("img"))])
    return value + swap_near(value) + swap_far(value) + far


def sum_core(kept, sent):
    return kept.astype(SINGLE) + swap_core(sent).astype(SINGLE)


def sum_sides(near, split):
    first, second = near[..., :split, :], near[..., split:, :]
    first_in = swap_y(first[2:].astype(HALF))
    second_in = swap_x(second[1::2].astype(HALF))
    return (first[:2] + first_in.astype(SINGLE), second[::2] + second_in.astype(SINGLE))


def sum_corners(first, second):
    first = first[0] + swap_x(first[1].astype(HALF)).astype(SINGLE)
    second = second[0] + swap_y(second[1].astype(HALF)).astype(SINGLE)
    return jnp.concatenate([first, second], axis=-2)


def together(*values):
    return lax.optimization_barrier(values)


def fits_planes(width, block):
    return lax.axis_size("row") == 4 and lax.axis_size("img") == 8 and 8 * block == 3 * width


def own_rows(weights, width):
    length = weights.shape[0]
    block, rest = length // width, length % width
    start = TAIL * width + rest * device_index() - 4 * width
    own = lax.dynamic_update_slice(jnp.zeros(((block + TAIL) * width,), HALF), weights, (start,))
    return own.reshape(block + TAIL, width), start


def per_device(activations, cotangent, weights):
    images, local_rows, columns, width = activations.shape
    tokens = images * local_rows * columns
    size = tokens // images
    rows_all = local_rows * lax.axis_size("row")
    far = images * rows_all
    first_row = lax.axis_index("row") * local_rows
    summary_count = float(images * lax.axis_size("img") * rows_all)
    block = weights.shape[0] // width
    planes = fits_planes(width, block)
    split = block // 2 // TAIL * TAIL
    me = device_index()
    index = me[None]
    z = lax.axis_index("img") // 2
    block_in = activations.reshape(tokens, width)

    row_means = jnp.mean(activations.astype(SINGLE), axis=2)
    if planes:
        own, start = own_rows(weights, width)
        shown = jnp.concatenate(
            [
                jnp.where(me == 0, own[TAIL - 4 : TAIL].astype(SINGLE), 0.0),
                jnp.where(me == 8, own[:TAIL].astype(SINGLE), 0.0),
            ]
        )
    else:
        gathered, matrix_rows = gather_weights(weights, width)
        shown = jnp.zeros((4 + TAIL, width), SINGLE)
    all_means, shown = gather_rows(row_means, shown)
    sums = jnp.stack([jnp.sum(all_means, axis=(0, 1)), jnp.sum(all_means * all_means, axis=(0, 1))])
    sums = jnp.concatenate([sums, shown])
    if planes:
        over_far, sums = together(swap_far(own), sums)
        over_near = swap_near(jnp.stack([own, over_far]))
        over_near, sums = together(over_near, sums + swap_y(sums))
        held = jnp.stack([own, over_near[0], over_far, over_near[1]])
        first_slot = lax.dynamic_index_in_dim(held, z, 0, keepdims=False)
        first_x, first_y = swap_x(first_slot), swap_y(first_slot)
        first_x, first_y, sums = together(first_x, first_y, sum_planes(sums))
        corner_x, corner_y = corners(first_x, first_y, split)
        other_slots = jnp.stack(
            [lax.dynamic_index_in_dim(held, z ^ i, 0, keepdims=False) for i in (1, 2, 3)]
        )
        corner_x, corner_y, other_slots, sums = together(corner_x, corner_y, other_slots, sums)
        first_pieces = with_cores(first_slot, first_x, first_y, corner_x, corner_y, split)
        other_x, other_y = swap_x(other_slots), swap_y(other_slots)
    else:
        for axis, distance, _ in image_hops():
            sums = sums + swap(sums, axis, distance)
    summary_mean = sums[0] / summary_count
    summary_var = sums[1] / summary_count - summary_mean * summary_mean
    summary_inv = lax.rsqrt(summary_var + EPS)
    standard = (all_means - summary_mean) * summary_inv
    vectors = sums[2:6] if planes else gathered.astype(SINGLE)
    gain_one, gain_sum, bias_sum, gain_two = (vectors[i : i + 1] for i in range(4))
    summary_low = (standard * gain_sum + bias_sum).astype(HALF).reshape(far, width)

    if planes:
        w_qkv, key_far, value_far = projection_weights(
            index, sums[6:].astype(HALF), summary_low, first_pieces, block
        )
    else:
        w_qkv, w_out, w_inner, w_outer = unpack(matrix_rows, width, FF)
        key_far = dot(summary_low, w_qkv[:, width : 2 * width]).astype(HALF)
        value_far = dot(summary_low, w_qkv[:, 2 * width :]).astype(HALF)
    key_far = key_far.reshape(images, rows_all, width)
    value_far = value_far.reshape(images, rows_all, width)

    forward = None
    for group in image_groups(images):
        forward = attention_forward(
            group,
            forward,
            block_in,
            gain_one,
            w_qkv,
            key_far,
            value_far,
            first_row[None],
            local_rows,
            columns,
        )
        if planes and group[0] == 0:
            other_x, other_y, forward = together(other_x, other_y, forward)
            other_corners = corners(other_x, other_y, split)
    if planes:
        other_corners, forward = together(other_corners, forward)
        other_pieces = with_cores(other_slots, other_x, other_y, *other_corners, split)
    query, key, value, mixed, probs = forward

    if planes:
        w_out, w_inner, w_outer = hidden_weights(index, other_pieces, block, width, FF)
        late_plan, early_plan = [], []
        for side in range(2):
            for place, mask in enumerate((0, 2, 4, 6)):

                def offset(i, mask=mask | side):
                    return lax.rem(i, 8) ^ mask

                late_plan.append((side, (place,), lambda i, at=offset: at(i) * block, block + TAIL))
                for slot in range(3):
                    early_plan.append(
                        (
                            side,
                            (place, slot),
                            lambda i, at=offset, slot=slot: (slot * 8 + at(i)) * block,
                            block + TAIL,
                        )
                    )
        early_shapes = [(4, 3, block + TAIL, width)] * 2
        late_shapes = [(4, block + TAIL, width)] * 2
    else:
        early_shapes = [(TAIL + width + 2 * FF, width)]
        late_shapes = [(TAIL + 3 * width, width)]
        early_plan = [(0, (), lambda i: i * 0, early_shapes[0][0])]
        late_plan = [(0, (), lambda i: i * 0, late_shapes[0][0])]

    out, middle_grad, mixed_grad, gain_two_grad, *early = feed_forward(
        index,
        block_in,
        mixed,
        cotangent.reshape(tokens, width),
        gain_two,
        w_out,
        w_inner,
        w_outer,
        size,
        early_plan,
        early_shapes,
    )
    standard_flat = standard.reshape(far, width)
    last = [gain_one.reshape(width, 1), gain_two_grad, w_qkv, summary_low, standard_flat, gain_sum]
    backward = None
    for group in image_groups(images):
        backward = attention_backward(
            group,
            backward,
            index,
            block_in,
            query,
            key,
            value,
            key_far,
            value_far,
            probs,
            mixed_grad,
            last,
            local_rows,
            columns,
            late_plan,
            late_shapes,
        )
        if planes and group[0] == 0:
            early, backward = together(sum_core(*early), backward)
    if planes:
        early, backward = together(sum_sides(early, split), backward)
    query_grad, key_grad, value_grad, standard_grad, small, *late = backward
    shared = jnp.concatenate([standard_grad, small])
    if planes:
        early, late, shared = together(
            sum_corners(*early), sum_core(*late), shared + swap_core(shared)
        )
        padded = jnp.concatenate([jnp.zeros_like(early[:1]), early])
        by_mask = [lax.dynamic_index_in_dim(padded, z ^ i, 0, keepdims=False) for i in range(4)]
        early_in = swap_near(jnp.stack([by_mask[1], by_mask[3]]).astype(HALF))
        small = shared[far:]
        across = lax.ppermute(small, ("img", "row"), [(i, i ^ 6) for i in range(32)])
        over_x = swap_x(shared)
        small = small + over_x[far:] + swap_y(small) + across
        late, small, shared = together(sum_sides(late, split), small, shared[:far] + over_x[:far])
        late, small, early_in = together(sum_corners(*late), sum_planes(small), early_in)
    else:
        for axis, distance, _ in row_hops():
            shared = shared + swap(shared, axis, distance)
        small = shared[far:]
        for axis, distance, _ in image_hops():
            small = small + swap(small, axis, distance)
    own_grad = lax.dynamic_slice_in_dim(
        shared[:far].reshape(images, rows_all, width), first_row, local_rows, axis=1
    )
    own_standard = lax.dynamic_slice_in_dim(standard, first_row, local_rows, axis=1)
    mean_grad = summary_inv * (
        own_grad - small[0] / summary_count - own_standard * (small[1] / summary_count)
    )
    input_grad = None
    for group in image_groups(images):
        input_grad = input_grads(
            group,
            input_grad,
            block_in,
            gain_one,
            query_grad,
            key_grad,
            value_grad,
            w_qkv,
            middle_grad,
            mean_grad / columns,
            local_rows,
            columns,
        )
        if planes and group[0] == 0:
            late = late + send_down(late.astype(HALF), 2).astype(SINGLE)
            early_own = by_mask[0] + early_in[0].astype(SINGLE)
            early_far = swap_far((by_mask[2] + early_in[1].astype(SINGLE)).astype(HALF))
            late, input_grad = together(late, input_grad)
    if planes:
        late_own = late + send_down(late.astype(HALF), 4).astype(SINGLE)
        early_own = early_own + early_far.astype(SINGLE)
        head = jnp.where(
            me == 0,
            jnp.concatenate([jnp.zeros((TAIL - 4, width), SINGLE), small[2:6]]),
            jnp.where(me == 8, small[8:], 0.0),
        )
        mine = jnp.where(z == 0, late_own, early_own)
        mine = jnp.concatenate([mine[:TAIL] + head, mine[TAIL:]])
        weight_grad = lax.dynamic_slice(mine.reshape(-1), (start,), weights.shape)
    else:
        grad_rows = jnp.concatenate([late[0][TAIL:], early[0][TAIL:]]).astype(SINGLE)
        weight_grad = scatter_grads(small[2:6], grad_rows, weights.shape[0])
    return (
        out.reshape(activations.shape),
        input_grad.reshape(activations.shape),
        weight_grad,
        summary_mean,
        summary_var,
    )


def solution(mesh):
    placed = (P("img", "row", None, None), P("img", "row", None, None), P(("img", "row")))
    return jax.shard_map(
        per_device,
        mesh=mesh,
        in_specs=placed,
        out_specs=(
            P("img", "row", None, None),
            P("img", "row", None, None),
            P(("img", "row")),
            P(),
            P(),
        ),
        check_vma=False,
    )
```

```python
import functools
import math

import jax
import jax.numpy as jnp
from jax import lax
from jax.experimental import pallas as pl
from jax.experimental.pallas import tpu as pltpu
from jax.sharding import PartitionSpec as P

FF = 2048
HEADS = 8
LANES = 128


EPS = 1e-05
NEGATIVE = -1e30
HALF = jnp.bfloat16
SINGLE = jnp.float32
VMEM_BYTES = 56 * 1024 * 1024

TAIL = 16


def swap(value, axis, distance):
    size = lax.axis_size(axis)
    return lax.ppermute(value, axis, [(i, i ^ distance) for i in range(size)])


def hops():
    rows, images = lax.axis_size("row"), lax.axis_size("img")
    inner = ("row", 1, 1)
    across = ("row", 2, 2)
    along = ("img", 1, rows)
    outer = []
    distance = images // 2
    while distance > 1:
        outer.append(("img", distance, distance * rows))
        distance //= 2
    distance = rows // 2
    while distance > 2:
        outer.append(("row", distance, distance))
        distance //= 2
    return inner, across, along, outer


def piece_order():
    inner, across, along, outer = hops()
    masks = [0]
    for _, _, mask in outer:
        masks = masks + [m ^ mask for m in masks]
    near = (
        masks
        + [m ^ across[2] for m in masks]
        + [m ^ along[2] for m in masks]
        + [m ^ across[2] ^ along[2] for m in masks]
    )
    return near + [m ^ inner[2] for m in near]


def device_index():
    return lax.axis_index("img") * lax.axis_size("row") + lax.axis_index("row")


def gather_pieces(own):
    inner, across, along, outer = hops()
    held = own[None]
    for axis, distance, _ in outer:
        held = jnp.concatenate([held, swap(held, axis, distance)])
    half = held.shape[0] // 2
    held_x = swap(held, across[0], across[1])
    held_y = swap(held, along[0], along[1])
    corner_first = swap(held_x[:half], along[0], along[1])
    corner_second = swap(held_y[half:], across[0], across[1])
    near = [held, held_x, held_y, corner_first, corner_second]
    far = [swap(part, inner[0], inner[1]) for part in near]
    return jnp.concatenate(near + far)


def scatter_pieces(pieces):
    inner, across, along, outer = hops()

    def add(kept, sent, axis, distance):
        return kept + swap(sent.astype(HALF), axis, distance).astype(SINGLE)

    count = pieces.shape[0] // 2
    near = add(pieces[:count], pieces[count:], inner[0], inner[1])
    quarter = count // 4
    half = quarter // 2
    held, held_x, held_y, corner = (near[i * quarter : (i + 1) * quarter] for i in range(4))
    first = add(
        jnp.concatenate([held[:half], held_x[:half]]),
        jnp.concatenate([held_y[:half], corner[:half]]),
        along[0],
        along[1],
    )
    second = add(
        jnp.concatenate([held[half:], held_y[half:]]),
        jnp.concatenate([held_x[half:], corner[half:]]),
        across[0],
        across[1],
    )
    first = add(first[:half], first[half:], across[0], across[1])
    second = add(second[:half], second[half:], along[0], along[1])
    held = jnp.concatenate([first, second])
    for axis, distance, _ in reversed(outer):
        half = held.shape[0] // 2
        held = add(held[:half], held[half:], axis, distance)
    return held[0]


def row_hops():
    inner, across, _, outer = hops()
    return [inner, across] + [hop for hop in outer if hop[0] == "row"]


def image_hops():
    _, _, along, outer = hops()
    return [along] + [hop for hop in outer if hop[0] == "img"]


def gather_rows(own, shown):
    width = own.shape[-1]
    count = shown.shape[0]
    held, masks = own[None], [0]
    for axis, distance, mask in row_hops():
        got = swap(jnp.concatenate([held.reshape(-1, width), shown]), axis, distance)
        held = jnp.concatenate([held, got[:-count].reshape(held.shape)])
        shown = shown + got[-count:]
        masks = masks + [m ^ mask for m in masks]
    place = [0] * len(masks)
    for at, mask in enumerate(masks):
        place[mask] = at
    order = jnp.asarray(place, jnp.int32)[jnp.arange(len(masks)) ^ lax.axis_index("row")]
    held = jnp.moveaxis(jnp.take(held, order, axis=0, mode="clip"), 0, 1)
    return held.reshape(own.shape[0], -1, width), shown


def gather_weights(weights, model_width):
    length = weights.shape[0]
    me = device_index()
    devices = lax.axis_size("img") * lax.axis_size("row")
    block = length // model_width
    rest = length % model_width
    start = TAIL * model_width + rest * me - 4 * model_width
    own = lax.dynamic_update_slice(jnp.zeros(((block + TAIL) * model_width,), HALF), weights, (start,))
    own = own.reshape(block + TAIL, model_width)
    pieces = gather_pieces(own)
    place = [0] * devices
    for at, mask in enumerate(piece_order()):
        place[mask] = at
    order = jnp.asarray(place, jnp.int32)[jnp.arange(devices) ^ me]
    pieces = jnp.take(pieces, order, axis=0, mode="clip")
    tails = jnp.concatenate([pieces[1:, :TAIL], jnp.zeros((1, TAIL, model_width), HALF)])
    body = jnp.concatenate([pieces[:, TAIL:block], pieces[:, block:] + tails], axis=1)
    return pieces[0, TAIL - 4 : TAIL], body.reshape(devices * block, model_width)


def scatter_grads(vectors, rows, length):
    model_width = rows.shape[1]
    me = device_index()
    devices = lax.axis_size("img") * lax.axis_size("row")
    block = length // model_width
    rest = length % model_width
    whole = jnp.concatenate([jnp.zeros((TAIL - 4, model_width), SINGLE), vectors, rows])
    place = jnp.asarray(piece_order(), jnp.int32)
    pieces = jnp.stack([whole[block * s : block * s + block + TAIL] for s in range(devices)])
    pieces = jnp.take(pieces, place ^ me, axis=0, mode="clip")
    mine = scatter_pieces(pieces)
    start = TAIL * model_width + rest * me - 4 * model_width
    return lax.dynamic_slice(mine.reshape(-1), (start,), (length,))


def dot(left, right):
    return jnp.dot(left, right, preferred_element_type=SINGLE)


def dot_rows(left, right):
    return lax.dot_general(left, right, (((1,), (1,)), ((), ())), preferred_element_type=SINGLE)


def dot_outer(left, right):
    return lax.dot_general(left, right, (((0,), (0,)), ((), ())), preferred_element_type=SINGLE)


def normalize(values):
    centred = values - jnp.mean(values, axis=-1, keepdims=True)
    inverse = lax.rsqrt(jnp.mean(centred * centred, axis=-1, keepdims=True) + EPS)
    return (centred * inverse, inverse)


def norm_back(grad_norm, normed, inverse):
    return inverse * (
        grad_norm
        - jnp.mean(grad_norm, axis=-1, keepdims=True)
        - normed * jnp.mean(grad_norm * normed, axis=-1, keepdims=True)
    )


def whole_block(shape):
    return pl.BlockSpec(shape, lambda *_: (0,) * len(shape), pipeline_mode=pl.Buffered(1))


def head_keys(rows_per_step, model_width):
    return [
        (row, pair, half)
        for row in range(rows_per_step)
        for pair in range(model_width // LANES)
        for half in range(2)
    ]


def attention_forward_kernel(
    scaling,
    rows_per_step,
    local_rows,
    first_row_ref,
    block_ref,
    gain_ref,
    w_ref,
    key_far_ref,
    value_far_ref,
    causal_ref,
    query_ref,
    key_ref,
    value_ref,
    mixed_ref,
    probs_ref,
):
    columns = causal_ref.shape[0]
    far = key_far_ref.shape[0]
    width = block_ref.shape[1]
    head_width = width // HEADS
    step = pl.program_id(0)
    normed, _ = normalize(block_ref[...].astype(SINGLE))
    attn_in = (normed * gain_ref[...]).astype(HALF)
    for i, ref in enumerate((query_ref, key_ref, value_ref)):
        ref[...] = dot(attn_in, w_ref[:, i * width : (i + 1) * width]).astype(HALF)
    first_half = lax.broadcasted_iota(jnp.int32, (columns + far, LANES), 1) < head_width
    far_index = lax.broadcasted_iota(jnp.int32, (far, columns), 0)
    keys = head_keys(rows_per_step, width)
    for start in range(0, len(keys), HEADS):
        group = keys[start : start + HEADS]
        scores, low, mixed = {}, {}, {}
        for row, pair, half in group:
            global_row = first_row_ref[0] + lax.rem(step * rows_per_step + row, local_rows)
            far_bias = jnp.where(far_index < global_row, 0.0, NEGATIVE)
            tokens = slice(row * columns, (row + 1) * columns)
            lanes = slice(pair * LANES, (pair + 1) * LANES)
            all_keys = jnp.concatenate([key_ref[tokens, lanes], key_far_ref[:, lanes]], axis=0)
            one_head = jnp.where(
                first_half if half == 0 else ~first_half, all_keys, jnp.zeros_like(all_keys)
            )
            found = dot_rows(one_head, query_ref[tokens, lanes])
            scores[row, pair, half] = jnp.concatenate(
                [found[:columns] + causal_ref[...], found[columns:] + far_bias], axis=0
            )
        for row, pair, half in group:
            found = scores.pop((row, pair, half))
            top = jnp.max(found, axis=0, keepdims=True)
            powers = jnp.exp((found - top) * scaling)
            inverse = 1.0 / jnp.sum(powers, axis=0, keepdims=True)
            low[row, pair, half] = (powers * inverse).astype(HALF)
            probs_ref[row, 2 * pair + half] = low[row, pair, half]
        for row, pair, half in group:
            tokens = slice(row * columns, (row + 1) * columns)
            lanes = slice(pair * LANES, (pair + 1) * LANES)
            all_values = jnp.concatenate([value_ref[tokens, lanes], value_far_ref[:, lanes]], axis=0)
            turned = all_values.T[half * head_width : (half + 1) * head_width]
            mixed[row, pair, half] = dot(turned, low[row, pair, half])
        for row, pair, half in group:
            if half == 0:
                tokens = slice(row * columns, (row + 1) * columns)
                lanes = slice(pair * LANES, (pair + 1) * LANES)
                both = jnp.concatenate([mixed[row, pair, 0], mixed[row, pair, 1]], axis=0)
                mixed_ref[tokens, lanes] = both.T.astype(HALF)


def image_groups(images):
    return [(0, 1), (1, images - 1)] if images > 1 else [(0, images)]


def step_groups(steps):
    if steps < 4:
        return [(0, steps)]
    first, last = steps // 3, max(1, steps // 6)
    return [(0, first), (first, steps - first - last), (steps - last, last)]


def kept_arrays(previous, start):
    if previous is None:
        return ([], [], {})
    specs = [pl.BlockSpec(memory_space=pl.ANY)] * len(previous)
    return (list(previous), specs, {start + i: i for i in range(len(previous))})


def attention_forward(
    group, previous, block_in, gain, w_qkv, key_far, value_far, first_row, local_rows, columns
):
    tokens, width = block_in.shape
    images, far, _ = key_far.shape
    first_image, count = group
    rows_per_step = math.gcd(local_rows, 2)
    steps = local_rows // rows_per_step
    first_step = first_image * steps
    size = rows_per_step * columns
    position = jnp.arange(columns)
    causal = jnp.where(position[:, None] <= position[None, :], 0.0, NEGATIVE).astype(SINGLE)
    block = pl.BlockSpec((size, width), lambda i, _: (first_step + i, 0))
    far_block = pl.BlockSpec((None, far, width), lambda i, _: (first_image + i // steps, 0, 0))
    probs_block = pl.BlockSpec(
        (rows_per_step, HEADS, columns + far, columns), lambda i, _: (first_step + i, 0, 0, 0)
    )
    inputs = [block_in, gain, w_qkv, key_far, value_far, causal]
    kept, kept_specs, aliases = kept_arrays(previous, 1 + len(inputs))
    low = jax.ShapeDtypeStruct((tokens, width), HALF)
    part = count * tokens // images
    kernel = functools.partial(
        attention_forward_kernel, 1.0 / math.sqrt(width // HEADS), rows_per_step, local_rows
    )

    def body(*refs):
        kernel(*refs[: 1 + len(inputs)], *refs[1 + len(inputs) + len(kept) :])

    return pl.pallas_call(
        body,
        grid_spec=pltpu.PrefetchScalarGridSpec(
            num_scalar_prefetch=1,
            grid=(count * steps,),
            in_specs=[
                block,
                whole_block((1, width)),
                whole_block((width, 3 * width)),
                far_block,
                far_block,
                whole_block((columns, columns)),
            ]
            + kept_specs,
            out_specs=[block] * 4 + [probs_block],
        ),
        out_shape=[low] * 4
        + [jax.ShapeDtypeStruct((images * local_rows, HEADS, columns + far, columns), HALF)],
        input_output_aliases=aliases,
        compiler_params=pltpu.CompilerParams(vmem_limit_bytes=VMEM_BYTES),
        cost_estimate=pl.CostEstimate(
            flops=part * width * (6 * width + 8 * (columns + far)),
            bytes_accessed=part * width * 12 + part * HEADS * (columns + far) * 2,
            transcendentals=part * HEADS * (columns + far),
        ),
        name="attention_forward",
    )(first_row, *inputs, *kept)


GELU_OUTER = math.sqrt(2.0 / math.pi)
GELU_CUBE = 0.044715


def gelu_and_slope(value):
    square = value * value
    gate = 0.5 * jnp.tanh(value * (GELU_OUTER * GELU_CUBE * square + GELU_OUTER)) + 0.5
    activated = value * gate
    slope = gate + activated * (1.0 - gate) * (6.0 * GELU_OUTER * GELU_CUBE * square + 2.0 * GELU_OUTER)
    return (activated, slope)


def start_pieces(plan, flat_ref, outs, sems, index):
    copies = []
    for i, (out, place, offset, rows) in enumerate(plan):
        source = flat_ref.at[pl.ds(pl.multiple_of(offset(index), TAIL), rows)]
        target = outs[out].at[place] if place else outs[out]
        copies.append(pltpu.make_async_copy(source, target, sems.at[i]))
    for copy in copies:
        copy.start()
    return copies


def feed_forward_kernel(
    chunk,
    plan,
    masks,
    block,
    index_ref,
    block_ref,
    mixed_ref,
    cotangent_ref,
    gain_ref,
    *rest,
):
    given, rest = rest[: len(masks)], rest[len(masks) :]
    out_ref, middle_grad_ref, mixed_grad_ref, grad_gain_ref, *rest = rest
    *pieces, grad_out_ref, grad_inner_ref, grad_outer_ref, w_inner_ref, flat_ref, sems = rest
    width, hidden = w_inner_ref.shape
    groups = hidden // width
    per = 256 // groups
    inner_start = TAIL + width
    outer_start = inner_start + hidden
    w_out_ref = flat_ref.at[TAIL:inner_start]
    w_outer_ref = flat_ref.at[outer_start:]

    @pl.when(pl.program_id(0) == 0)
    def _():
        for ref in (grad_out_ref, grad_inner_ref, grad_outer_ref, grad_gain_ref):
            ref[...] = jnp.zeros_like(ref)
        if block is None:
            flat_ref[...] = given[0][...]
        else:
            placed = [(ref, mask, first) for ref, (mask, first) in zip(given, masks)]
            assemble(flat_ref, placed, lax.rem(index_ref[0], 8), block, 3)
        mix = weave(groups, per)
        for c in range(width // per):
            start = inner_start + c * groups * per
            parted = dot_outer(mix, flat_ref[start : start + groups * per]).astype(HALF)
            for g in range(groups):
                w_inner_ref[c * per : (c + 1) * per, g * width : (g + 1) * width] = parted[
                    g * per : (g + 1) * per
                ]

    mixed = mixed_ref[...]
    cotangent = cotangent_ref[...]
    middle = block_ref[...].astype(SINGLE) + dot(mixed, w_out_ref[...])
    normed, inverse = normalize(middle)
    ff_in = (normed * gain_ref[...]).astype(HALF)
    out = middle
    ff_grad = jnp.zeros_like(middle)
    cotangent_turned = cotangent.T
    ff_turned = ff_in.T
    count = hidden // chunk
    spans = [slice(j * chunk, (j + 1) * chunk) for j in range(count)]

    def products(j):
        return (dot(ff_in, w_inner_ref[:, spans[j]]), dot_rows(cotangent, w_outer_ref[spans[j], :]))

    ready = products(0)
    for j in range(count):
        inner, act_grad = ready
        if j + 1 < count:
            ready = products(j + 1)
        activated, slope = gelu_and_slope(inner)
        activated = activated.astype(HALF)
        inner_grad = (slope * act_grad).astype(HALF)
        out = out + dot(activated, w_outer_ref[spans[j], :])
        ff_grad = ff_grad + dot_rows(inner_grad, w_inner_ref[:, spans[j]])
        grad_inner_ref[:, spans[j]] += dot(ff_turned, inner_grad)
        grad_outer_ref[:, spans[j]] += dot(cotangent_turned, activated)
    out_ref[...] = out.astype(HALF)
    grad_gain_ref[...] += jnp.sum(ff_grad * normed, axis=0, keepdims=True)
    middle_grad = cotangent.astype(SINGLE) + norm_back(ff_grad * gain_ref[...], normed, inverse)
    middle_grad_ref[...] = middle_grad
    branch_grad = middle_grad.astype(HALF)
    mixed_grad_ref[...] = dot_rows(branch_grad, w_out_ref[...]).astype(HALF)
    grad_out_ref[...] += dot_outer(mixed, branch_grad)

    @pl.when(pl.program_id(0) == pl.num_programs(0) - 1)
    def _():
        flat_ref[:TAIL] = jnp.zeros((TAIL, width), HALF)
        flat_ref[TAIL : TAIL + width] = grad_out_ref[...].astype(HALF)
        mix = weave(groups, per)
        for c in range(width // per):
            parts = [
                grad_inner_ref[c * per : (c + 1) * per, g * width : (g + 1) * width].astype(HALF)
                for g in range(groups)
            ]
            start = TAIL + width + c * groups * per
            woven = dot(mix, jnp.concatenate(parts, axis=0))
            flat_ref[start : start + groups * per] = woven.astype(HALF)
        start = TAIL + width + hidden
        for j in range(hidden // width):
            turned = grad_outer_ref[:, j * width : (j + 1) * width].astype(HALF).T
            flat_ref[start + j * width : start + (j + 1) * width] = turned
        for copy in start_pieces(plan, flat_ref, pieces, sems, index_ref[0]):
            copy.wait()


def weave(groups, per):
    size = groups * per
    row = lax.broadcasted_iota(jnp.int32, (size, size), 0)
    column = lax.broadcasted_iota(jnp.int32, (size, size), 1)
    wanted = lax.rem(row, groups) * per + lax.div(row, groups)
    return (wanted == column).astype(SINGLE).astype(HALF)


def piece_outputs(shapes):
    return (
        [pl.BlockSpec(memory_space=pl.ANY)] * len(shapes),
        [jax.ShapeDtypeStruct(shape, HALF) for shape in shapes],
    )


def feed_forward(index, block_in, mixed, cotangent, gain, given, block, hidden, size, plan, shapes):
    tokens, width = block_in.shape
    tile = pl.BlockSpec((size, width), lambda i, _: (i, 0))
    piece_specs, piece_shapes = piece_outputs(shapes)
    masks = [entry[1:] for entry in given]
    return pl.pallas_call(
        functools.partial(feed_forward_kernel, 512, plan, masks, block),
        grid_spec=pltpu.PrefetchScalarGridSpec(
            num_scalar_prefetch=1,
            grid=(tokens // size,),
            in_specs=[tile, tile, tile, whole_block((1, width))] + vmem_specs(len(given)),
            out_specs=[tile, tile, tile, whole_block((1, width))] + piece_specs,
            scratch_shapes=[
                pltpu.VMEM((width, width), SINGLE),
                pltpu.VMEM((width, hidden), SINGLE),
                pltpu.VMEM((width, hidden), SINGLE),
                pltpu.VMEM((width, hidden), HALF),
                pltpu.VMEM((TAIL + width + 2 * hidden, width), HALF),
                pltpu.SemaphoreType.DMA((len(plan),)),
            ],
        ),
        out_shape=[
            jax.ShapeDtypeStruct((tokens, width), HALF),
            jax.ShapeDtypeStruct((tokens, width), SINGLE),
            jax.ShapeDtypeStruct((tokens, width), HALF),
            jax.ShapeDtypeStruct((1, width), SINGLE),
        ]
        + piece_shapes,
        compiler_params=pltpu.CompilerParams(vmem_limit_bytes=VMEM_BYTES),
        cost_estimate=pl.CostEstimate(
            flops=tokens * width * (6 * width + 12 * hidden),
            bytes_accessed=tokens * width * 14 + width * hidden * 8,
            transcendentals=tokens * hidden,
        ),
        name="feed_forward",
    )(index, block_in, mixed, cotangent, gain, *[entry[0] for entry in given])


def attention_backward_kernel(
    scaling,
    rows_per_step,
    per_image,
    first_step,
    plan,
    ends,
    index_ref,
    block_ref,
    query_ref,
    key_ref,
    value_ref,
    key_far_ref,
    value_far_ref,
    probs_ref,
    mixed_grad_ref,
    *rest,
):
    rest = list(rest)
    earlier = None
    if first_step > 0:
        earlier, rest = rest[:3], rest[6:]
    if ends:
        fixed, rest = rest[:6], rest[6:]
    query_grad_ref, key_grad_ref, value_grad_ref, *rest = rest
    if ends:
        shared_ref, *rest = rest
        small_ref = shared_ref.at[shared_ref.shape[0] - 8 - TAIL :]
        *pieces, total_ref, key_far_grad_ref, value_far_grad_ref, flat_ref, sems = rest
    else:
        total_ref, key_far_grad_ref, value_far_grad_ref = rest
    width = query_ref.shape[1]
    head_width = width // HEADS
    far = key_far_ref.shape[0]
    columns = query_ref.shape[0] // rows_per_step
    image = lax.div(first_step + pl.program_id(0), per_image)

    @pl.when(pl.program_id(0) == 0)
    def _():
        for i, ref in enumerate((total_ref, key_far_grad_ref, value_far_grad_ref)):
            ref[...] = jnp.zeros_like(ref) if earlier is None else earlier[i][...]

    first_half = lax.broadcasted_iota(jnp.int32, (columns + far, LANES), 1) < head_width
    keys = head_keys(rows_per_step, width)
    for start in range(0, len(keys), HEADS):
        group = keys[start : start + HEADS]
        prob_grad, score_grad, value_grad, key_grad, query_grad = {}, {}, {}, {}, {}
        for row, pair, half in group:
            tokens = slice(row * columns, (row + 1) * columns)
            lanes = slice(pair * LANES, (pair + 1) * LANES)
            all_values = jnp.concatenate([value_ref[tokens, lanes], value_far_ref[:, lanes]], axis=0)
            one_head = jnp.where(
                first_half if half == 0 else ~first_half, all_values, jnp.zeros_like(all_values)
            )
            prob_grad[row, pair, half] = dot_rows(one_head, mixed_grad_ref[tokens, lanes])
        for row, pair, half in group:
            tokens = slice(row * columns, (row + 1) * columns)
            lanes = slice(pair * LANES, (pair + 1) * LANES)
            value_grad[row, pair, half] = dot(
                probs_ref[row, 2 * pair + half], mixed_grad_ref[tokens, lanes]
            )
        for row, pair, half in group:
            probs = probs_ref[row, 2 * pair + half].astype(SINGLE)
            grad = prob_grad.pop((row, pair, half))
            total = jnp.sum(probs * grad, axis=0, keepdims=True)
            score_grad[row, pair, half] = (probs * (grad - total)).astype(HALF)
        for row, pair, half in group:
            tokens = slice(row * columns, (row + 1) * columns)
            lanes = slice(pair * LANES, (pair + 1) * LANES)
            key_grad[row, pair, half] = dot(score_grad[row, pair, half], query_ref[tokens, lanes])
            all_keys = jnp.concatenate([key_ref[tokens, lanes], key_far_ref[:, lanes]], axis=0)
            turned = all_keys.T[half * head_width : (half + 1) * head_width]
            query_grad[row, pair, half] = dot(turned, score_grad[row, pair, half])
        for row, pair, half in group:
            if half == 0:
                tokens = slice(row * columns, (row + 1) * columns)
                lanes = slice(pair * LANES, (pair + 1) * LANES)
                first, second = (row, pair, 0), (row, pair, 1)
                value_both = jnp.where(first_half, value_grad[first], value_grad[second])
                key_both = jnp.where(first_half, key_grad[first], key_grad[second]) * scaling
                value_grad_ref[tokens, lanes] = value_both[:columns].astype(HALF)
                key_grad_ref[tokens, lanes] = key_both[:columns].astype(HALF)
                value_far_grad_ref[image, :, lanes] += value_both[columns:]
                key_far_grad_ref[image, :, lanes] += key_both[columns:]
                query_both = jnp.concatenate([query_grad[first], query_grad[second]], axis=0) * scaling
                query_grad_ref[tokens, lanes] = query_both.T.astype(HALF)
    normed, _ = normalize(block_ref[...].astype(SINGLE))
    turned = normed.astype(HALF).T
    for i, ref in enumerate((query_grad_ref, key_grad_ref, value_grad_ref)):
        total_ref[:, i * width : (i + 1) * width] += dot(turned, ref[...])
    if not ends:
        return

    @pl.when(pl.program_id(0) == pl.num_programs(0) - 1)
    def _():
        gain_ref, gain_two_grad_ref, w_ref, summary_ref, standard_ref, gain_sum_ref = fixed

        key_low = key_far_grad_ref[...].reshape(-1, width).astype(HALF)
        value_low = value_far_grad_ref[...].reshape(-1, width).astype(HALF)
        gain = jnp.broadcast_to(gain_ref[...], (8, width)).T[:, :1]
        matched = jnp.zeros((width, width), SINGLE)
        flat_ref[:TAIL] = jnp.zeros((TAIL, width), HALF)
        for i in range(3):
            total = total_ref[:, i * width : (i + 1) * width]
            matched = matched + total * w_ref[:, i * width : (i + 1) * width].astype(SINGLE)
            grad = total * gain
            if i > 0:
                grad = grad + dot_outer(summary_ref[...], key_low if i == 1 else value_low)
            flat_ref[TAIL + i * width : TAIL + (i + 1) * width] = grad.astype(HALF)
            if i == 2:
                small_ref[8:] = grad[width - TAIL :]
        copies = start_pieces(plan, flat_ref, pieces, sems, index_ref[0])
        summary_grad = dot_rows(key_low, w_ref[:, width : 2 * width]) + dot_rows(
            value_low, w_ref[:, 2 * width :]
        )
        standard = standard_ref[...]
        standard_grad = summary_grad * gain_sum_ref[...]
        shared_ref[: standard.shape[0]] = standard_grad

        def fold(value):
            return jnp.sum(value, axis=0, keepdims=True)

        small_ref[0:1] = fold(standard_grad)
        small_ref[1:2] = fold(standard_grad * standard)
        small_ref[2:3] = fold(matched.T)
        small_ref[3:4] = fold(summary_grad * standard)
        small_ref[4:5] = fold(summary_grad)
        small_ref[5:6] = gain_two_grad_ref[...]
        small_ref[6:8] = jnp.zeros((2, width), SINGLE)
        for copy in copies:
            copy.wait()


def attention_backward(
    group,
    previous,
    index,
    block_in,
    query,
    key,
    value,
    key_far,
    value_far,
    probs,
    mixed_grad,
    last,
    local_rows,
    columns,
    plan,
    shapes,
):
    tokens, width = query.shape
    images, far, _ = key_far.shape
    first_step, count = group
    rows_per_step = math.gcd(local_rows, 4)
    per_image = local_rows // rows_per_step
    ends = first_step + count == images * per_image
    size = rows_per_step * columns
    part = count * size
    block = pl.BlockSpec((size, width), lambda i, _: (first_step + i, 0))
    far_block = pl.BlockSpec((None, far, width), lambda i, _: ((first_step + i) // per_image, 0, 0))
    probs_block = pl.BlockSpec(
        (rows_per_step, HEADS, columns + far, columns), lambda i, _: (first_step + i, 0, 0, 0)
    )
    inputs = [block_in, query, key, value, key_far, value_far, probs, mixed_grad]
    in_specs = [block] * 4 + [far_block] * 2 + [probs_block, block]
    aliases = {}
    total_shape = (width, 3 * width)
    far_shape = (images, far, width)
    if previous is not None:
        sums = list(previous[3:])
        inputs = inputs + sums
        in_specs = in_specs + [whole_block(array.shape) for array in sums]
        kept, kept_specs, aliases = kept_arrays(previous[:3], 1 + len(inputs))
        inputs, in_specs = inputs + kept, in_specs + kept_specs
    out_specs = [block] * 3
    out_shape = [jax.ShapeDtypeStruct((tokens, width), HALF)] * 3
    scratch = []
    if ends:
        inputs = inputs + list(last)
        in_specs = in_specs + [whole_block(array.shape) for array in last]
        piece_specs, piece_shapes = piece_outputs(shapes)
        summaries = images * far
        shared_shape = (summaries + 8 + TAIL, width)
        out_specs += [whole_block(shared_shape)] + piece_specs
        out_shape += [jax.ShapeDtypeStruct(shared_shape, SINGLE)] + piece_shapes
        scratch = [
            pltpu.VMEM(total_shape, SINGLE),
            pltpu.VMEM(far_shape, SINGLE),
            pltpu.VMEM(far_shape, SINGLE),
            pltpu.VMEM((TAIL + 3 * width, width), HALF),
            pltpu.SemaphoreType.DMA((len(plan),)),
        ]
    else:
        out_specs += [whole_block(total_shape), whole_block(far_shape), whole_block(far_shape)]
        out_shape += [
            jax.ShapeDtypeStruct(total_shape, SINGLE),
            jax.ShapeDtypeStruct(far_shape, SINGLE),
            jax.ShapeDtypeStruct(far_shape, SINGLE),
        ]
    return pl.pallas_call(
        functools.partial(
            attention_backward_kernel,
            1.0 / math.sqrt(width // HEADS),
            rows_per_step,
            per_image,
            first_step,
            plan,
            ends,
        ),
        grid_spec=pltpu.PrefetchScalarGridSpec(
            num_scalar_prefetch=1,
            grid=(count,),
            in_specs=in_specs,
            out_specs=out_specs,
            scratch_shapes=scratch,
        ),
        out_shape=out_shape,
        input_output_aliases=aliases,
        compiler_params=pltpu.CompilerParams(vmem_limit_bytes=VMEM_BYTES),
        cost_estimate=pl.CostEstimate(
            flops=part * width * (6 * width + 16 * (columns + far)),
            bytes_accessed=part * width * 16 + part * HEADS * (columns + far) * 2,
            transcendentals=0,
        ),
        name="attention_backward",
    )(index, *inputs)


def input_grad_kernel(
    rows_per_step,
    block_ref,
    gain_ref,
    query_grad_ref,
    key_grad_ref,
    value_grad_ref,
    w_ref,
    middle_grad_ref,
    mean_grad_ref,
    out_ref,
):
    width = block_ref.shape[1]
    columns = block_ref.shape[0] // rows_per_step

    attn_grad = (
        dot_rows(query_grad_ref[...], w_ref[:, :width])
        + dot_rows(key_grad_ref[...], w_ref[:, width : 2 * width])
        + dot_rows(value_grad_ref[...], w_ref[:, 2 * width :])
    )
    normed, inverse = normalize(block_ref[...].astype(SINGLE))
    total = middle_grad_ref[...] + norm_back(attn_grad * gain_ref[...], normed, inverse)
    for row in range(rows_per_step):
        tokens = slice(row * columns, (row + 1) * columns)
        out_ref[tokens] = total[tokens] + mean_grad_ref[row : row + 1]


def input_grads(
    group,
    previous,
    block_in,
    gain,
    query_grad,
    key_grad,
    value_grad,
    w_qkv,
    middle_grad,
    mean_grad,
    local_rows,
    columns,
):
    tokens, width = block_in.shape
    images = mean_grad.shape[0]
    first_image, count = group
    rows_per_step = math.gcd(local_rows, 2)
    per_image = local_rows // rows_per_step
    first_step = first_image * per_image
    size = rows_per_step * columns
    part = count * tokens // images
    block = pl.BlockSpec((size, width), lambda i: (first_step + i, 0))
    inputs = [block_in, gain, query_grad, key_grad, value_grad, w_qkv, middle_grad]
    inputs = inputs + [mean_grad.reshape(tokens // size, rows_per_step, width)]
    kept, kept_specs, aliases = kept_arrays(None if previous is None else [previous], len(inputs))
    kernel = functools.partial(input_grad_kernel, rows_per_step)

    def body(*refs):
        kernel(*refs[: len(inputs)], *refs[len(inputs) + len(kept) :])

    return pl.pallas_call(
        body,
        grid=(count * per_image,),
        in_specs=[block, whole_block((1, width))]
        + [block] * 3
        + [whole_block((width, 3 * width)), block]
        + [pl.BlockSpec((None, rows_per_step, width), lambda i: (first_step + i, 0, 0))]
        + kept_specs,
        out_specs=block,
        out_shape=jax.ShapeDtypeStruct((tokens, width), SINGLE),
        input_output_aliases=aliases,
        compiler_params=pltpu.CompilerParams(vmem_limit_bytes=VMEM_BYTES),
        cost_estimate=pl.CostEstimate(
            flops=part * width * 6 * width, bytes_accessed=part * width * 16, transcendentals=0
        ),
        name="input_grads",
    )(*inputs, *kept)


def assemble(flat_ref, pieces, index, block, count):
    plane = 8 * block
    width = flat_ref.shape[1]
    for at in range(0, count * plane + 1, block):
        flat_ref[at : at + TAIL] = jnp.zeros((TAIL, width), HALF)
    for ref, mask, first in pieces:
        spot = pl.multiple_of((index ^ mask) * block, TAIL)
        for slot in range(count):
            part = ref.at[slot] if len(ref.shape) == 3 else ref
            last = first + part.shape[0]
            for low, high in ((0, TAIL), (TAIL, block), (block, block + TAIL)):
                low, high = max(low, first), min(high, last)
                if low >= high:
                    continue
                rows = pl.ds(spot + (slot * plane + low), high - low)
                value = part[low - first : high - first]
                if low < TAIL or low >= block:
                    value = flat_ref[rows] + value
                flat_ref[rows] = value


def projection_weights_kernel(masks, block, index_ref, tail_ref, summary_ref, *refs):
    *piece_refs, w_ref, key_far_ref, value_far_ref, flat_ref = refs
    width = flat_ref.shape[1]
    pieces = [(ref, mask, first) for ref, (mask, first) in zip(piece_refs, masks)]
    assemble(flat_ref, pieces, lax.rem(index_ref[0], 8), block, 1)
    flat_ref[3 * width :] += tail_ref[...]
    for i in range(3):
        w_ref[:, i * width : (i + 1) * width] = flat_ref[TAIL + i * width : TAIL + (i + 1) * width]
    key_far_ref[...] = dot(summary_ref[...], w_ref[:, width : 2 * width]).astype(HALF)
    value_far_ref[...] = dot(summary_ref[...], w_ref[:, 2 * width :]).astype(HALF)


def vmem_specs(count):
    return [pl.BlockSpec(memory_space=pltpu.VMEM)] * count


def projection_weights(index, tail, summary_low, pieces, block):
    width = tail.shape[1]
    arrays, masks = [p[0] for p in pieces], [p[1:] for p in pieces]
    far = summary_low.shape[0]
    return pl.pallas_call(
        functools.partial(projection_weights_kernel, masks, block),
        in_specs=[pl.BlockSpec(memory_space=pltpu.SMEM)] + vmem_specs(2 + len(arrays)),
        out_specs=vmem_specs(3),
        out_shape=[
            jax.ShapeDtypeStruct((width, 3 * width), HALF),
            jax.ShapeDtypeStruct((far, width), HALF),
            jax.ShapeDtypeStruct((far, width), HALF),
        ],
        scratch_shapes=[pltpu.VMEM((TAIL + 3 * width, width), HALF)],
        compiler_params=pltpu.CompilerParams(vmem_limit_bytes=VMEM_BYTES),
        name="projection_weights",
    )(index, tail, summary_low, *arrays)


def swap_core(value):
    return swap(value, "row", 1)


def swap_x(value):
    return swap(value, "row", 2)


def swap_y(value):
    return swap(value, "img", 1)


def swap_both(value):
    size = lax.axis_size("img") * lax.axis_size("row")
    return lax.ppermute(value, ("img", "row"), [(i, i ^ 6) for i in range(size)])


def swap_near(value):
    return swap(value, "img", 2)


def swap_far(value):
    return swap(value, "img", 4)


def send_far(value):
    return lax.ppermute(value, "img", [(i, i ^ 4) for i in range(lax.axis_size("img")) if i // 2 != 2])


def send_down(value, distance):
    size = lax.axis_size("img")
    senders = [i for i in range(size) if i & distance and not i & (distance - 1) & ~1]
    return lax.ppermute(value, "img", [(i, i ^ distance) for i in senders])


def corners(over_x, over_y, split):
    rows = over_x.ndim - 2
    first = lax.slice_in_dim(over_x, 0, split, axis=rows)
    second = lax.slice_in_dim(over_y, split, over_y.shape[rows], axis=rows)
    return (swap_y(first), swap_x(second))


def with_cores(value, over_x, over_y, corner_first, corner_second, split):
    near = [(value, 0, 0), (over_x, 2, 0), (over_y, 4, 0), (corner_first, 6, 0), (corner_second, 6, split)]
    return near + [(swap_core(array), mask | 1, first) for array, mask, first in near]


def sum_planes(value):
    far = lax.ppermute(value, "img", [(i, i ^ 6) for i in range(lax.axis_size("img"))])
    return value + swap_near(value) + swap_far(value) + far


def piece_plan(block, slots):
    plan, shapes = [], []
    rows = block + TAIL
    for out, (side, masks) in enumerate(((0, (0,)), (0, (2, 4, 6)), (1, (0, 2, 4, 6)))):
        shapes.append((len(masks), slots, rows))
        for place, mask in enumerate(masks):
            for slot in range(slots):

                def offset(index, mask=mask | side, slot=slot):
                    return (slot * 8 + (lax.rem(index, 8) ^ mask)) * block

                plan.append((out, (place, slot), offset, rows))
    return plan, shapes


def sum_core(kept, sent, other):
    other = swap_core(other).astype(SINGLE)
    return (kept[0].astype(SINGLE) + other[0], (sent.astype(SINGLE) + other[1:]).astype(HALF))


def across_plane(sent):
    return (swap_x(sent[0]), swap_y(sent[1]), swap_both(sent[2]))


def sum_plane(kept, over_x, over_y, over_both):
    return (kept + over_x.astype(SINGLE)) + (over_y.astype(SINGLE) + over_both.astype(SINGLE))


def together(*values):
    return lax.optimization_barrier(values)


def fits_planes(width, block):
    return lax.axis_size("row") == 4 and lax.axis_size("img") == 8 and 8 * block == 3 * width


def own_rows(weights, width):
    length = weights.shape[0]
    block, rest = length // width, length % width
    start = TAIL * width + rest * device_index() - 4 * width
    own = lax.dynamic_update_slice(jnp.zeros(((block + TAIL) * width,), HALF), weights, (start,))
    return own.reshape(block + TAIL, width), start


def per_device(activations, cotangent, weights):
    images, local_rows, columns, width = activations.shape
    tokens = images * local_rows * columns
    size = tokens // images
    rows_all = local_rows * lax.axis_size("row")
    far = images * rows_all
    first_row = lax.axis_index("row") * local_rows
    summary_count = float(images * lax.axis_size("img") * rows_all)
    block = weights.shape[0] // width
    planes = fits_planes(width, block)
    split = block // 2 // TAIL * TAIL
    me = device_index()
    index = me[None]
    z = lax.axis_index("img") // 2
    block_in = activations.reshape(tokens, width)

    row_means = jnp.mean(activations.astype(SINGLE), axis=2)
    if planes:
        own, start = own_rows(weights, width)
        shown = jnp.concatenate(
            [
                jnp.where(me == 0, own[TAIL - 4 : TAIL].astype(SINGLE), 0.0),
                jnp.where(me == 8, own[:TAIL].astype(SINGLE), 0.0),
            ]
        )
    else:
        gathered, matrix_rows = gather_weights(weights, width)
        shown = jnp.zeros((4 + TAIL, width), SINGLE)
    all_means, shown = gather_rows(row_means, shown)
    sums = jnp.stack([jnp.sum(all_means, axis=(0, 1)), jnp.sum(all_means * all_means, axis=(0, 1))])
    sums = jnp.concatenate([sums, shown])
    if planes:
        over_far, sums = together(swap_far(own), sums)
        over_near = swap_near(jnp.stack([own, over_far]))
        over_near, sums = together(over_near, sum_planes(sums + swap_y(sums)))
        held = jnp.stack([own, over_near[0], over_far, over_near[1]])
        first_slot = lax.dynamic_index_in_dim(held, z, 0, keepdims=False)
        first_near = [swap_x(first_slot), swap_y(first_slot), swap_both(first_slot)]
        other_slots = jnp.stack(
            [lax.dynamic_index_in_dim(held, z ^ i, 0, keepdims=False) for i in (1, 2, 3)]
        )
        first_near, other_slots, sums = together(first_near, other_slots, sums)
        first_pieces = [(array, 2 * i, 0) for i, array in enumerate([first_slot] + list(first_near))]
        first_pieces += [(swap_core(array), mask | 1, 0) for array, mask, _ in first_pieces]
        other_x, other_y = swap_x(other_slots), swap_y(other_slots)
    else:
        for axis, distance, _ in image_hops():
            sums = sums + swap(sums, axis, distance)
    summary_mean = sums[0] / summary_count
    summary_var = sums[1] / summary_count - summary_mean * summary_mean
    summary_inv = lax.rsqrt(summary_var + EPS)
    standard = (all_means - summary_mean) * summary_inv
    vectors = sums[2:6] if planes else gathered.astype(SINGLE)
    gain_one, gain_sum, bias_sum, gain_two = (vectors[i : i + 1] for i in range(4))
    summary_low = (standard * gain_sum + bias_sum).astype(HALF).reshape(far, width)

    if planes:
        w_qkv, key_far, value_far = projection_weights(
            index, sums[6:].astype(HALF), summary_low, first_pieces, block
        )
    else:
        w_qkv = jnp.concatenate([matrix_rows[i * width : (i + 1) * width] for i in range(3)], axis=1)
        key_far = dot(summary_low, w_qkv[:, width : 2 * width]).astype(HALF)
        value_far = dot(summary_low, w_qkv[:, 2 * width :]).astype(HALF)
    key_far = key_far.reshape(images, rows_all, width)
    value_far = value_far.reshape(images, rows_all, width)

    forward = None
    for group in image_groups(images):
        forward = attention_forward(
            group,
            forward,
            block_in,
            gain_one,
            w_qkv,
            key_far,
            value_far,
            first_row[None],
            local_rows,
            columns,
        )
        if planes and group[0] == 0:
            other_x, other_y, forward = together(other_x, other_y, forward)
            other_corners = corners(other_x, other_y, split)
    if planes:
        other_corners, forward = together(other_corners, forward)
        given = with_cores(other_slots, other_x, other_y, *other_corners, split)
    query, key, value, mixed, probs = forward

    if planes:
        late_plan, late_shapes = piece_plan(block, 1)
        early_plan, early_shapes = piece_plan(block, 3)
        early_shapes = [shape + (width,) for shape in early_shapes]
        late_shapes = [shape + (width,) for shape in late_shapes]
    else:
        early_shapes = [(TAIL + width + 2 * FF, width)]
        late_shapes = [(TAIL + 3 * width, width)]
        early_plan = [(0, (), lambda i: i * 0, early_shapes[0][0])]
        late_plan = [(0, (), lambda i: i * 0, late_shapes[0][0])]
        given = [(jnp.pad(matrix_rows[3 * width :], ((TAIL, 0), (0, 0))), 0, 0)]

    out, middle_grad, mixed_grad, gain_two_grad, *early = feed_forward(
        index,
        block_in,
        mixed,
        cotangent.reshape(tokens, width),
        gain_two,
        given,
        block if planes else None,
        FF,
        size,
        early_plan,
        early_shapes,
    )
    standard_flat = standard.reshape(far, width)
    last = [gain_one, gain_two_grad, w_qkv, summary_low, standard_flat, gain_sum]
    if planes:
        (early_kept, early_sent), mixed_grad = together(sum_core(*early), mixed_grad)
        early_in = across_plane(early_sent)
    steps = images * local_rows // math.gcd(local_rows, 4)
    backward = attention_backward(
        (0, steps),
        None,
        index,
        block_in,
        query,
        key,
        value,
        key_far,
        value_far,
        probs,
        mixed_grad,
        last,
        local_rows,
        columns,
        late_plan,
        late_shapes,
    )
    query_grad, key_grad, value_grad, shared, *late = backward
    if planes:
        (late_kept, late_sent), shared, early = together(
            sum_core(*late), shared + swap_core(shared), sum_plane(early_kept, *early_in)
        )
        late_in = across_plane(late_sent)
        by_mask = [
            jnp.where(z == i, 0.0, lax.dynamic_index_in_dim(early, (z ^ i) - 1, 0, keepdims=False))
            for i in range(4)
        ]
        early_in = swap_near(jnp.stack([by_mask[1], by_mask[3]]).astype(HALF))
        small = shared[far:]
        over_x = swap_x(shared)
        small = small + over_x[far:] + swap_y(small) + swap_both(small)
        late_in, small, shared, early_in = together(
            late_in, small, shared[:far] + over_x[:far], early_in
        )
        late = sum_plane(late_kept, *late_in)[0]
        late = late + send_down(late.astype(HALF), 2).astype(SINGLE)
        late, small = together(late, sum_planes(small))
    else:
        for axis, distance, _ in row_hops():
            shared = shared + swap(shared, axis, distance)
        small = shared[far:]
        for axis, distance, _ in image_hops():
            small = small + swap(small, axis, distance)
    own_grad = lax.dynamic_slice_in_dim(
        shared[:far].reshape(images, rows_all, width), first_row, local_rows, axis=1
    )
    own_standard = lax.dynamic_slice_in_dim(standard, first_row, local_rows, axis=1)
    mean_grad = summary_inv * (
        own_grad - small[0] / summary_count - own_standard * (small[1] / summary_count)
    )
    input_grad = None
    for group in [(0, images)]:
        input_grad = input_grads(
            group,
            input_grad,
            block_in,
            gain_one,
            query_grad,
            key_grad,
            value_grad,
            w_qkv,
            middle_grad,
            mean_grad / columns,
            local_rows,
            columns,
        )
    if planes:
        late_own = late + send_down(late.astype(HALF), 4).astype(SINGLE)
        early_far = send_far((by_mask[2] + early_in[1].astype(SINGLE)).astype(HALF))
        early_own = by_mask[0] + early_in[0].astype(SINGLE) + early_far.astype(SINGLE)
        head = jnp.where(
            me == 0,
            jnp.concatenate([jnp.zeros((TAIL - 4, width), SINGLE), small[2:6]]),
            jnp.where(me == 8, small[8:], 0.0),
        )
        mine = jnp.where(z == 0, late_own, early_own)
        mine = jnp.concatenate([mine[:TAIL] + head, mine[TAIL:]])
        weight_grad = lax.dynamic_slice(mine.reshape(-1), (start,), weights.shape)
    else:
        grad_rows = jnp.concatenate([late[0][TAIL:], early[0][TAIL:]]).astype(SINGLE)
        weight_grad = scatter_grads(small[2:6], grad_rows, weights.shape[0])
    return (
        out.reshape(activations.shape),
        input_grad.reshape(activations.shape),
        weight_grad,
        summary_mean,
        summary_var,
    )


def solution(mesh):
    placed = (P("img", "row", None, None), P("img", "row", None, None), P(("img", "row")))
    return jax.shard_map(
        per_device,
        mesh=mesh,
        in_specs=placed,
        out_specs=(
            P("img", "row", None, None),
            P("img", "row", None, None),
            P(("img", "row")),
            P(),
            P(),
        ),
        check_vma=False,
    )
```

```python
import functools
import math

import jax
import jax.numpy as jnp
from jax import lax
from jax.experimental import pallas as pl
from jax.experimental.pallas import tpu as pltpu
from jax.sharding import PartitionSpec as P

FF = 2048
HEADS = 8
LANES = 128


EPS = 1e-05
NEGATIVE = -1e30
HALF = jnp.bfloat16
SINGLE = jnp.float32
VMEM_BYTES = 56 * 1024 * 1024

TAIL = 16


def swap(value, axis, distance):
    size = lax.axis_size(axis)
    return lax.ppermute(value, axis, [(i, i ^ distance) for i in range(size)])


def hops():
    rows, images = lax.axis_size("row"), lax.axis_size("img")
    inner = ("row", 1, 1)
    across = ("row", 2, 2)
    along = ("img", 1, rows)
    outer = []
    distance = images // 2
    while distance > 1:
        outer.append(("img", distance, distance * rows))
        distance //= 2
    distance = rows // 2
    while distance > 2:
        outer.append(("row", distance, distance))
        distance //= 2
    return inner, across, along, outer


def piece_order():
    inner, across, along, outer = hops()
    masks = [0]
    for _, _, mask in outer:
        masks = masks + [m ^ mask for m in masks]
    near = (
        masks
        + [m ^ across[2] for m in masks]
        + [m ^ along[2] for m in masks]
        + [m ^ across[2] ^ along[2] for m in masks]
    )
    return near + [m ^ inner[2] for m in near]


def device_index():
    return lax.axis_index("img") * lax.axis_size("row") + lax.axis_index("row")


def gather_pieces(own):
    inner, across, along, outer = hops()
    held = own[None]
    for axis, distance, _ in outer:
        held = jnp.concatenate([held, swap(held, axis, distance)])
    half = held.shape[0] // 2
    held_x = swap(held, across[0], across[1])
    held_y = swap(held, along[0], along[1])
    corner_first = swap(held_x[:half], along[0], along[1])
    corner_second = swap(held_y[half:], across[0], across[1])
    near = [held, held_x, held_y, corner_first, corner_second]
    far = [swap(part, inner[0], inner[1]) for part in near]
    return jnp.concatenate(near + far)


def scatter_pieces(pieces):
    inner, across, along, outer = hops()

    def add(kept, sent, axis, distance):
        return kept + swap(sent.astype(HALF), axis, distance).astype(SINGLE)

    count = pieces.shape[0] // 2
    near = add(pieces[:count], pieces[count:], inner[0], inner[1])
    quarter = count // 4
    half = quarter // 2
    held, held_x, held_y, corner = (near[i * quarter : (i + 1) * quarter] for i in range(4))
    first = add(
        jnp.concatenate([held[:half], held_x[:half]]),
        jnp.concatenate([held_y[:half], corner[:half]]),
        along[0],
        along[1],
    )
    second = add(
        jnp.concatenate([held[half:], held_y[half:]]),
        jnp.concatenate([held_x[half:], corner[half:]]),
        across[0],
        across[1],
    )
    first = add(first[:half], first[half:], across[0], across[1])
    second = add(second[:half], second[half:], along[0], along[1])
    held = jnp.concatenate([first, second])
    for axis, distance, _ in reversed(outer):
        half = held.shape[0] // 2
        held = add(held[:half], held[half:], axis, distance)
    return held[0]


def row_hops():
    inner, across, _, outer = hops()
    return [inner, across] + [hop for hop in outer if hop[0] == "row"]


def image_hops():
    _, _, along, outer = hops()
    return [along] + [hop for hop in outer if hop[0] == "img"]


def gather_rows(own):
    held, masks = own[None], [0]
    for axis, distance, mask in row_hops():
        held = jnp.concatenate([held, swap(held, axis, distance)])
        masks = masks + [m ^ mask for m in masks]
    place = [0] * len(masks)
    for at, mask in enumerate(masks):
        place[mask] = at
    order = jnp.asarray(place, jnp.int32)[jnp.arange(len(masks)) ^ lax.axis_index("row")]
    held = jnp.moveaxis(jnp.take(held, order, axis=0, mode="clip"), 0, 1)
    return held.reshape(own.shape[0], -1, own.shape[-1])


def gather_weights(weights, model_width):
    length = weights.shape[0]
    me = device_index()
    devices = lax.axis_size("img") * lax.axis_size("row")
    block = length // model_width
    rest = length % model_width
    start = TAIL * model_width + rest * me - 4 * model_width
    own = lax.dynamic_update_slice(jnp.zeros(((block + TAIL) * model_width,), HALF), weights, (start,))
    own = own.reshape(block + TAIL, model_width)
    pieces = gather_pieces(own)
    place = [0] * devices
    for at, mask in enumerate(piece_order()):
        place[mask] = at
    order = jnp.asarray(place, jnp.int32)[jnp.arange(devices) ^ me]
    pieces = jnp.take(pieces, order, axis=0, mode="clip")
    tails = jnp.concatenate([pieces[1:, :TAIL], jnp.zeros((1, TAIL, model_width), HALF)])
    body = jnp.concatenate([pieces[:, TAIL:block], pieces[:, block:] + tails], axis=1)
    return pieces[0, TAIL - 4 : TAIL], body.reshape(devices * block, model_width)


def scatter_grads(vectors, rows, length):
    model_width = rows.shape[1]
    me = device_index()
    devices = lax.axis_size("img") * lax.axis_size("row")
    block = length // model_width
    rest = length % model_width
    whole = jnp.concatenate([jnp.zeros((TAIL - 4, model_width), SINGLE), vectors, rows])
    place = jnp.asarray(piece_order(), jnp.int32)
    pieces = jnp.stack([whole[block * s : block * s + block + TAIL] for s in range(devices)])
    pieces = jnp.take(pieces, place ^ me, axis=0, mode="clip")
    mine = scatter_pieces(pieces)
    start = TAIL * model_width + rest * me - 4 * model_width
    return lax.dynamic_slice(mine.reshape(-1), (start,), (length,))


def dot(left, right):
    return jnp.dot(left, right, preferred_element_type=SINGLE)


def dot_rows(left, right):
    return lax.dot_general(left, right, (((1,), (1,)), ((), ())), preferred_element_type=SINGLE)


def dot_outer(left, right):
    return lax.dot_general(left, right, (((0,), (0,)), ((), ())), preferred_element_type=SINGLE)


def normalize(values):
    centred = values - jnp.mean(values, axis=-1, keepdims=True)
    inverse = lax.rsqrt(jnp.mean(centred * centred, axis=-1, keepdims=True) + EPS)
    return (centred * inverse, inverse)


def norm_back(grad_norm, normed, inverse):
    return inverse * (
        grad_norm
        - jnp.mean(grad_norm, axis=-1, keepdims=True)
        - normed * jnp.mean(grad_norm * normed, axis=-1, keepdims=True)
    )


def whole_block(shape):
    return pl.BlockSpec(shape, lambda *_: (0,) * len(shape), pipeline_mode=pl.Buffered(1))


def head_keys(rows_per_step, model_width):
    return [
        (row, pair, half)
        for row in range(rows_per_step)
        for pair in range(model_width // LANES)
        for half in range(2)
    ]


def attention_forward_kernel(
    scaling,
    rows_per_step,
    local_rows,
    first_row_ref,
    block_ref,
    gain_ref,
    w_ref,
    key_far_ref,
    value_far_ref,
    causal_ref,
    query_ref,
    key_ref,
    value_ref,
    mixed_ref,
    probs_ref,
):
    columns = causal_ref.shape[0]
    far = key_far_ref.shape[0]
    width = block_ref.shape[1]
    head_width = width // HEADS
    step = pl.program_id(0)
    normed, _ = normalize(block_ref[...].astype(SINGLE))
    attn_in = (normed * gain_ref[...]).astype(HALF)
    for i, ref in enumerate((query_ref, key_ref, value_ref)):
        ref[...] = dot(attn_in, w_ref[:, i * width : (i + 1) * width]).astype(HALF)
    first_half = lax.broadcasted_iota(jnp.int32, (columns + far, LANES), 1) < head_width
    far_index = lax.broadcasted_iota(jnp.int32, (far, columns), 0)
    keys = head_keys(rows_per_step, width)
    for start in range(0, len(keys), HEADS):
        group = keys[start : start + HEADS]
        scores, low, mixed = {}, {}, {}
        for row, pair, half in group:
            global_row = first_row_ref[0] + lax.rem(step * rows_per_step + row, local_rows)
            far_bias = jnp.where(far_index < global_row, 0.0, NEGATIVE)
            tokens = slice(row * columns, (row + 1) * columns)
            lanes = slice(pair * LANES, (pair + 1) * LANES)
            all_keys = jnp.concatenate([key_ref[tokens, lanes], key_far_ref[:, lanes]], axis=0)
            one_head = jnp.where(
                first_half if half == 0 else ~first_half, all_keys, jnp.zeros_like(all_keys)
            )
            found = dot_rows(one_head, query_ref[tokens, lanes])
            scores[row, pair, half] = jnp.concatenate(
                [found[:columns] + causal_ref[...], found[columns:] + far_bias], axis=0
            )
        for row, pair, half in group:
            found = scores.pop((row, pair, half))
            top = jnp.max(found, axis=0, keepdims=True)
            powers = jnp.exp((found - top) * scaling)
            inverse = 1.0 / jnp.sum(powers, axis=0, keepdims=True)
            low[row, pair, half] = (powers * inverse).astype(HALF)
            probs_ref[row, 2 * pair + half] = low[row, pair, half]
        for row, pair, half in group:
            tokens = slice(row * columns, (row + 1) * columns)
            lanes = slice(pair * LANES, (pair + 1) * LANES)
            all_values = jnp.concatenate([value_ref[tokens, lanes], value_far_ref[:, lanes]], axis=0)
            turned = all_values.T[half * head_width : (half + 1) * head_width]
            mixed[row, pair, half] = dot(turned, low[row, pair, half])
        for row, pair, half in group:
            if half == 0:
                tokens = slice(row * columns, (row + 1) * columns)
                lanes = slice(pair * LANES, (pair + 1) * LANES)
                both = jnp.concatenate([mixed[row, pair, 0], mixed[row, pair, 1]], axis=0)
                mixed_ref[tokens, lanes] = both.T.astype(HALF)


def image_groups(images):
    return [(0, 1), (1, images - 1)] if images > 1 else [(0, images)]


def step_groups(steps):
    if steps < 4:
        return [(0, steps)]
    first, last = steps // 3, max(1, steps // 6)
    return [(0, first), (first, steps - first - last), (steps - last, last)]


def kept_arrays(previous, start):
    if previous is None:
        return ([], [], {})
    specs = [pl.BlockSpec(memory_space=pl.ANY)] * len(previous)
    return (list(previous), specs, {start + i: i for i in range(len(previous))})


def attention_forward(
    group, previous, block_in, gain, w_qkv, key_far, value_far, first_row, local_rows, columns
):
    tokens, width = block_in.shape
    images, far, _ = key_far.shape
    first_image, count = group
    rows_per_step = math.gcd(local_rows, 2)
    steps = local_rows // rows_per_step
    first_step = first_image * steps
    size = rows_per_step * columns
    position = jnp.arange(columns)
    causal = jnp.where(position[:, None] <= position[None, :], 0.0, NEGATIVE).astype(SINGLE)
    block = pl.BlockSpec((size, width), lambda i, _: (first_step + i, 0))
    far_block = pl.BlockSpec((None, far, width), lambda i, _: (first_image + i // steps, 0, 0))
    probs_block = pl.BlockSpec(
        (rows_per_step, HEADS, columns + far, columns), lambda i, _: (first_step + i, 0, 0, 0)
    )
    inputs = [block_in, gain, w_qkv, key_far, value_far, causal]
    kept, kept_specs, aliases = kept_arrays(previous, 1 + len(inputs))
    low = jax.ShapeDtypeStruct((tokens, width), HALF)
    part = count * tokens // images
    kernel = functools.partial(
        attention_forward_kernel, 1.0 / math.sqrt(width // HEADS), rows_per_step, local_rows
    )

    def body(*refs):
        kernel(*refs[: 1 + len(inputs)], *refs[1 + len(inputs) + len(kept) :])

    return pl.pallas_call(
        body,
        grid_spec=pltpu.PrefetchScalarGridSpec(
            num_scalar_prefetch=1,
            grid=(count * steps,),
            in_specs=[
                block,
                whole_block((1, width)),
                whole_block((width, 3 * width)),
                far_block,
                far_block,
                whole_block((columns, columns)),
            ]
            + kept_specs,
            out_specs=[block] * 4 + [probs_block],
        ),
        out_shape=[low] * 4
        + [jax.ShapeDtypeStruct((images * local_rows, HEADS, columns + far, columns), HALF)],
        input_output_aliases=aliases,
        compiler_params=pltpu.CompilerParams(vmem_limit_bytes=VMEM_BYTES),
        cost_estimate=pl.CostEstimate(
            flops=part * width * (6 * width + 8 * (columns + far)),
            bytes_accessed=part * width * 12 + part * HEADS * (columns + far) * 2,
            transcendentals=part * HEADS * (columns + far),
        ),
        name="attention_forward",
    )(first_row, *inputs, *kept)


GELU_OUTER = math.sqrt(2.0 / math.pi)
GELU_CUBE = 0.044715


def gelu_and_slope(value):
    square = value * value
    gate = 0.5 * jnp.tanh(value * (GELU_OUTER * GELU_CUBE * square + GELU_OUTER)) + 0.5
    activated = value * gate
    slope = gate + activated * (1.0 - gate) * (6.0 * GELU_OUTER * GELU_CUBE * square + 2.0 * GELU_OUTER)
    return (activated, slope)


def start_pieces(plan, flat_ref, outs, sems, index):
    copies = []
    for i, (out, place, offset, rows) in enumerate(plan):
        source = flat_ref.at[pl.ds(pl.multiple_of(offset(index), TAIL), rows)]
        target = outs[out].at[place] if place else outs[out]
        copies.append(pltpu.make_async_copy(source, target, sems.at[i]))
    for copy in copies:
        copy.start()
    return copies


def feed_forward_kernel(
    chunk,
    plan,
    masks,
    block,
    index_ref,
    block_ref,
    mixed_ref,
    cotangent_ref,
    gain_ref,
    *rest,
):
    given, rest = rest[: len(masks)], rest[len(masks) :]
    out_ref, middle_grad_ref, mixed_grad_ref, grad_gain_ref, *rest = rest
    *pieces, grad_out_ref, grad_inner_ref, grad_outer_ref, w_inner_ref, flat_ref, sems = rest
    width, hidden = w_inner_ref.shape
    groups = hidden // width
    per = 256 // groups
    inner_start = TAIL + width
    outer_start = inner_start + hidden
    w_out_ref = flat_ref.at[TAIL:inner_start]
    w_outer_ref = flat_ref.at[outer_start:]

    @pl.when(pl.program_id(0) == 0)
    def _():
        for ref in (grad_out_ref, grad_inner_ref, grad_outer_ref, grad_gain_ref):
            ref[...] = jnp.zeros_like(ref)
        if block is None:
            flat_ref[...] = given[0][...]
        else:
            placed = [(ref, mask, first) for ref, (mask, first) in zip(given, masks)]
            assemble(flat_ref, placed, lax.rem(index_ref[0], 8), block, 3)
        mix = weave(groups, per)
        for c in range(width // per):
            start = inner_start + c * groups * per
            parted = dot_outer(mix, flat_ref[start : start + groups * per]).astype(HALF)
            for g in range(groups):
                w_inner_ref[c * per : (c + 1) * per, g * width : (g + 1) * width] = parted[
                    g * per : (g + 1) * per
                ]

    mixed = mixed_ref[...]
    cotangent = cotangent_ref[...]
    middle = block_ref[...].astype(SINGLE) + dot(mixed, w_out_ref[...])
    normed, inverse = normalize(middle)
    ff_in = (normed * gain_ref[...]).astype(HALF)
    out = middle
    ff_grad = jnp.zeros_like(middle)
    cotangent_turned = cotangent.T
    ff_turned = ff_in.T
    count = hidden // chunk
    spans = [slice(j * chunk, (j + 1) * chunk) for j in range(count)]

    def products(j):
        return (dot(ff_in, w_inner_ref[:, spans[j]]), dot_rows(cotangent, w_outer_ref[spans[j], :]))

    ready = products(0)
    for j in range(count):
        inner, act_grad = ready
        if j + 1 < count:
            ready = products(j + 1)
        activated, slope = gelu_and_slope(inner)
        activated = activated.astype(HALF)
        inner_grad = (slope * act_grad).astype(HALF)
        out = out + dot(activated, w_outer_ref[spans[j], :])
        ff_grad = ff_grad + dot_rows(inner_grad, w_inner_ref[:, spans[j]])
        grad_inner_ref[:, spans[j]] += dot(ff_turned, inner_grad)
        grad_outer_ref[:, spans[j]] += dot(cotangent_turned, activated)
    out_ref[...] = out.astype(HALF)
    grad_gain_ref[...] += jnp.sum(ff_grad * normed, axis=0, keepdims=True)
    middle_grad = cotangent.astype(SINGLE) + norm_back(ff_grad * gain_ref[...], normed, inverse)
    middle_grad_ref[...] = middle_grad
    branch_grad = middle_grad.astype(HALF)
    mixed_grad_ref[...] = dot_rows(branch_grad, w_out_ref[...]).astype(HALF)
    grad_out_ref[...] += dot_outer(mixed, branch_grad)

    @pl.when(pl.program_id(0) == pl.num_programs(0) - 1)
    def _():
        flat_ref[:TAIL] = jnp.zeros((TAIL, width), HALF)
        flat_ref[TAIL : TAIL + width] = grad_out_ref[...].astype(HALF)
        mix = weave(groups, per)
        for c in range(width // per):
            parts = [
                grad_inner_ref[c * per : (c + 1) * per, g * width : (g + 1) * width].astype(HALF)
                for g in range(groups)
            ]
            start = TAIL + width + c * groups * per
            woven = dot(mix, jnp.concatenate(parts, axis=0))
            flat_ref[start : start + groups * per] = woven.astype(HALF)
        start = TAIL + width + hidden
        for j in range(hidden // width):
            turned = grad_outer_ref[:, j * width : (j + 1) * width].astype(HALF).T
            flat_ref[start + j * width : start + (j + 1) * width] = turned
        for copy in start_pieces(plan, flat_ref, pieces, sems, index_ref[0]):
            copy.wait()


def weave(groups, per):
    size = groups * per
    row = lax.broadcasted_iota(jnp.int32, (size, size), 0)
    column = lax.broadcasted_iota(jnp.int32, (size, size), 1)
    wanted = lax.rem(row, groups) * per + lax.div(row, groups)
    return (wanted == column).astype(SINGLE).astype(HALF)


def piece_outputs(shapes):
    return (
        [pl.BlockSpec(memory_space=pl.ANY)] * len(shapes),
        [jax.ShapeDtypeStruct(shape, HALF) for shape in shapes],
    )


def feed_forward(index, block_in, mixed, cotangent, gain, given, block, hidden, size, plan, shapes):
    tokens, width = block_in.shape
    tile = pl.BlockSpec((size, width), lambda i, _: (i, 0))
    piece_specs, piece_shapes = piece_outputs(shapes)
    masks = [entry[1:] for entry in given]
    return pl.pallas_call(
        functools.partial(feed_forward_kernel, 512, plan, masks, block),
        grid_spec=pltpu.PrefetchScalarGridSpec(
            num_scalar_prefetch=1,
            grid=(tokens // size,),
            in_specs=[tile, tile, tile, whole_block((1, width))] + vmem_specs(len(given)),
            out_specs=[tile, tile, tile, whole_block((1, width))] + piece_specs,
            scratch_shapes=[
                pltpu.VMEM((width, width), SINGLE),
                pltpu.VMEM((width, hidden), SINGLE),
                pltpu.VMEM((width, hidden), SINGLE),
                pltpu.VMEM((width, hidden), HALF),
                pltpu.VMEM((TAIL + width + 2 * hidden, width), HALF),
                pltpu.SemaphoreType.DMA((len(plan),)),
            ],
        ),
        out_shape=[
            jax.ShapeDtypeStruct((tokens, width), HALF),
            jax.ShapeDtypeStruct((tokens, width), SINGLE),
            jax.ShapeDtypeStruct((tokens, width), HALF),
            jax.ShapeDtypeStruct((1, width), SINGLE),
        ]
        + piece_shapes,
        compiler_params=pltpu.CompilerParams(vmem_limit_bytes=VMEM_BYTES),
        cost_estimate=pl.CostEstimate(
            flops=tokens * width * (6 * width + 12 * hidden),
            bytes_accessed=tokens * width * 14 + width * hidden * 8,
            transcendentals=tokens * hidden,
        ),
        name="feed_forward",
    )(index, block_in, mixed, cotangent, gain, *[entry[0] for entry in given])


def attention_backward_kernel(
    scaling,
    rows_per_step,
    per_image,
    first_step,
    plan,
    ends,
    index_ref,
    block_ref,
    query_ref,
    key_ref,
    value_ref,
    key_far_ref,
    value_far_ref,
    probs_ref,
    mixed_grad_ref,
    *rest,
):
    rest = list(rest)
    earlier = None
    if first_step > 0:
        earlier, rest = rest[:3], rest[6:]
    if ends:
        fixed, rest = rest[:6], rest[6:]
    query_grad_ref, key_grad_ref, value_grad_ref, *rest = rest
    if ends:
        shared_ref, *rest = rest
        small_ref = shared_ref.at[shared_ref.shape[0] - 8 - TAIL :]
        *pieces, total_ref, key_far_grad_ref, value_far_grad_ref, flat_ref, sems = rest
    else:
        total_ref, key_far_grad_ref, value_far_grad_ref = rest
    width = query_ref.shape[1]
    head_width = width // HEADS
    far = key_far_ref.shape[0]
    columns = query_ref.shape[0] // rows_per_step
    image = lax.div(first_step + pl.program_id(0), per_image)

    @pl.when(pl.program_id(0) == 0)
    def _():
        for i, ref in enumerate((total_ref, key_far_grad_ref, value_far_grad_ref)):
            ref[...] = jnp.zeros_like(ref) if earlier is None else earlier[i][...]

    first_half = lax.broadcasted_iota(jnp.int32, (columns + far, LANES), 1) < head_width
    keys = head_keys(rows_per_step, width)
    for start in range(0, len(keys), HEADS):
        group = keys[start : start + HEADS]
        prob_grad, score_grad, value_grad, key_grad, query_grad = {}, {}, {}, {}, {}
        for row, pair, half in group:
            tokens = slice(row * columns, (row + 1) * columns)
            lanes = slice(pair * LANES, (pair + 1) * LANES)
            all_values = jnp.concatenate([value_ref[tokens, lanes], value_far_ref[:, lanes]], axis=0)
            one_head = jnp.where(
                first_half if half == 0 else ~first_half, all_values, jnp.zeros_like(all_values)
            )
            prob_grad[row, pair, half] = dot_rows(one_head, mixed_grad_ref[tokens, lanes])
        for row, pair, half in group:
            tokens = slice(row * columns, (row + 1) * columns)
            lanes = slice(pair * LANES, (pair + 1) * LANES)
            value_grad[row, pair, half] = dot(
                probs_ref[row, 2 * pair + half], mixed_grad_ref[tokens, lanes]
            )
        for row, pair, half in group:
            probs = probs_ref[row, 2 * pair + half].astype(SINGLE)
            grad = prob_grad.pop((row, pair, half))
            total = jnp.sum(probs * grad, axis=0, keepdims=True)
            score_grad[row, pair, half] = (probs * (grad - total)).astype(HALF)
        for row, pair, half in group:
            tokens = slice(row * columns, (row + 1) * columns)
            lanes = slice(pair * LANES, (pair + 1) * LANES)
            key_grad[row, pair, half] = dot(score_grad[row, pair, half], query_ref[tokens, lanes])
            all_keys = jnp.concatenate([key_ref[tokens, lanes], key_far_ref[:, lanes]], axis=0)
            turned = all_keys.T[half * head_width : (half + 1) * head_width]
            query_grad[row, pair, half] = dot(turned, score_grad[row, pair, half])
        for row, pair, half in group:
            if half == 0:
                tokens = slice(row * columns, (row + 1) * columns)
                lanes = slice(pair * LANES, (pair + 1) * LANES)
                first, second = (row, pair, 0), (row, pair, 1)
                value_both = jnp.where(first_half, value_grad[first], value_grad[second])
                key_both = jnp.where(first_half, key_grad[first], key_grad[second]) * scaling
                value_grad_ref[tokens, lanes] = value_both[:columns].astype(HALF)
                key_grad_ref[tokens, lanes] = key_both[:columns].astype(HALF)
                value_far_grad_ref[image, :, lanes] += value_both[columns:]
                key_far_grad_ref[image, :, lanes] += key_both[columns:]
                query_both = jnp.concatenate([query_grad[first], query_grad[second]], axis=0) * scaling
                query_grad_ref[tokens, lanes] = query_both.T.astype(HALF)
    normed, _ = normalize(block_ref[...].astype(SINGLE))
    turned = normed.astype(HALF).T
    for i, ref in enumerate((query_grad_ref, key_grad_ref, value_grad_ref)):
        total_ref[:, i * width : (i + 1) * width] += dot(turned, ref[...])
    if not ends:
        return

    @pl.when(pl.program_id(0) == pl.num_programs(0) - 1)
    def _():
        gain_ref, gain_two_grad_ref, w_ref, summary_ref, standard_ref, gain_sum_ref = fixed

        key_low = key_far_grad_ref[...].reshape(-1, width).astype(HALF)
        value_low = value_far_grad_ref[...].reshape(-1, width).astype(HALF)
        gain = jnp.broadcast_to(gain_ref[...], (8, width)).T[:, :1]
        matched = jnp.zeros((width, width), SINGLE)
        flat_ref[:TAIL] = jnp.zeros((TAIL, width), HALF)
        for i in range(3):
            total = total_ref[:, i * width : (i + 1) * width]
            matched = matched + total * w_ref[:, i * width : (i + 1) * width].astype(SINGLE)
            grad = total * gain
            if i > 0:
                grad = grad + dot_outer(summary_ref[...], key_low if i == 1 else value_low)
            flat_ref[TAIL + i * width : TAIL + (i + 1) * width] = grad.astype(HALF)
            if i == 2:
                small_ref[8:] = grad[width - TAIL :]
        copies = start_pieces(plan, flat_ref, pieces, sems, index_ref[0])
        summary_grad = dot_rows(key_low, w_ref[:, width : 2 * width]) + dot_rows(
            value_low, w_ref[:, 2 * width :]
        )
        standard = standard_ref[...]
        standard_grad = summary_grad * gain_sum_ref[...]
        shared_ref[: standard.shape[0]] = standard_grad

        def fold(value):
            return jnp.sum(value, axis=0, keepdims=True)

        small_ref[0:1] = fold(standard_grad)
        small_ref[1:2] = fold(standard_grad * standard)
        small_ref[2:3] = fold(matched.T)
        small_ref[3:4] = fold(summary_grad * standard)
        small_ref[4:5] = fold(summary_grad)
        small_ref[5:6] = gain_two_grad_ref[...]
        small_ref[6:8] = jnp.zeros((2, width), SINGLE)
        for copy in copies:
            copy.wait()


def attention_backward(
    group,
    previous,
    index,
    block_in,
    query,
    key,
    value,
    key_far,
    value_far,
    probs,
    mixed_grad,
    last,
    local_rows,
    columns,
    plan,
    shapes,
):
    tokens, width = query.shape
    images, far, _ = key_far.shape
    first_step, count = group
    rows_per_step = math.gcd(local_rows, 4)
    per_image = local_rows // rows_per_step
    ends = first_step + count == images * per_image
    size = rows_per_step * columns
    part = count * size
    block = pl.BlockSpec((size, width), lambda i, _: (first_step + i, 0))
    far_block = pl.BlockSpec((None, far, width), lambda i, _: ((first_step + i) // per_image, 0, 0))
    probs_block = pl.BlockSpec(
        (rows_per_step, HEADS, columns + far, columns), lambda i, _: (first_step + i, 0, 0, 0)
    )
    inputs = [block_in, query, key, value, key_far, value_far, probs, mixed_grad]
    in_specs = [block] * 4 + [far_block] * 2 + [probs_block, block]
    aliases = {}
    total_shape = (width, 3 * width)
    far_shape = (images, far, width)
    if previous is not None:
        sums = list(previous[3:])
        inputs = inputs + sums
        in_specs = in_specs + [whole_block(array.shape) for array in sums]
        kept, kept_specs, aliases = kept_arrays(previous[:3], 1 + len(inputs))
        inputs, in_specs = inputs + kept, in_specs + kept_specs
    out_specs = [block] * 3
    out_shape = [jax.ShapeDtypeStruct((tokens, width), HALF)] * 3
    scratch = []
    if ends:
        inputs = inputs + list(last)
        in_specs = in_specs + [whole_block(array.shape) for array in last]
        piece_specs, piece_shapes = piece_outputs(shapes)
        summaries = images * far
        shared_shape = (summaries + 8 + TAIL, width)
        out_specs += [whole_block(shared_shape)] + piece_specs
        out_shape += [jax.ShapeDtypeStruct(shared_shape, SINGLE)] + piece_shapes
        scratch = [
            pltpu.VMEM(total_shape, SINGLE),
            pltpu.VMEM(far_shape, SINGLE),
            pltpu.VMEM(far_shape, SINGLE),
            pltpu.VMEM((TAIL + 3 * width, width), HALF),
            pltpu.SemaphoreType.DMA((len(plan),)),
        ]
    else:
        out_specs += [whole_block(total_shape), whole_block(far_shape), whole_block(far_shape)]
        out_shape += [
            jax.ShapeDtypeStruct(total_shape, SINGLE),
            jax.ShapeDtypeStruct(far_shape, SINGLE),
            jax.ShapeDtypeStruct(far_shape, SINGLE),
        ]
    return pl.pallas_call(
        functools.partial(
            attention_backward_kernel,
            1.0 / math.sqrt(width // HEADS),
            rows_per_step,
            per_image,
            first_step,
            plan,
            ends,
        ),
        grid_spec=pltpu.PrefetchScalarGridSpec(
            num_scalar_prefetch=1,
            grid=(count,),
            in_specs=in_specs,
            out_specs=out_specs,
            scratch_shapes=scratch,
        ),
        out_shape=out_shape,
        input_output_aliases=aliases,
        compiler_params=pltpu.CompilerParams(vmem_limit_bytes=VMEM_BYTES),
        cost_estimate=pl.CostEstimate(
            flops=part * width * (6 * width + 16 * (columns + far)),
            bytes_accessed=part * width * 16 + part * HEADS * (columns + far) * 2,
            transcendentals=0,
        ),
        name="attention_backward",
    )(index, *inputs)


def input_grad_kernel(
    block_ref,
    gain_ref,
    query_grad_ref,
    key_grad_ref,
    value_grad_ref,
    w_ref,
    middle_grad_ref,
    out_ref,
):
    width = block_ref.shape[1]
    attn_grad = (
        dot_rows(query_grad_ref[...], w_ref[:, :width])
        + dot_rows(key_grad_ref[...], w_ref[:, width : 2 * width])
        + dot_rows(value_grad_ref[...], w_ref[:, 2 * width :])
    )
    normed, inverse = normalize(block_ref[...].astype(SINGLE))
    out_ref[...] = middle_grad_ref[...] + norm_back(attn_grad * gain_ref[...], normed, inverse)


def input_grads(
    block_in, gain, query_grad, key_grad, value_grad, w_qkv, middle_grad, local_rows, columns
):
    tokens, width = block_in.shape
    size = math.gcd(local_rows, 2) * columns
    block = pl.BlockSpec((size, width), lambda i: (i, 0))
    return pl.pallas_call(
        input_grad_kernel,
        grid=(tokens // size,),
        in_specs=[block, whole_block((1, width))]
        + [block] * 3
        + [whole_block((width, 3 * width)), block],
        out_specs=block,
        out_shape=jax.ShapeDtypeStruct((tokens, width), SINGLE),
        compiler_params=pltpu.CompilerParams(vmem_limit_bytes=VMEM_BYTES),
        cost_estimate=pl.CostEstimate(
            flops=tokens * width * 6 * width, bytes_accessed=tokens * width * 16, transcendentals=0
        ),
        name="input_grads",
    )(block_in, gain, query_grad, key_grad, value_grad, w_qkv, middle_grad)


def assemble(flat_ref, pieces, index, block, count):
    plane = 8 * block
    width = flat_ref.shape[1]
    for at in range(0, count * plane + 1, block):
        flat_ref[at : at + TAIL] = jnp.zeros((TAIL, width), HALF)
    for ref, mask, first in pieces:
        spot = pl.multiple_of((index ^ mask) * block, TAIL)
        for slot in range(count):
            part = ref.at[slot] if len(ref.shape) == 3 else ref
            last = first + part.shape[0]
            for low, high in ((0, TAIL), (TAIL, block), (block, block + TAIL)):
                low, high = max(low, first), min(high, last)
                if low >= high:
                    continue
                rows = pl.ds(spot + (slot * plane + low), high - low)
                value = part[low - first : high - first]
                if low < TAIL or low >= block:
                    value = flat_ref[rows] + value
                flat_ref[rows] = value


def parts_of(value):
    high = lax.reduce_precision(value, 8, 7)
    middle = lax.reduce_precision(value - high, 8, 7)
    low = value - high - middle
    return [part.astype(HALF) for part in (high, middle, low)]


def whole_of(parts):
    rows = parts.shape[0] // 3
    parts = parts.astype(SINGLE)
    return (parts[:rows] + parts[rows : 2 * rows]) + parts[2 * rows :]


def projection_weights_kernel(
    masks,
    block,
    images,
    local_rows,
    summary_count,
    index_ref,
    *refs,
):
    piece_refs, refs = refs[: len(masks)], refs[len(masks) :]
    w_ref, key_far_ref, value_far_ref, standard_ref, summary_ref, *refs = refs
    *stat_refs, flat_ref, shown_ref, means_ref = refs
    width = flat_ref.shape[1]
    rows = block + TAIL
    here = lax.rem(index_ref[0], 8)
    assemble(
        flat_ref, [(ref.at[:rows], mask, 0) for ref, mask in zip(piece_refs, masks)], here, block, 1
    )
    for ref, mask in zip(piece_refs, masks):
        shown_ref[here ^ mask] = ref[rows:]
    flat_ref[3 * width :] += shown_ref[0, :TAIL]
    for i in range(3):
        w_ref[:, i * width : (i + 1) * width] = flat_ref[TAIL + i * width : TAIL + (i + 1) * width]
    own_rows = images * local_rows
    total = jnp.zeros((2, width), SINGLE)
    for j in range(8):
        total = total + whole_of(shown_ref[j, TAIL:])[own_rows : own_rows + 2]
    for j in range(4):
        means = whole_of(shown_ref[lax.div(here, 4) * 4 + j, TAIL:])
        for image in range(images):
            start = (image * 4 + j) * local_rows
            means_ref[start : start + local_rows] = means[image * local_rows : (image + 1) * local_rows]
    vectors = flat_ref[:TAIL].astype(SINGLE)[TAIL - 4 :]
    mean = total[:1] / summary_count
    variance = total[1:] / summary_count - mean * mean
    inverse = lax.rsqrt(variance + EPS)
    standard = (means_ref[...] - mean) * inverse
    summary = (standard * vectors[1:2] + vectors[2:3]).astype(HALF)
    standard_ref[...] = standard
    summary_ref[...] = summary
    vector_rows = [vectors[i : i + 1] for i in range(4)]
    for ref, value in zip(stat_refs, [mean, variance, inverse] + vector_rows):
        ref[...] = value
    key_far_ref[...] = dot(summary, w_ref[:, width : 2 * width]).astype(HALF)
    value_far_ref[...] = dot(summary, w_ref[:, 2 * width :]).astype(HALF)


def vmem_specs(count):
    return [pl.BlockSpec(memory_space=pltpu.VMEM)] * count


def projection_weights(index, pieces, block, images, local_rows, summary_count):
    arrays, masks = [p[0] for p in pieces], [p[1] for p in pieces]
    width = arrays[0].shape[1]
    far = 4 * images * local_rows
    return pl.pallas_call(
        functools.partial(
            projection_weights_kernel, masks, block, images, local_rows, summary_count
        ),
        in_specs=[pl.BlockSpec(memory_space=pltpu.SMEM)] + vmem_specs(len(arrays)),
        out_specs=vmem_specs(12),
        out_shape=[
            jax.ShapeDtypeStruct((width, 3 * width), HALF),
            jax.ShapeDtypeStruct((far, width), HALF),
            jax.ShapeDtypeStruct((far, width), HALF),
            jax.ShapeDtypeStruct((far, width), SINGLE),
            jax.ShapeDtypeStruct((far, width), HALF),
        ]
        + [jax.ShapeDtypeStruct((1, width), SINGLE)] * 7,
        scratch_shapes=[
            pltpu.VMEM((TAIL + 3 * width, width), HALF),
            pltpu.VMEM((8, 4 * TAIL, width), HALF),
            pltpu.VMEM((far, width), SINGLE),
        ],
        compiler_params=pltpu.CompilerParams(vmem_limit_bytes=VMEM_BYTES),
        name="projection_weights",
    )(index, *arrays)


def with_sums(value, small):
    high = lax.reduce_precision(small[:8], 8, 7)
    return jnp.concatenate(
        [value, high.astype(HALF), (small[:8] - high).astype(HALF), small[8:].astype(HALF)]
    )


def sums_of(rows):
    rows = rows.astype(SINGLE)
    return jnp.concatenate([rows[:8] + rows[8:16], rows[16:]])


def swap_core(value):
    return swap(value, "row", 1)


def swap_x(value):
    return swap(value, "row", 2)


def swap_y(value):
    return swap(value, "img", 1)


def swap_both(value):
    size = lax.axis_size("img") * lax.axis_size("row")
    return lax.ppermute(value, ("img", "row"), [(i, i ^ 6) for i in range(size)])


def swap_near(value):
    return swap(value, "img", 2)


def swap_far(value):
    return swap(value, "img", 4)


def send_far(value):
    return lax.ppermute(value, "img", [(i, i ^ 4) for i in range(lax.axis_size("img")) if i // 2 != 2])


def piece_plan(block, slots):
    plan, shapes = [], []
    rows = block + TAIL
    for out, (side, masks) in enumerate(((0, (0,)), (0, (2,)), (0, (4,)), (0, (6,)), (1, (0, 2, 4, 6)))):
        shapes.append((len(masks), slots, rows))
        for place, mask in enumerate(masks):
            for slot in range(slots):

                def offset(index, mask=mask | side, slot=slot):
                    return (slot * 8 + (lax.rem(index, 8) ^ mask)) * block

                plan.append((out, (place, slot), offset, rows))
    return plan, shapes


def sum_core(kept, over_x, over_y, over_both, other):
    other = swap_core(other)
    own = kept[0].astype(SINGLE) + other[0].astype(SINGLE)
    sent = [
        (piece[0].astype(SINGLE) + other[i + 1].astype(SINGLE)).astype(HALF)
        for i, piece in enumerate((over_x, over_y, over_both))
    ]
    return (own, sent)


def send_down(value):
    return lax.ppermute(value, "img", [(i, i ^ 4) for i in range(lax.axis_size("img")) if i // 2 == 2])


def across_plane(sent):
    return (swap_x(sent[0]), swap_y(sent[1]), swap_both(sent[2]))


def sum_plane(kept, over_x, over_y, over_both):
    return (kept + over_x.astype(SINGLE)) + (over_y.astype(SINGLE) + over_both.astype(SINGLE))


def together(*values):
    return lax.optimization_barrier(values)


def fits_planes(width, block):
    return lax.axis_size("row") == 4 and lax.axis_size("img") == 8 and 8 * block == 3 * width


def own_rows(weights, width):
    length = weights.shape[0]
    block, rest = length // width, length % width
    start = TAIL * width + rest * device_index() - 4 * width
    own = lax.dynamic_update_slice(jnp.zeros(((block + TAIL) * width,), HALF), weights, (start,))
    return own.reshape(block + TAIL, width), start


def per_device(activations, cotangent, weights):
    images, local_rows, columns, width = activations.shape
    tokens = images * local_rows * columns
    size = tokens // images
    rows_all = local_rows * lax.axis_size("row")
    far = images * rows_all
    first_row = lax.axis_index("row") * local_rows
    summary_count = float(images * lax.axis_size("img") * rows_all)
    block = weights.shape[0] // width
    planes = fits_planes(width, block)
    split = block // 2 // TAIL * TAIL
    me = device_index()
    index = me[None]
    z = lax.axis_index("img") // 2
    block_in = activations.reshape(tokens, width)

    row_means = jnp.mean(activations.astype(SINGLE), axis=2)
    sums = jnp.stack([jnp.sum(row_means, axis=(0, 1)), jnp.sum(row_means * row_means, axis=(0, 1))])
    if planes:
        own, start = own_rows(weights, width)
        piece_rows = block + TAIL
        own = jnp.concatenate([own] + parts_of(sums) + [jnp.zeros((TAIL - 6, width), HALF)])
        over_far = swap_far(own)
        over_near = swap_near(jnp.stack([own, over_far]))
        held = [own, over_near[0], over_far, over_near[1]]
        sums = [whole_of(array[piece_rows : piece_rows + 6]) for array in held]
        sums = (sums[0] + sums[1]) + (sums[2] + sums[3])
        held = jnp.stack([array[:piece_rows] for array in held])
        slots = [lax.dynamic_index_in_dim(held, z ^ i, 0, keepdims=False) for i in range(4)]
        means = row_means.reshape(-1, width)
        spare = jnp.zeros((TAIL - 2 - means.shape[0], width), SINGLE)
        known = parts_of(jnp.concatenate([means, sums, spare]))
        first_slot = jnp.concatenate([slots[0], slots[1][:TAIL]] + known)
        other_slots = jnp.stack(slots[1:])
        first_near = [swap_x(first_slot), swap_y(first_slot), swap_both(first_slot)]
        first_near, other_slots = together(first_near, other_slots)
        first_pieces = [(array, 2 * i) for i, array in enumerate([first_slot] + list(first_near))]
        first_pieces += [(swap_core(array), mask | 1) for array, mask in first_pieces]
        other_near = [swap_x(other_slots), swap_y(other_slots), swap_both(other_slots)]
        w_qkv, key_far, value_far, standard, summary_low, *stats = projection_weights(
            index, first_pieces, block, images, local_rows, summary_count
        )
        summary_mean, summary_var, summary_inv = (row.reshape(width) for row in stats[:3])
        gain_one, gain_sum, bias_sum, gain_two = stats[3:]
        standard = standard.reshape(images, rows_all, width)
    else:
        vectors, matrix_rows = gather_weights(weights, width)
        gain_one, gain_sum, bias_sum, gain_two = (
            vectors[i : i + 1].astype(SINGLE) for i in range(4)
        )
        all_means = gather_rows(row_means)
        for axis, distance, _ in row_hops() + image_hops():
            sums = sums + swap(sums, axis, distance)
        summary_mean = sums[0] / summary_count
        summary_var = sums[1] / summary_count - summary_mean * summary_mean
        summary_inv = lax.rsqrt(summary_var + EPS)
        standard = (all_means - summary_mean) * summary_inv
        summary_low = (standard * gain_sum + bias_sum).astype(HALF).reshape(far, width)
        w_qkv = jnp.concatenate([matrix_rows[i * width : (i + 1) * width] for i in range(3)], axis=1)
        key_far = dot(summary_low, w_qkv[:, width : 2 * width]).astype(HALF)
        value_far = dot(summary_low, w_qkv[:, 2 * width :]).astype(HALF)
    key_far = key_far.reshape(images, rows_all, width)
    value_far = value_far.reshape(images, rows_all, width)

    forward = attention_forward(
        (0, images),
        None,
        block_in,
        gain_one,
        w_qkv,
        key_far,
        value_far,
        first_row[None],
        local_rows,
        columns,
    )
    if planes:
        other_near, forward = together(other_near, forward)
        given = [(array, 2 * i, 0) for i, array in enumerate([other_slots] + list(other_near))]
        given += [(swap_core(array), mask | 1, 0) for array, mask, _ in given]
    query, key, value, mixed, probs = forward

    if planes:
        late_plan, late_shapes = piece_plan(block, 1)
        early_plan, early_shapes = piece_plan(block, 3)
        early_shapes = [shape + (width,) for shape in early_shapes]
        late_shapes = [shape + (width,) for shape in late_shapes]
    else:
        early_shapes = [(TAIL + width + 2 * FF, width)]
        late_shapes = [(TAIL + 3 * width, width)]
        early_plan = [(0, (), lambda i: i * 0, early_shapes[0][0])]
        late_plan = [(0, (), lambda i: i * 0, late_shapes[0][0])]
        given = [(jnp.pad(matrix_rows[3 * width :], ((TAIL, 0), (0, 0))), 0, 0)]

    out, middle_grad, mixed_grad, gain_two_grad, *early = feed_forward(
        index,
        block_in,
        mixed,
        cotangent.reshape(tokens, width),
        gain_two,
        given,
        block if planes else None,
        FF,
        size,
        early_plan,
        early_shapes,
    )
    standard_flat = standard.reshape(far, width)
    last = [gain_one, gain_two_grad, w_qkv, summary_low, standard_flat, gain_sum]
    if planes:
        (early_kept, early_sent), mixed_grad = together(sum_core(*early), mixed_grad)
        early_in = across_plane(early_sent)
    steps = images * local_rows // math.gcd(local_rows, 4)
    backward = attention_backward(
        (0, steps),
        None,
        index,
        block_in,
        query,
        key,
        value,
        key_far,
        value_far,
        probs,
        mixed_grad,
        last,
        local_rows,
        columns,
        late_plan,
        late_shapes,
    )
    query_grad, key_grad, value_grad, shared, *late = backward
    if planes:
        (late_kept, late_sent), shared, early = together(
            sum_core(*late), shared + swap_core(shared), sum_plane(early_kept, *early_in)
        )
        small = shared[far:]
        late_sent = [with_sums(sent[0], small) for sent in late_sent]
        late_sent[0] = jnp.concatenate([late_sent[0], shared[:far].astype(HALF)])
        late_in = across_plane(late_sent)
        by_mask = [
            jnp.where(z == i, 0.0, lax.dynamic_index_in_dim(early, (z ^ i) - 1, 0, keepdims=False))
            for i in range(4)
        ]
        early_in = swap_near(jnp.stack([by_mask[1], by_mask[3]]).astype(HALF))
        late_in, early_in = together(late_in, early_in)
        rows = late_kept.shape[1]
        both = rows + small.shape[0] + 8
        late = sum_plane(late_kept[0], *[array[:rows] for array in late_in])
        over_x, over_y, over_both = (sums_of(array[rows:both]) for array in late_in)
        shared = shared[:far] + late_in[0][both:].astype(SINGLE)
        small = (small + over_x) + (over_y + over_both)
        early_far = send_far((by_mask[2] + early_in[1].astype(SINGLE)).astype(HALF))
        near_in = swap_near(with_sums(late.astype(HALF), small))
    else:
        for axis, distance, _ in row_hops():
            shared = shared + swap(shared, axis, distance)
        small = shared[far:]
        for axis, distance, _ in image_hops():
            small = small + swap(small, axis, distance)
    input_grad = input_grads(
        block_in, gain_one, query_grad, key_grad, value_grad, w_qkv, middle_grad, local_rows, columns
    )
    if planes:
        near_in, early_far, input_grad = together(near_in, early_far, input_grad)
        late = late + near_in[:rows].astype(SINGLE)
        small = small + sums_of(near_in[rows:])
        late_own = late + send_down(late.astype(HALF)).astype(SINGLE)
        small = small + swap_far(small)
    own_grad = lax.dynamic_slice_in_dim(
        shared[:far].reshape(images, rows_all, width), first_row, local_rows, axis=1
    )
    own_standard = lax.dynamic_slice_in_dim(standard, first_row, local_rows, axis=1)
    mean_grad = summary_inv * (
        own_grad - small[0] / summary_count - own_standard * (small[1] / summary_count)
    )
    input_grad = input_grad.reshape(activations.shape) + (mean_grad / columns)[:, :, None, :]
    if planes:
        early_own = by_mask[0] + early_in[0].astype(SINGLE) + early_far.astype(SINGLE)
        head = jnp.where(
            me == 0,
            jnp.concatenate([jnp.zeros((TAIL - 4, width), SINGLE), small[2:6]]),
            jnp.where(me == 8, small[8:], 0.0),
        )
        mine = jnp.where(z == 0, late_own, early_own)
        mine = jnp.concatenate([mine[:TAIL] + head, mine[TAIL:]])
        weight_grad = lax.dynamic_slice(mine.reshape(-1), (start,), weights.shape)
    else:
        grad_rows = jnp.concatenate([late[0][TAIL:], early[0][TAIL:]]).astype(SINGLE)
        weight_grad = scatter_grads(small[2:6], grad_rows, weights.shape[0])
    return (
        out.reshape(activations.shape),
        input_grad,
        weight_grad,
        summary_mean,
        summary_var,
    )


def solution(mesh):
    placed = (P("img", "row", None, None), P("img", "row", None, None), P(("img", "row")))
    return jax.shard_map(
        per_device,
        mesh=mesh,
        in_specs=placed,
        out_specs=(
            P("img", "row", None, None),
            P("img", "row", None, None),
            P(("img", "row")),
            P(),
            P(),
        ),
        check_vma=False,
    )
```

```python
import functools
import math

import jax
import jax.numpy as jnp
from jax import lax
from jax.experimental import pallas as pl
from jax.experimental.pallas import tpu as pltpu
from jax.sharding import PartitionSpec as P

FF = 2048
HEADS = 8
LANES = 128


EPS = 1e-05
NEGATIVE = -1e30
HALF = jnp.bfloat16
SINGLE = jnp.float32
VMEM_BYTES = 56 * 1024 * 1024

TAIL = 16


def swap(value, axis, distance):
    size = lax.axis_size(axis)
    return lax.ppermute(value, axis, [(i, i ^ distance) for i in range(size)])


def hops():
    rows, images = lax.axis_size("row"), lax.axis_size("img")
    inner = ("row", 1, 1)
    across = ("row", 2, 2)
    along = ("img", 1, rows)
    outer = []
    distance = images // 2
    while distance > 1:
        outer.append(("img", distance, distance * rows))
        distance //= 2
    distance = rows // 2
    while distance > 2:
        outer.append(("row", distance, distance))
        distance //= 2
    return inner, across, along, outer


def piece_order():
    inner, across, along, outer = hops()
    masks = [0]
    for _, _, mask in outer:
        masks = masks + [m ^ mask for m in masks]
    near = (
        masks
        + [m ^ across[2] for m in masks]
        + [m ^ along[2] for m in masks]
        + [m ^ across[2] ^ along[2] for m in masks]
    )
    return near + [m ^ inner[2] for m in near]


def device_index():
    return lax.axis_index("img") * lax.axis_size("row") + lax.axis_index("row")


def gather_pieces(own):
    inner, across, along, outer = hops()
    held = own[None]
    for axis, distance, _ in outer:
        held = jnp.concatenate([held, swap(held, axis, distance)])
    half = held.shape[0] // 2
    held_x = swap(held, across[0], across[1])
    held_y = swap(held, along[0], along[1])
    corner_first = swap(held_x[:half], along[0], along[1])
    corner_second = swap(held_y[half:], across[0], across[1])
    near = [held, held_x, held_y, corner_first, corner_second]
    far = [swap(part, inner[0], inner[1]) for part in near]
    return jnp.concatenate(near + far)


def scatter_pieces(pieces):
    inner, across, along, outer = hops()

    def add(kept, sent, axis, distance):
        return kept + swap(sent.astype(HALF), axis, distance).astype(SINGLE)

    count = pieces.shape[0] // 2
    near = add(pieces[:count], pieces[count:], inner[0], inner[1])
    quarter = count // 4
    half = quarter // 2
    held, held_x, held_y, corner = (near[i * quarter : (i + 1) * quarter] for i in range(4))
    first = add(
        jnp.concatenate([held[:half], held_x[:half]]),
        jnp.concatenate([held_y[:half], corner[:half]]),
        along[0],
        along[1],
    )
    second = add(
        jnp.concatenate([held[half:], held_y[half:]]),
        jnp.concatenate([held_x[half:], corner[half:]]),
        across[0],
        across[1],
    )
    first = add(first[:half], first[half:], across[0], across[1])
    second = add(second[:half], second[half:], along[0], along[1])
    held = jnp.concatenate([first, second])
    for axis, distance, _ in reversed(outer):
        half = held.shape[0] // 2
        held = add(held[:half], held[half:], axis, distance)
    return held[0]


def row_hops():
    inner, across, _, outer = hops()
    return [inner, across] + [hop for hop in outer if hop[0] == "row"]


def image_hops():
    _, _, along, outer = hops()
    return [along] + [hop for hop in outer if hop[0] == "img"]


def gather_rows(own):
    held, masks = own[None], [0]
    for axis, distance, mask in row_hops():
        held = jnp.concatenate([held, swap(held, axis, distance)])
        masks = masks + [m ^ mask for m in masks]
    place = [0] * len(masks)
    for at, mask in enumerate(masks):
        place[mask] = at
    order = jnp.asarray(place, jnp.int32)[jnp.arange(len(masks)) ^ lax.axis_index("row")]
    held = jnp.moveaxis(jnp.take(held, order, axis=0, mode="clip"), 0, 1)
    return held.reshape(own.shape[0], -1, own.shape[-1])


def gather_weights(weights, model_width):
    length = weights.shape[0]
    me = device_index()
    devices = lax.axis_size("img") * lax.axis_size("row")
    block = length // model_width
    rest = length % model_width
    start = TAIL * model_width + rest * me - 4 * model_width
    own = lax.dynamic_update_slice(jnp.zeros(((block + TAIL) * model_width,), HALF), weights, (start,))
    own = own.reshape(block + TAIL, model_width)
    pieces = gather_pieces(own)
    place = [0] * devices
    for at, mask in enumerate(piece_order()):
        place[mask] = at
    order = jnp.asarray(place, jnp.int32)[jnp.arange(devices) ^ me]
    pieces = jnp.take(pieces, order, axis=0, mode="clip")
    tails = jnp.concatenate([pieces[1:, :TAIL], jnp.zeros((1, TAIL, model_width), HALF)])
    body = jnp.concatenate([pieces[:, TAIL:block], pieces[:, block:] + tails], axis=1)
    return pieces[0, TAIL - 4 : TAIL], body.reshape(devices * block, model_width)


def scatter_grads(vectors, rows, length):
    model_width = rows.shape[1]
    me = device_index()
    devices = lax.axis_size("img") * lax.axis_size("row")
    block = length // model_width
    rest = length % model_width
    whole = jnp.concatenate([jnp.zeros((TAIL - 4, model_width), SINGLE), vectors, rows])
    place = jnp.asarray(piece_order(), jnp.int32)
    pieces = jnp.stack([whole[block * s : block * s + block + TAIL] for s in range(devices)])
    pieces = jnp.take(pieces, place ^ me, axis=0, mode="clip")
    mine = scatter_pieces(pieces)
    start = TAIL * model_width + rest * me - 4 * model_width
    return lax.dynamic_slice(mine.reshape(-1), (start,), (length,))


def dot(left, right):
    return jnp.dot(left, right, preferred_element_type=SINGLE)


def dot_rows(left, right):
    return lax.dot_general(left, right, (((1,), (1,)), ((), ())), preferred_element_type=SINGLE)


def dot_outer(left, right):
    return lax.dot_general(left, right, (((0,), (0,)), ((), ())), preferred_element_type=SINGLE)


def normalize(values):
    centred = values - jnp.mean(values, axis=-1, keepdims=True)
    inverse = lax.rsqrt(jnp.mean(centred * centred, axis=-1, keepdims=True) + EPS)
    return (centred * inverse, inverse)


def norm_back(grad_norm, normed, inverse):
    return inverse * (
        grad_norm
        - jnp.mean(grad_norm, axis=-1, keepdims=True)
        - normed * jnp.mean(grad_norm * normed, axis=-1, keepdims=True)
    )


def whole_block(shape):
    return pl.BlockSpec(shape, lambda *_: (0,) * len(shape), pipeline_mode=pl.Buffered(1))


def head_keys(rows_per_step, model_width):
    return [
        (row, pair, half)
        for row in range(rows_per_step)
        for pair in range(model_width // LANES)
        for half in range(2)
    ]


def attention_forward_kernel(
    scaling,
    rows_per_step,
    local_rows,
    first_row_ref,
    block_ref,
    gain_ref,
    w_ref,
    key_far_ref,
    value_far_ref,
    causal_ref,
    query_ref,
    key_ref,
    value_ref,
    mixed_ref,
    probs_ref,
):
    columns = causal_ref.shape[0]
    far = key_far_ref.shape[0]
    width = block_ref.shape[1]
    head_width = width // HEADS
    step = pl.program_id(0)
    normed, _ = normalize(block_ref[...].astype(SINGLE))
    attn_in = (normed * gain_ref[...]).astype(HALF)
    for i, ref in enumerate((query_ref, key_ref, value_ref)):
        ref[...] = dot(attn_in, w_ref[:, i * width : (i + 1) * width]).astype(HALF)
    first_half = lax.broadcasted_iota(jnp.int32, (columns + far, LANES), 1) < head_width
    far_index = lax.broadcasted_iota(jnp.int32, (far, columns), 0)
    keys = head_keys(rows_per_step, width)
    for start in range(0, len(keys), 4 * HEADS):
        group = keys[start : start + 4 * HEADS]
        scores, low, mixed = {}, {}, {}
        for row, pair, half in group:
            global_row = first_row_ref[0] + lax.rem(step * rows_per_step + row, local_rows)
            far_bias = jnp.where(far_index < global_row, 0.0, NEGATIVE)
            tokens = slice(row * columns, (row + 1) * columns)
            lanes = slice(pair * LANES, (pair + 1) * LANES)
            all_keys = jnp.concatenate([key_ref[tokens, lanes], key_far_ref[:, lanes]], axis=0)
            one_head = jnp.where(
                first_half if half == 0 else ~first_half, all_keys, jnp.zeros_like(all_keys)
            )
            found = dot_rows(one_head, query_ref[tokens, lanes])
            scores[row, pair, half] = jnp.concatenate(
                [found[:columns] + causal_ref[...], found[columns:] + far_bias], axis=0
            )
        for row, pair, half in group:
            found = scores.pop((row, pair, half))
            top = jnp.max(found, axis=0, keepdims=True)
            powers = jnp.exp2((found - top) * (scaling * math.log2(math.e)))
            inverse = 1.0 / jnp.sum(powers, axis=0, keepdims=True)
            low[row, pair, half] = (powers * inverse).astype(HALF)
            probs_ref[row, 2 * pair + half] = low[row, pair, half]
        for row, pair, half in group:
            tokens = slice(row * columns, (row + 1) * columns)
            lanes = slice(pair * LANES, (pair + 1) * LANES)
            all_values = jnp.concatenate([value_ref[tokens, lanes], value_far_ref[:, lanes]], axis=0)
            turned = all_values.T[half * head_width : (half + 1) * head_width]
            mixed[row, pair, half] = dot(turned, low[row, pair, half])
        for row, pair, half in group:
            if half == 0:
                tokens = slice(row * columns, (row + 1) * columns)
                lanes = slice(pair * LANES, (pair + 1) * LANES)
                both = jnp.concatenate([mixed[row, pair, 0], mixed[row, pair, 1]], axis=0)
                mixed_ref[tokens, lanes] = both.T.astype(HALF)


def image_groups(images):
    return [(0, 1), (1, images - 1)] if images > 1 else [(0, images)]


def step_groups(steps):
    if steps < 4:
        return [(0, steps)]
    first, last = steps // 3, max(1, steps // 6)
    return [(0, first), (first, steps - first - last), (steps - last, last)]


def kept_arrays(previous, start):
    if previous is None:
        return ([], [], {})
    specs = [pl.BlockSpec(memory_space=pl.ANY)] * len(previous)
    return (list(previous), specs, {start + i: i for i in range(len(previous))})


def attention_forward(
    group, previous, block_in, gain, w_qkv, key_far, value_far, first_row, local_rows, columns
):
    tokens, width = block_in.shape
    images, far, _ = key_far.shape
    first_image, count = group
    rows_per_step = math.gcd(local_rows, 4)
    steps = local_rows // rows_per_step
    first_step = first_image * steps
    size = rows_per_step * columns
    position = jnp.arange(columns)
    causal = jnp.where(position[:, None] <= position[None, :], 0.0, NEGATIVE).astype(SINGLE)
    block = pl.BlockSpec((size, width), lambda i, _: (first_step + i, 0))
    far_block = pl.BlockSpec((None, far, width), lambda i, _: (first_image + i // steps, 0, 0))
    probs_block = pl.BlockSpec(
        (rows_per_step, HEADS, columns + far, columns), lambda i, _: (first_step + i, 0, 0, 0)
    )
    inputs = [block_in, gain, w_qkv, key_far, value_far, causal]
    kept, kept_specs, aliases = kept_arrays(previous, 1 + len(inputs))
    low = jax.ShapeDtypeStruct((tokens, width), HALF)
    part = count * tokens // images
    kernel = functools.partial(
        attention_forward_kernel, 1.0 / math.sqrt(width // HEADS), rows_per_step, local_rows
    )

    def body(*refs):
        kernel(*refs[: 1 + len(inputs)], *refs[1 + len(inputs) + len(kept) :])

    return pl.pallas_call(
        body,
        grid_spec=pltpu.PrefetchScalarGridSpec(
            num_scalar_prefetch=1,
            grid=(count * steps,),
            in_specs=[
                block,
                whole_block((1, width)),
                whole_block((width, 3 * width)),
                far_block,
                far_block,
                whole_block((columns, columns)),
            ]
            + kept_specs,
            out_specs=[block] * 4 + [probs_block],
        ),
        out_shape=[low] * 4
        + [jax.ShapeDtypeStruct((images * local_rows, HEADS, columns + far, columns), HALF)],
        input_output_aliases=aliases,
        compiler_params=pltpu.CompilerParams(vmem_limit_bytes=VMEM_BYTES),
        cost_estimate=pl.CostEstimate(
            flops=part * width * (6 * width + 8 * (columns + far)),
            bytes_accessed=part * width * 12 + part * HEADS * (columns + far) * 2,
            transcendentals=part * HEADS * (columns + far),
        ),
        name="attention_forward",
    )(first_row, *inputs, *kept)


GELU_OUTER = math.sqrt(2.0 / math.pi)
GELU_CUBE = 0.044715


def gelu_and_slope(value):
    square = value * value
    gate = 0.5 * jnp.tanh(value * (GELU_OUTER * GELU_CUBE * square + GELU_OUTER)) + 0.5
    activated = value * gate
    slope = gate + activated * (1.0 - gate) * (6.0 * GELU_OUTER * GELU_CUBE * square + 2.0 * GELU_OUTER)
    return (activated, slope)


def start_pieces(plan, flat_ref, outs, sems, index):
    copies = []
    for i, (out, place, offset, rows) in enumerate(plan):
        source = flat_ref.at[pl.ds(pl.multiple_of(offset(index), TAIL), rows)]
        target = outs[out].at[place] if place else outs[out]
        copies.append(pltpu.make_async_copy(source, target, sems.at[i]))
    for copy in copies:
        copy.start()
    return copies


def feed_forward_kernel(
    chunk,
    plan,
    masks,
    block,
    index_ref,
    block_ref,
    mixed_ref,
    cotangent_ref,
    gain_ref,
    *rest,
):
    given, rest = rest[: max(1, 3 * len(masks))], rest[max(1, 3 * len(masks)) :]
    out_ref, middle_grad_ref, mixed_grad_ref, grad_gain_ref, *rest = rest
    *pieces, grad_out_ref, grad_inner_ref, grad_outer_ref, w_inner_ref, flat_ref, sems = rest
    width, hidden = w_inner_ref.shape
    groups = hidden // width
    per = 256 // groups
    inner_start = TAIL + width
    outer_start = inner_start + hidden
    w_out_ref = flat_ref.at[TAIL:inner_start]
    w_outer_ref = flat_ref.at[outer_start:]

    @pl.when(pl.program_id(0) == 0)
    def _():
        for ref in (grad_out_ref, grad_inner_ref, grad_outer_ref, grad_gain_ref):
            ref[...] = jnp.zeros_like(ref)
        if block is None:
            flat_ref[...] = given[0][...]
        else:
            plane = 8 * block
            here, z = lax.rem(index_ref[0], 8), lax.div(index_ref[0], 8)
            own, first, last = (
                list(zip(given[i * len(masks) : (i + 1) * len(masks)], masks)) for i in range(3)
            )
            clear_seams(flat_ref, block, 3)

            @pl.when(z == 0)
            def _():
                assemble(flat_ref, first, here, block, 0)

            @pl.when(z > 0)
            def _():
                assemble(flat_ref, own, here, block, (z - 1) * plane)

            for i, slot in enumerate(second_slots(z)):
                pieces_here = [(ref.at[i], mask) for ref, mask in last]
                assemble(flat_ref, pieces_here, here, block, (slot - 1) * plane)
        mix = weave(groups, per)
        for c in range(width // per):
            start = inner_start + c * groups * per
            parted = dot_outer(mix, flat_ref[start : start + groups * per]).astype(HALF)
            for g in range(groups):
                w_inner_ref[c * per : (c + 1) * per, g * width : (g + 1) * width] = parted[
                    g * per : (g + 1) * per
                ]

    mixed = mixed_ref[...]
    cotangent = cotangent_ref[...]
    middle = block_ref[...].astype(SINGLE) + dot(mixed, w_out_ref[...])
    normed, inverse = normalize(middle)
    ff_in = (normed * gain_ref[...]).astype(HALF)
    out = middle
    ff_grad = jnp.zeros_like(middle)
    cotangent_turned = cotangent.T
    ff_turned = ff_in.T
    count = hidden // chunk
    spans = [slice(j * chunk, (j + 1) * chunk) for j in range(count)]

    def products(j):
        return (dot(ff_in, w_inner_ref[:, spans[j]]), dot_rows(cotangent, w_outer_ref[spans[j], :]))

    ready = products(0)
    for j in range(count):
        inner, act_grad = ready
        if j + 1 < count:
            ready = products(j + 1)
        activated, slope = gelu_and_slope(inner)
        activated = activated.astype(HALF)
        inner_grad = (slope * act_grad).astype(HALF)
        out = out + dot(activated, w_outer_ref[spans[j], :])
        ff_grad = ff_grad + dot_rows(inner_grad, w_inner_ref[:, spans[j]])
        grad_inner_ref[:, spans[j]] += dot(ff_turned, inner_grad)
        grad_outer_ref[:, spans[j]] += dot(cotangent_turned, activated)
    out_ref[...] = out.astype(HALF)
    grad_gain_ref[...] += jnp.sum(ff_grad * normed, axis=0, keepdims=True)
    middle_grad = cotangent.astype(SINGLE) + norm_back(ff_grad * gain_ref[...], normed, inverse)
    middle_grad_ref[...] = middle_grad
    branch_grad = middle_grad.astype(HALF)
    mixed_grad_ref[...] = dot_rows(branch_grad, w_out_ref[...]).astype(HALF)
    grad_out_ref[...] += dot_outer(mixed, branch_grad)

    @pl.when(pl.program_id(0) == pl.num_programs(0) - 1)
    def _():
        flat_ref[:TAIL] = jnp.zeros((TAIL, width), HALF)
        flat_ref[TAIL : TAIL + width] = grad_out_ref[...].astype(HALF)
        mix = weave(groups, per)
        for c in range(width // per):
            parts = [
                grad_inner_ref[c * per : (c + 1) * per, g * width : (g + 1) * width].astype(HALF)
                for g in range(groups)
            ]
            start = TAIL + width + c * groups * per
            woven = dot(mix, jnp.concatenate(parts, axis=0))
            flat_ref[start : start + groups * per] = woven.astype(HALF)
        start = TAIL + width + hidden
        for j in range(hidden // width):
            turned = grad_outer_ref[:, j * width : (j + 1) * width].astype(HALF).T
            flat_ref[start + j * width : start + (j + 1) * width] = turned
        for copy in start_pieces(plan, flat_ref, pieces, sems, index_ref[0]):
            copy.wait()


def weave(groups, per):
    size = groups * per
    row = lax.broadcasted_iota(jnp.int32, (size, size), 0)
    column = lax.broadcasted_iota(jnp.int32, (size, size), 1)
    wanted = lax.rem(row, groups) * per + lax.div(row, groups)
    return (wanted == column).astype(SINGLE).astype(HALF)


def piece_outputs(shapes):
    return (
        [pl.BlockSpec(memory_space=pl.ANY)] * len(shapes),
        [jax.ShapeDtypeStruct(shape, HALF) for shape in shapes],
    )


def feed_forward(index, block_in, mixed, cotangent, gain, given, block, hidden, size, plan, shapes):
    tokens, width = block_in.shape
    tile = pl.BlockSpec((size, width), lambda i, _: (i, 0))
    piece_specs, piece_shapes = piece_outputs(shapes)
    masks = [] if block is None else [mask for _, mask in given[: len(given) // 3]]
    arrays = [given] if block is None else [array for array, _ in given]
    return pl.pallas_call(
        functools.partial(feed_forward_kernel, 256, plan, masks, block),
        grid_spec=pltpu.PrefetchScalarGridSpec(
            num_scalar_prefetch=1,
            grid=(tokens // size,),
            in_specs=[tile, tile, tile, whole_block((1, width))] + vmem_specs(len(arrays)),
            out_specs=[tile, tile, tile, whole_block((1, width))] + piece_specs,
            scratch_shapes=[
                pltpu.VMEM((width, width), SINGLE),
                pltpu.VMEM((width, hidden), SINGLE),
                pltpu.VMEM((width, hidden), SINGLE),
                pltpu.VMEM((width, hidden), HALF),
                pltpu.VMEM((TAIL + width + 2 * hidden, width), HALF),
                pltpu.SemaphoreType.DMA((len(plan),)),
            ],
        ),
        out_shape=[
            jax.ShapeDtypeStruct((tokens, width), HALF),
            jax.ShapeDtypeStruct((tokens, width), SINGLE),
            jax.ShapeDtypeStruct((tokens, width), HALF),
            jax.ShapeDtypeStruct((1, width), SINGLE),
        ]
        + piece_shapes,
        compiler_params=pltpu.CompilerParams(vmem_limit_bytes=VMEM_BYTES),
        cost_estimate=pl.CostEstimate(
            flops=tokens * width * (6 * width + 12 * hidden),
            bytes_accessed=tokens * width * 14 + width * hidden * 8,
            transcendentals=tokens * hidden,
        ),
        name="feed_forward",
    )(index, block_in, mixed, cotangent, gain, *arrays)


def attention_backward_kernel(
    scaling,
    rows_per_step,
    per_image,
    first_step,
    plan,
    ends,
    index_ref,
    block_ref,
    query_ref,
    key_ref,
    value_ref,
    key_far_ref,
    value_far_ref,
    probs_ref,
    mixed_grad_ref,
    *rest,
):
    rest = list(rest)
    earlier = None
    if first_step > 0:
        earlier, rest = rest[:3], rest[6:]
    if ends:
        fixed, rest = rest[:6], rest[6:]
    query_grad_ref, key_grad_ref, value_grad_ref, *rest = rest
    if ends:
        shared_ref, *rest = rest
        small_ref = shared_ref.at[shared_ref.shape[0] - 8 - TAIL :]
        *pieces, total_ref, key_far_grad_ref, value_far_grad_ref, flat_ref, sems = rest
    else:
        total_ref, key_far_grad_ref, value_far_grad_ref = rest
    width = query_ref.shape[1]
    head_width = width // HEADS
    far = key_far_ref.shape[0]
    columns = query_ref.shape[0] // rows_per_step
    image = lax.div(first_step + pl.program_id(0), per_image)

    @pl.when(pl.program_id(0) == 0)
    def _():
        for i, ref in enumerate((total_ref, key_far_grad_ref, value_far_grad_ref)):
            ref[...] = jnp.zeros_like(ref) if earlier is None else earlier[i][...]

    first_half = lax.broadcasted_iota(jnp.int32, (columns + far, LANES), 1) < head_width
    keys = head_keys(rows_per_step, width)
    for start in range(0, len(keys), 2 * HEADS):
        group = keys[start : start + 2 * HEADS]
        prob_grad, score_grad, value_grad, key_grad, query_grad = {}, {}, {}, {}, {}
        for row, pair, half in group:
            tokens = slice(row * columns, (row + 1) * columns)
            lanes = slice(pair * LANES, (pair + 1) * LANES)
            all_values = jnp.concatenate([value_ref[tokens, lanes], value_far_ref[:, lanes]], axis=0)
            one_head = jnp.where(
                first_half if half == 0 else ~first_half, all_values, jnp.zeros_like(all_values)
            )
            prob_grad[row, pair, half] = dot_rows(one_head, mixed_grad_ref[tokens, lanes])
        for row, pair, half in group:
            tokens = slice(row * columns, (row + 1) * columns)
            lanes = slice(pair * LANES, (pair + 1) * LANES)
            value_grad[row, pair, half] = dot(
                probs_ref[row, 2 * pair + half], mixed_grad_ref[tokens, lanes]
            )
        for row, pair, half in group:
            probs = probs_ref[row, 2 * pair + half].astype(SINGLE)
            grad = prob_grad.pop((row, pair, half))
            total = jnp.sum(probs * grad, axis=0, keepdims=True)
            score_grad[row, pair, half] = (probs * (grad - total)).astype(HALF)
        for row, pair, half in group:
            tokens = slice(row * columns, (row + 1) * columns)
            lanes = slice(pair * LANES, (pair + 1) * LANES)
            key_grad[row, pair, half] = dot(score_grad[row, pair, half], query_ref[tokens, lanes])
            all_keys = jnp.concatenate([key_ref[tokens, lanes], key_far_ref[:, lanes]], axis=0)
            turned = all_keys.T[half * head_width : (half + 1) * head_width]
            query_grad[row, pair, half] = dot(turned, score_grad[row, pair, half])
        for row, pair, half in group:
            if half == 0:
                tokens = slice(row * columns, (row + 1) * columns)
                lanes = slice(pair * LANES, (pair + 1) * LANES)
                first, second = (row, pair, 0), (row, pair, 1)
                value_both = jnp.where(first_half, value_grad[first], value_grad[second])
                key_both = jnp.where(first_half, key_grad[first], key_grad[second]) * scaling
                value_grad_ref[tokens, lanes] = value_both[:columns].astype(HALF)
                key_grad_ref[tokens, lanes] = key_both[:columns].astype(HALF)
                value_far_grad_ref[image, :, lanes] += value_both[columns:]
                key_far_grad_ref[image, :, lanes] += key_both[columns:]
                query_both = jnp.concatenate([query_grad[first], query_grad[second]], axis=0) * scaling
                query_grad_ref[tokens, lanes] = query_both.T.astype(HALF)
    normed, _ = normalize(block_ref[...].astype(SINGLE))
    turned = normed.astype(HALF).T
    for i, ref in enumerate((query_grad_ref, key_grad_ref, value_grad_ref)):
        total_ref[:, i * width : (i + 1) * width] += dot(turned, ref[...])
    if not ends:
        return

    @pl.when(pl.program_id(0) == pl.num_programs(0) - 1)
    def _():
        gain_ref, gain_two_grad_ref, w_ref, summary_ref, standard_ref, gain_sum_ref = fixed

        key_low = key_far_grad_ref[...].reshape(-1, width).astype(HALF)
        value_low = value_far_grad_ref[...].reshape(-1, width).astype(HALF)
        gain = jnp.broadcast_to(gain_ref[...], (8, width)).T[:, :1]
        matched = jnp.zeros((width, width), SINGLE)
        flat_ref[:TAIL] = jnp.zeros((TAIL, width), HALF)
        for i in range(3):
            total = total_ref[:, i * width : (i + 1) * width]
            matched = matched + total * w_ref[:, i * width : (i + 1) * width].astype(SINGLE)
            grad = total * gain
            if i > 0:
                grad = grad + dot_outer(summary_ref[...], key_low if i == 1 else value_low)
            flat_ref[TAIL + i * width : TAIL + (i + 1) * width] = grad.astype(HALF)
            if i == 2:
                small_ref[8:] = grad[width - TAIL :]
        copies = start_pieces(plan, flat_ref, pieces, sems, index_ref[0])
        summary_grad = dot_rows(key_low, w_ref[:, width : 2 * width]) + dot_rows(
            value_low, w_ref[:, 2 * width :]
        )
        standard = standard_ref[...]
        standard_grad = summary_grad * gain_sum_ref[...]
        shared_ref[: standard.shape[0]] = standard_grad

        def fold(value):
            return jnp.sum(value, axis=0, keepdims=True)

        small_ref[0:1] = fold(standard_grad)
        small_ref[1:2] = fold(standard_grad * standard)
        small_ref[2:3] = fold(matched.T)
        small_ref[3:4] = fold(summary_grad * standard)
        small_ref[4:5] = fold(summary_grad)
        small_ref[5:6] = gain_two_grad_ref[...]
        small_ref[6:8] = jnp.zeros((2, width), SINGLE)
        for copy in copies:
            copy.wait()


def attention_backward(
    group,
    previous,
    index,
    block_in,
    query,
    key,
    value,
    key_far,
    value_far,
    probs,
    mixed_grad,
    last,
    local_rows,
    columns,
    plan,
    shapes,
):
    tokens, width = query.shape
    images, far, _ = key_far.shape
    first_step, count = group
    rows_per_step = math.gcd(local_rows, 4)
    per_image = local_rows // rows_per_step
    ends = first_step + count == images * per_image
    size = rows_per_step * columns
    part = count * size
    block = pl.BlockSpec((size, width), lambda i, _: (first_step + i, 0))
    far_block = pl.BlockSpec((None, far, width), lambda i, _: ((first_step + i) // per_image, 0, 0))
    probs_block = pl.BlockSpec(
        (rows_per_step, HEADS, columns + far, columns), lambda i, _: (first_step + i, 0, 0, 0)
    )
    inputs = [block_in, query, key, value, key_far, value_far, probs, mixed_grad]
    in_specs = [block] * 4 + [far_block] * 2 + [probs_block, block]
    aliases = {}
    total_shape = (width, 3 * width)
    far_shape = (images, far, width)
    if previous is not None:
        sums = list(previous[3:])
        inputs = inputs + sums
        in_specs = in_specs + [whole_block(array.shape) for array in sums]
        kept, kept_specs, aliases = kept_arrays(previous[:3], 1 + len(inputs))
        inputs, in_specs = inputs + kept, in_specs + kept_specs
    out_specs = [block] * 3
    out_shape = [jax.ShapeDtypeStruct((tokens, width), HALF)] * 3
    scratch = []
    if ends:
        inputs = inputs + list(last)
        in_specs = in_specs + [whole_block(array.shape) for array in last]
        piece_specs, piece_shapes = piece_outputs(shapes)
        summaries = images * far
        shared_shape = (summaries + 8 + TAIL, width)
        out_specs += [whole_block(shared_shape)] + piece_specs
        out_shape += [jax.ShapeDtypeStruct(shared_shape, SINGLE)] + piece_shapes
        scratch = [
            pltpu.VMEM(total_shape, SINGLE),
            pltpu.VMEM(far_shape, SINGLE),
            pltpu.VMEM(far_shape, SINGLE),
            pltpu.VMEM((TAIL + 3 * width, width), HALF),
            pltpu.SemaphoreType.DMA((len(plan),)),
        ]
    else:
        out_specs += [whole_block(total_shape), whole_block(far_shape), whole_block(far_shape)]
        out_shape += [
            jax.ShapeDtypeStruct(total_shape, SINGLE),
            jax.ShapeDtypeStruct(far_shape, SINGLE),
            jax.ShapeDtypeStruct(far_shape, SINGLE),
        ]
    return pl.pallas_call(
        functools.partial(
            attention_backward_kernel,
            1.0 / math.sqrt(width // HEADS),
            rows_per_step,
            per_image,
            first_step,
            plan,
            ends,
        ),
        grid_spec=pltpu.PrefetchScalarGridSpec(
            num_scalar_prefetch=1,
            grid=(count,),
            in_specs=in_specs,
            out_specs=out_specs,
            scratch_shapes=scratch,
        ),
        out_shape=out_shape,
        input_output_aliases=aliases,
        compiler_params=pltpu.CompilerParams(vmem_limit_bytes=VMEM_BYTES),
        cost_estimate=pl.CostEstimate(
            flops=part * width * (6 * width + 16 * (columns + far)),
            bytes_accessed=part * width * 16 + part * HEADS * (columns + far) * 2,
            transcendentals=0,
        ),
        name="attention_backward",
    )(index, *inputs)


def input_grad_kernel(
    block_ref,
    gain_ref,
    query_grad_ref,
    key_grad_ref,
    value_grad_ref,
    w_ref,
    middle_grad_ref,
    out_ref,
):
    width = block_ref.shape[1]
    attn_grad = (
        dot_rows(query_grad_ref[...], w_ref[:, :width])
        + dot_rows(key_grad_ref[...], w_ref[:, width : 2 * width])
        + dot_rows(value_grad_ref[...], w_ref[:, 2 * width :])
    )
    normed, inverse = normalize(block_ref[...].astype(SINGLE))
    out_ref[...] = middle_grad_ref[...] + norm_back(attn_grad * gain_ref[...], normed, inverse)


def input_grads(
    block_in, gain, query_grad, key_grad, value_grad, w_qkv, middle_grad, local_rows, columns
):
    tokens, width = block_in.shape
    size = math.gcd(local_rows, 2) * columns
    block = pl.BlockSpec((size, width), lambda i: (i, 0))
    return pl.pallas_call(
        input_grad_kernel,
        grid=(tokens // size,),
        in_specs=[block, whole_block((1, width))]
        + [block] * 3
        + [whole_block((width, 3 * width)), block],
        out_specs=block,
        out_shape=jax.ShapeDtypeStruct((tokens, width), SINGLE),
        compiler_params=pltpu.CompilerParams(vmem_limit_bytes=VMEM_BYTES),
        cost_estimate=pl.CostEstimate(
            flops=tokens * width * 6 * width, bytes_accessed=tokens * width * 16, transcendentals=0
        ),
        name="input_grads",
    )(block_in, gain, query_grad, key_grad, value_grad, w_qkv, middle_grad)


def clear_seams(flat_ref, block, count):
    for at in range(0, count * 8 * block + 1, block):
        flat_ref[at : at + TAIL] = jnp.zeros((TAIL, flat_ref.shape[1]), HALF)


def assemble(flat_ref, pieces, index, block, base):
    for ref, mask in pieces:
        spot = pl.multiple_of(base + (index ^ mask) * block, TAIL)
        for low, high in ((0, TAIL), (TAIL, block), (block, block + TAIL)):
            rows = pl.ds(spot + low, high - low)
            value = ref[low:high]
            if low != TAIL:
                value = flat_ref[rows] + value
            flat_ref[rows] = value


def second_slots(z):
    return [jnp.where(z < 2, 2, 1), jnp.where(z < 3, 3, 2)]


def parts_of(value):
    high = lax.reduce_precision(value, 8, 7)
    middle = lax.reduce_precision(value - high, 8, 7)
    low = value - high - middle
    return [part.astype(HALF) for part in (high, middle, low)]


def whole_of(parts):
    rows = parts.shape[0] // 3
    parts = parts.astype(SINGLE)
    return (parts[:rows] + parts[rows : 2 * rows]) + parts[2 * rows :]


def projection_weights_kernel(
    masks,
    block,
    images,
    local_rows,
    summary_count,
    index_ref,
    *refs,
):
    count = len(masks)
    own_refs, piece_refs, refs = refs[:count], refs[count : 2 * count], refs[2 * count :]
    w_ref, key_far_ref, value_far_ref, standard_ref, summary_ref, *refs = refs
    *stat_refs, flat_ref, shown_ref, means_ref = refs
    width = flat_ref.shape[1]
    rows = block + TAIL
    here = lax.rem(index_ref[0], 8)
    clear_seams(flat_ref, block, 1)

    @pl.when(index_ref[0] < 8)
    def _():
        assemble(flat_ref, list(zip(own_refs, masks)), here, block, 0)

    @pl.when(index_ref[0] >= 8)
    def _():
        assemble(flat_ref, list(zip(piece_refs, masks)), here, block, 0)

    for ref, mask in zip(piece_refs, masks):
        shown_ref[here ^ mask] = ref[rows:]
    flat_ref[3 * width :] += shown_ref[0, :TAIL]
    for i in range(3):
        w_ref[:, i * width : (i + 1) * width] = flat_ref[TAIL + i * width : TAIL + (i + 1) * width]
    own_rows = images * local_rows
    total = jnp.zeros((2, width), SINGLE)
    for j in range(8):
        total = total + whole_of(shown_ref[j, TAIL:])[own_rows : own_rows + 2]
    for j in range(4):
        means = whole_of(shown_ref[lax.div(here, 4) * 4 + j, TAIL:])
        for image in range(images):
            start = (image * 4 + j) * local_rows
            means_ref[start : start + local_rows] = means[image * local_rows : (image + 1) * local_rows]
    vectors = flat_ref[:TAIL].astype(SINGLE)[TAIL - 4 :]
    mean = total[:1] / summary_count
    variance = total[1:] / summary_count - mean * mean
    inverse = lax.rsqrt(variance + EPS)
    standard = (means_ref[...] - mean) * inverse
    summary = (standard * vectors[1:2] + vectors[2:3]).astype(HALF)
    standard_ref[...] = standard
    summary_ref[...] = summary
    vector_rows = [vectors[i : i + 1] for i in range(4)]
    for ref, value in zip(stat_refs, [mean, variance, inverse] + vector_rows):
        ref[...] = value
    key_far_ref[...] = dot(summary, w_ref[:, width : 2 * width]).astype(HALF)
    value_far_ref[...] = dot(summary, w_ref[:, 2 * width :]).astype(HALF)


def vmem_specs(count):
    return [pl.BlockSpec(memory_space=pltpu.VMEM)] * count


def projection_weights(index, own_pieces, pieces, block, images, local_rows, summary_count):
    arrays, masks = [p[0] for p in own_pieces + pieces], [p[1] for p in pieces]
    width = arrays[0].shape[1]
    far = 4 * images * local_rows
    return pl.pallas_call(
        functools.partial(
            projection_weights_kernel, masks, block, images, local_rows, summary_count
        ),
        in_specs=[pl.BlockSpec(memory_space=pltpu.SMEM)] + vmem_specs(len(arrays)),
        out_specs=vmem_specs(12),
        out_shape=[
            jax.ShapeDtypeStruct((width, 3 * width), HALF),
            jax.ShapeDtypeStruct((far, width), HALF),
            jax.ShapeDtypeStruct((far, width), HALF),
            jax.ShapeDtypeStruct((far, width), SINGLE),
            jax.ShapeDtypeStruct((far, width), HALF),
        ]
        + [jax.ShapeDtypeStruct((1, width), SINGLE)] * 7,
        scratch_shapes=[
            pltpu.VMEM((TAIL + 3 * width, width), HALF),
            pltpu.VMEM((8, 4 * TAIL, width), HALF),
            pltpu.VMEM((far, width), SINGLE),
        ],
        compiler_params=pltpu.CompilerParams(vmem_limit_bytes=VMEM_BYTES),
        name="projection_weights",
    )(index, *arrays)


def with_sums(value, small):
    high = lax.reduce_precision(small[:8], 8, 7)
    return jnp.concatenate(
        [value, high.astype(HALF), (small[:8] - high).astype(HALF), small[8:].astype(HALF)]
    )


def sums_of(rows):
    rows = rows.astype(SINGLE)
    return jnp.concatenate([rows[:8] + rows[8:16], rows[16:]])


def swap_core(value):
    return swap(value, "row", 1)


def swap_x(value):
    return swap(value, "row", 2)


def swap_y(value):
    return swap(value, "img", 1)


def swap_both(value):
    size = lax.axis_size("img") * lax.axis_size("row")
    return lax.ppermute(value, ("img", "row"), [(i, i ^ 6) for i in range(size)])


def swap_near(value):
    return swap(value, "img", 2)


def swap_far(value):
    return swap(value, "img", 4)


def send_far(value):
    return lax.ppermute(value, "img", [(i, i ^ 4) for i in range(lax.axis_size("img")) if i // 2 != 2])


def piece_plan(block, slots):
    plan, shapes = [], []
    rows = block + TAIL
    for out, (side, masks) in enumerate(((0, (0,)), (0, (2,)), (0, (4,)), (0, (6,)), (1, (0, 2, 4, 6)))):
        shapes.append((len(masks), slots, rows))
        for place, mask in enumerate(masks):
            for slot in range(slots):

                def offset(index, mask=mask | side, slot=slot):
                    return (slot * 8 + (lax.rem(index, 8) ^ mask)) * block

                plan.append((out, (place, slot), offset, rows))
    return plan, shapes


def sum_core(kept, over_x, over_y, over_both, other):
    other = swap_core(other)
    own = kept[0].astype(SINGLE) + other[0].astype(SINGLE)
    sent = [
        (piece[0].astype(SINGLE) + other[i + 1].astype(SINGLE)).astype(HALF)
        for i, piece in enumerate((over_x, over_y, over_both))
    ]
    return (own, sent)


def send_down(value):
    return lax.ppermute(value, "img", [(i, i ^ 4) for i in range(lax.axis_size("img")) if i // 2 == 2])


def plane_pieces(own, near):
    pieces = [(array, 2 * i) for i, array in enumerate([own] + list(near))]
    return pieces + [(swap_core(array), mask | 1) for array, mask in pieces]


def across_plane(sent):
    return (swap_x(sent[0]), swap_y(sent[1]), swap_both(sent[2]))


def sum_plane(kept, over_x, over_y, over_both):
    return (kept + over_x.astype(SINGLE)) + (over_y.astype(SINGLE) + over_both.astype(SINGLE))


def together(*values):
    return lax.optimization_barrier(values)


def fits_planes(width, block):
    return lax.axis_size("row") == 4 and lax.axis_size("img") == 8 and 8 * block == 3 * width


def own_rows(weights, width):
    length = weights.shape[0]
    block, rest = length // width, length % width
    start = TAIL * width + rest * device_index() - 4 * width
    own = lax.dynamic_update_slice(jnp.zeros(((block + TAIL) * width,), HALF), weights, (start,))
    return own.reshape(block + TAIL, width), start


def per_device(activations, cotangent, weights):
    images, local_rows, columns, width = activations.shape
    tokens = images * local_rows * columns
    size = tokens // images
    rows_all = local_rows * lax.axis_size("row")
    far = images * rows_all
    first_row = lax.axis_index("row") * local_rows
    summary_count = float(images * lax.axis_size("img") * rows_all)
    block = weights.shape[0] // width
    planes = fits_planes(width, block)
    split = block // 2 // TAIL * TAIL
    me = device_index()
    index = me[None]
    z = lax.axis_index("img") // 2
    block_in = activations.reshape(tokens, width)

    row_means = jnp.mean(activations.astype(SINGLE), axis=2)
    sums = jnp.stack([jnp.sum(row_means, axis=(0, 1)), jnp.sum(row_means * row_means, axis=(0, 1))])
    if planes:
        weights, sums, row_means = together(weights, sums, row_means)
        own, start = own_rows(weights, width)
        piece_rows = block + TAIL
        own = jnp.concatenate([own] + parts_of(sums) + [jnp.zeros((TAIL - 6, width), HALF)])
        over_far = swap_far(own)
        own_rows_only = own[:piece_rows]
        own_near = across_plane([own_rows_only] * 3)
        over_near = swap_near(jnp.stack([own, over_far]))
        over_near, own_near = together(over_near, own_near)
        own_pieces = plane_pieces(own_rows_only, own_near)
        held = [own, over_near[0], over_far, over_near[1]]
        sums = [whole_of(array[piece_rows : piece_rows + 6]) for array in held]
        sums = (sums[0] + sums[1]) + (sums[2] + sums[3])
        held = jnp.stack([array[:piece_rows] for array in held])

        def slot(i):
            return lax.dynamic_index_in_dim(held, z ^ i, 0, keepdims=False)

        means = row_means.reshape(-1, width)
        spare = jnp.zeros((TAIL - 2 - means.shape[0], width), SINGLE)
        known = parts_of(jnp.concatenate([means, sums, spare]))
        first_slot = jnp.concatenate([slot(jnp.where(z == 0, 1, 0)), slot(1)[:TAIL]] + known)
        last_slots = jnp.stack([slot(i) for i in second_slots(z)])
        first_near, last_slots = together(across_plane([first_slot] * 3), last_slots)
        first_pieces = plane_pieces(first_slot, first_near)
        last_near = across_plane([last_slots] * 3)
        w_qkv, key_far, value_far, standard, summary_low, *stats = projection_weights(
            index, own_pieces, first_pieces, block, images, local_rows, summary_count
        )
        summary_mean, summary_var, summary_inv = (row.reshape(width) for row in stats[:3])
        gain_one, gain_sum, bias_sum, gain_two = stats[3:]
        standard = standard.reshape(images, rows_all, width)
    else:
        vectors, matrix_rows = gather_weights(weights, width)
        gain_one, gain_sum, bias_sum, gain_two = (
            vectors[i : i + 1].astype(SINGLE) for i in range(4)
        )
        all_means = gather_rows(row_means)
        for axis, distance, _ in row_hops() + image_hops():
            sums = sums + swap(sums, axis, distance)
        summary_mean = sums[0] / summary_count
        summary_var = sums[1] / summary_count - summary_mean * summary_mean
        summary_inv = lax.rsqrt(summary_var + EPS)
        standard = (all_means - summary_mean) * summary_inv
        summary_low = (standard * gain_sum + bias_sum).astype(HALF).reshape(far, width)
        w_qkv = jnp.concatenate([matrix_rows[i * width : (i + 1) * width] for i in range(3)], axis=1)
        key_far = dot(summary_low, w_qkv[:, width : 2 * width]).astype(HALF)
        value_far = dot(summary_low, w_qkv[:, 2 * width :]).astype(HALF)
    key_far = key_far.reshape(images, rows_all, width)
    value_far = value_far.reshape(images, rows_all, width)

    forward = attention_forward(
        (0, images),
        None,
        block_in,
        gain_one,
        w_qkv,
        key_far,
        value_far,
        first_row[None],
        local_rows,
        columns,
    )
    if planes:
        last_near, forward = together(last_near, forward)
        given = own_pieces + first_pieces + plane_pieces(last_slots, last_near)
    query, key, value, mixed, probs = forward

    if planes:
        late_plan, late_shapes = piece_plan(block, 1)
        early_plan, early_shapes = piece_plan(block, 3)
        early_shapes = [shape + (width,) for shape in early_shapes]
        late_shapes = [shape + (width,) for shape in late_shapes]
    else:
        early_shapes = [(TAIL + width + 2 * FF, width)]
        late_shapes = [(TAIL + 3 * width, width)]
        early_plan = [(0, (), lambda i: i * 0, early_shapes[0][0])]
        late_plan = [(0, (), lambda i: i * 0, late_shapes[0][0])]
        given = jnp.pad(matrix_rows[3 * width :], ((TAIL, 0), (0, 0)))

    out, middle_grad, mixed_grad, gain_two_grad, *early = feed_forward(
        index,
        block_in,
        mixed,
        cotangent.reshape(tokens, width),
        gain_two,
        given,
        block if planes else None,
        FF,
        size,
        early_plan,
        early_shapes,
    )
    standard_flat = standard.reshape(far, width)
    last = [gain_one, gain_two_grad, w_qkv, summary_low, standard_flat, gain_sum]
    if planes:
        (early_kept, early_sent), mixed_grad = together(sum_core(*early), mixed_grad)
        early_in = across_plane(early_sent)
    steps = images * local_rows // math.gcd(local_rows, 4)
    backward = attention_backward(
        (0, steps),
        None,
        index,
        block_in,
        query,
        key,
        value,
        key_far,
        value_far,
        probs,
        mixed_grad,
        last,
        local_rows,
        columns,
        late_plan,
        late_shapes,
    )
    query_grad, key_grad, value_grad, shared, *late = backward
    if planes:
        (late_kept, late_sent), shared, early = together(
            sum_core(*late), shared + swap_core(shared), sum_plane(early_kept, *early_in)
        )
        small = shared[far:]
        late_sent = [with_sums(sent[0], small) for sent in late_sent]
        late_sent[0] = jnp.concatenate([late_sent[0], shared[:far].astype(HALF)])
        late_in = across_plane(late_sent)
        by_mask = [
            jnp.where(z == i, 0.0, lax.dynamic_index_in_dim(early, (z ^ i) - 1, 0, keepdims=False))
            for i in range(4)
        ]
        early_in = swap_near(jnp.stack([by_mask[1], by_mask[3]]).astype(HALF))
        late_in, early_in = together(late_in, early_in)
        rows = late_kept.shape[1]
        both = rows + small.shape[0] + 8
        late = sum_plane(late_kept[0], *[array[:rows] for array in late_in])
        over_x, over_y, over_both = (sums_of(array[rows:both]) for array in late_in)
        shared = shared[:far] + late_in[0][both:].astype(SINGLE)
        small = (small + over_x) + (over_y + over_both)
        early_far = send_far((by_mask[2] + early_in[1].astype(SINGLE)).astype(HALF))
        near_in = swap_near(with_sums(late.astype(HALF), small))
    else:
        for axis, distance, _ in row_hops():
            shared = shared + swap(shared, axis, distance)
        small = shared[far:]
        for axis, distance, _ in image_hops():
            small = small + swap(small, axis, distance)
    input_grad = input_grads(
        block_in, gain_one, query_grad, key_grad, value_grad, w_qkv, middle_grad, local_rows, columns
    )
    if planes:
        near_in, early_far, input_grad = together(near_in, early_far, input_grad)
        late = late + near_in[:rows].astype(SINGLE)
        small = small + sums_of(near_in[rows:])
        late_own = late + send_down(late.astype(HALF)).astype(SINGLE)
        small = small + swap_far(small)
    own_grad = lax.dynamic_slice_in_dim(
        shared[:far].reshape(images, rows_all, width), first_row, local_rows, axis=1
    )
    own_standard = lax.dynamic_slice_in_dim(standard, first_row, local_rows, axis=1)
    mean_grad = summary_inv * (
        own_grad - small[0] / summary_count - own_standard * (small[1] / summary_count)
    )
    input_grad = input_grad.reshape(activations.shape) + (mean_grad / columns)[:, :, None, :]
    if planes:
        early_own = by_mask[0] + early_in[0].astype(SINGLE) + early_far.astype(SINGLE)
        head = jnp.where(
            me == 0,
            jnp.concatenate([jnp.zeros((TAIL - 4, width), SINGLE), small[2:6]]),
            jnp.where(me == 8, small[8:], 0.0),
        )
        mine = jnp.where(z == 0, late_own, early_own)
        mine = jnp.concatenate([mine[:TAIL] + head, mine[TAIL:]])
        weight_grad = lax.dynamic_slice(mine.reshape(-1), (start,), weights.shape)
    else:
        grad_rows = jnp.concatenate([late[0][TAIL:], early[0][TAIL:]]).astype(SINGLE)
        weight_grad = scatter_grads(small[2:6], grad_rows, weights.shape[0])
    return (
        out.reshape(activations.shape),
        input_grad,
        weight_grad,
        summary_mean,
        summary_var,
    )


def solution(mesh):
    placed = (P("img", "row", None, None), P("img", "row", None, None), P(("img", "row")))
    return jax.shard_map(
        per_device,
        mesh=mesh,
        in_specs=placed,
        out_specs=(
            P("img", "row", None, None),
            P("img", "row", None, None),
            P(("img", "row")),
            P(),
            P(),
        ),
        check_vma=False,
    )
```

```python
import functools
import math

import jax
import jax.numpy as jnp
from jax import lax
from jax.experimental import pallas as pl
from jax.experimental.pallas import tpu as pltpu
from jax.sharding import PartitionSpec as P

FF = 2048
HEADS = 8
LANES = 128


EPS = 1e-05
NEGATIVE = -1e30
HALF = jnp.bfloat16
SINGLE = jnp.float32
VMEM_BYTES = 56 * 1024 * 1024

TAIL = 16


def swap(value, axis, distance):
    size = lax.axis_size(axis)
    return lax.ppermute(value, axis, [(i, i ^ distance) for i in range(size)])


def hops():
    rows, images = lax.axis_size("row"), lax.axis_size("img")
    inner = ("row", 1, 1)
    across = ("row", 2, 2)
    along = ("img", 1, rows)
    outer = []
    distance = images // 2
    while distance > 1:
        outer.append(("img", distance, distance * rows))
        distance //= 2
    distance = rows // 2
    while distance > 2:
        outer.append(("row", distance, distance))
        distance //= 2
    return inner, across, along, outer


def piece_order():
    inner, across, along, outer = hops()
    masks = [0]
    for _, _, mask in outer:
        masks = masks + [m ^ mask for m in masks]
    near = (
        masks
        + [m ^ across[2] for m in masks]
        + [m ^ along[2] for m in masks]
        + [m ^ across[2] ^ along[2] for m in masks]
    )
    return near + [m ^ inner[2] for m in near]


def device_index():
    return lax.axis_index("img") * lax.axis_size("row") + lax.axis_index("row")


def gather_pieces(own):
    inner, across, along, outer = hops()
    held = own[None]
    for axis, distance, _ in outer:
        held = jnp.concatenate([held, swap(held, axis, distance)])
    half = held.shape[0] // 2
    held_x = swap(held, across[0], across[1])
    held_y = swap(held, along[0], along[1])
    corner_first = swap(held_x[:half], along[0], along[1])
    corner_second = swap(held_y[half:], across[0], across[1])
    near = [held, held_x, held_y, corner_first, corner_second]
    far = [swap(part, inner[0], inner[1]) for part in near]
    return jnp.concatenate(near + far)


def scatter_pieces(pieces):
    inner, across, along, outer = hops()

    def add(kept, sent, axis, distance):
        return kept + swap(sent.astype(HALF), axis, distance).astype(SINGLE)

    count = pieces.shape[0] // 2
    near = add(pieces[:count], pieces[count:], inner[0], inner[1])
    quarter = count // 4
    half = quarter // 2
    held, held_x, held_y, corner = (near[i * quarter : (i + 1) * quarter] for i in range(4))
    first = add(
        jnp.concatenate([held[:half], held_x[:half]]),
        jnp.concatenate([held_y[:half], corner[:half]]),
        along[0],
        along[1],
    )
    second = add(
        jnp.concatenate([held[half:], held_y[half:]]),
        jnp.concatenate([held_x[half:], corner[half:]]),
        across[0],
        across[1],
    )
    first = add(first[:half], first[half:], across[0], across[1])
    second = add(second[:half], second[half:], along[0], along[1])
    held = jnp.concatenate([first, second])
    for axis, distance, _ in reversed(outer):
        half = held.shape[0] // 2
        held = add(held[:half], held[half:], axis, distance)
    return held[0]


def row_hops():
    inner, across, _, outer = hops()
    return [inner, across] + [hop for hop in outer if hop[0] == "row"]


def image_hops():
    _, _, along, outer = hops()
    return [along] + [hop for hop in outer if hop[0] == "img"]


def gather_rows(own):
    held, masks = own[None], [0]
    for axis, distance, mask in row_hops():
        held = jnp.concatenate([held, swap(held, axis, distance)])
        masks = masks + [m ^ mask for m in masks]
    place = [0] * len(masks)
    for at, mask in enumerate(masks):
        place[mask] = at
    order = jnp.asarray(place, jnp.int32)[jnp.arange(len(masks)) ^ lax.axis_index("row")]
    held = jnp.moveaxis(jnp.take(held, order, axis=0, mode="clip"), 0, 1)
    return held.reshape(own.shape[0], -1, own.shape[-1])


def gather_weights(weights, model_width):
    length = weights.shape[0]
    me = device_index()
    devices = lax.axis_size("img") * lax.axis_size("row")
    block = length // model_width
    rest = length % model_width
    start = TAIL * model_width + rest * me - 4 * model_width
    own = lax.dynamic_update_slice(jnp.zeros(((block + TAIL) * model_width,), HALF), weights, (start,))
    own = own.reshape(block + TAIL, model_width)
    pieces = gather_pieces(own)
    place = [0] * devices
    for at, mask in enumerate(piece_order()):
        place[mask] = at
    order = jnp.asarray(place, jnp.int32)[jnp.arange(devices) ^ me]
    pieces = jnp.take(pieces, order, axis=0, mode="clip")
    tails = jnp.concatenate([pieces[1:, :TAIL], jnp.zeros((1, TAIL, model_width), HALF)])
    body = jnp.concatenate([pieces[:, TAIL:block], pieces[:, block:] + tails], axis=1)
    return pieces[0, TAIL - 4 : TAIL], body.reshape(devices * block, model_width)


def scatter_grads(vectors, rows, length):
    model_width = rows.shape[1]
    me = device_index()
    devices = lax.axis_size("img") * lax.axis_size("row")
    block = length // model_width
    rest = length % model_width
    whole = jnp.concatenate([jnp.zeros((TAIL - 4, model_width), SINGLE), vectors, rows])
    place = jnp.asarray(piece_order(), jnp.int32)
    pieces = jnp.stack([whole[block * s : block * s + block + TAIL] for s in range(devices)])
    pieces = jnp.take(pieces, place ^ me, axis=0, mode="clip")
    mine = scatter_pieces(pieces)
    start = TAIL * model_width + rest * me - 4 * model_width
    return lax.dynamic_slice(mine.reshape(-1), (start,), (length,))


def dot(left, right):
    return jnp.dot(left, right, preferred_element_type=SINGLE)


def dot_rows(left, right):
    return lax.dot_general(left, right, (((1,), (1,)), ((), ())), preferred_element_type=SINGLE)


def dot_outer(left, right):
    return lax.dot_general(left, right, (((0,), (0,)), ((), ())), preferred_element_type=SINGLE)


def normalize(values):
    centred = values - jnp.mean(values, axis=-1, keepdims=True)
    inverse = lax.rsqrt(jnp.mean(centred * centred, axis=-1, keepdims=True) + EPS)
    return (centred * inverse, inverse)


def norm_back(grad_norm, normed, inverse):
    return inverse * (
        grad_norm
        - jnp.mean(grad_norm, axis=-1, keepdims=True)
        - normed * jnp.mean(grad_norm * normed, axis=-1, keepdims=True)
    )


def whole_block(shape):
    return pl.BlockSpec(shape, lambda *_: (0,) * len(shape), pipeline_mode=pl.Buffered(1))


def head_keys(rows_per_step, model_width):
    return [
        (row, pair, half)
        for row in range(rows_per_step)
        for pair in range(model_width // LANES)
        for half in range(2)
    ]


def attention_forward_kernel(
    scaling,
    rows_per_step,
    local_rows,
    first_row_ref,
    block_ref,
    gain_ref,
    w_ref,
    key_far_ref,
    value_far_ref,
    query_ref,
    key_ref,
    value_ref,
    mixed_ref,
    probs_ref,
):
    columns = block_ref.shape[0] // rows_per_step
    far = key_far_ref.shape[0]
    width = block_ref.shape[1]
    head_width = width // HEADS
    step = pl.program_id(0)
    normed, _ = normalize(block_ref[...].astype(SINGLE))
    attn_in = (normed * gain_ref[...]).astype(HALF)
    for i, ref in enumerate((query_ref, key_ref, value_ref)):
        ref[...] = dot(attn_in, w_ref[:, i * width : (i + 1) * width]).astype(HALF)
    first_half = lax.broadcasted_iota(jnp.int32, (columns + far, LANES), 1) < head_width
    far_index = lax.broadcasted_iota(jnp.int32, (far, columns), 0)
    key_index = lax.broadcasted_iota(jnp.int32, (columns, columns), 0)
    query_index = lax.broadcasted_iota(jnp.int32, (columns, columns), 1)
    causal = jnp.where(key_index <= query_index, 0.0, NEGATIVE)
    keys = head_keys(rows_per_step, width)
    for start in range(0, len(keys), 4 * HEADS):
        group = keys[start : start + 4 * HEADS]
        scores, low, mixed = {}, {}, {}
        for row, pair, half in group:
            global_row = first_row_ref[0] + lax.rem(step * rows_per_step + row, local_rows)
            far_bias = jnp.where(far_index < global_row, 0.0, NEGATIVE)
            tokens = slice(row * columns, (row + 1) * columns)
            lanes = slice(pair * LANES, (pair + 1) * LANES)
            all_keys = jnp.concatenate([key_ref[tokens, lanes], key_far_ref[:, lanes]], axis=0)
            one_head = jnp.where(
                first_half if half == 0 else ~first_half, all_keys, jnp.zeros_like(all_keys)
            )
            found = dot_rows(one_head, query_ref[tokens, lanes])
            scores[row, pair, half] = jnp.concatenate(
                [found[:columns] + causal, found[columns:] + far_bias], axis=0
            )
        for row, pair, half in group:
            found = scores.pop((row, pair, half))
            top = jnp.max(found, axis=0, keepdims=True)
            powers = jnp.exp2((found - top) * (scaling * math.log2(math.e)))
            inverse = 1.0 / jnp.sum(powers, axis=0, keepdims=True)
            low[row, pair, half] = (powers * inverse).astype(HALF)
            probs_ref[row, 2 * pair + half] = low[row, pair, half]
        for row, pair, half in group:
            tokens = slice(row * columns, (row + 1) * columns)
            lanes = slice(pair * LANES, (pair + 1) * LANES)
            all_values = jnp.concatenate([value_ref[tokens, lanes], value_far_ref[:, lanes]], axis=0)
            turned = all_values.T[half * head_width : (half + 1) * head_width]
            mixed[row, pair, half] = dot(turned, low[row, pair, half])
        for row, pair, half in group:
            if half == 0:
                tokens = slice(row * columns, (row + 1) * columns)
                lanes = slice(pair * LANES, (pair + 1) * LANES)
                both = jnp.concatenate([mixed[row, pair, 0], mixed[row, pair, 1]], axis=0)
                mixed_ref[tokens, lanes] = both.T.astype(HALF)


def image_groups(images):
    return [(0, 1), (1, images - 1)] if images > 1 else [(0, images)]


def step_groups(steps):
    if steps < 4:
        return [(0, steps)]
    first, last = steps // 3, max(1, steps // 6)
    return [(0, first), (first, steps - first - last), (steps - last, last)]


def kept_arrays(previous, start):
    if previous is None:
        return ([], [], {})
    specs = [pl.BlockSpec(memory_space=pl.ANY)] * len(previous)
    return (list(previous), specs, {start + i: i for i in range(len(previous))})


def attention_forward(
    group, previous, block_in, gain, w_qkv, key_far, value_far, first_row, local_rows, columns
):
    tokens, width = block_in.shape
    images, far, _ = key_far.shape
    first_image, count = group
    rows_per_step = math.gcd(local_rows, 4)
    steps = local_rows // rows_per_step
    first_step = first_image * steps
    size = rows_per_step * columns
    block = pl.BlockSpec((size, width), lambda i, _: (first_step + i, 0))
    far_block = pl.BlockSpec((None, far, width), lambda i, _: (first_image + i // steps, 0, 0))
    probs_block = pl.BlockSpec(
        (rows_per_step, HEADS, columns + far, columns), lambda i, _: (first_step + i, 0, 0, 0)
    )
    inputs = [block_in, gain, w_qkv, key_far, value_far]
    kept, kept_specs, aliases = kept_arrays(previous, 1 + len(inputs))
    low = jax.ShapeDtypeStruct((tokens, width), HALF)
    part = count * tokens // images
    kernel = functools.partial(
        attention_forward_kernel, 1.0 / math.sqrt(width // HEADS), rows_per_step, local_rows
    )

    def body(*refs):
        kernel(*refs[: 1 + len(inputs)], *refs[1 + len(inputs) + len(kept) :])

    return pl.pallas_call(
        body,
        grid_spec=pltpu.PrefetchScalarGridSpec(
            num_scalar_prefetch=1,
            grid=(count * steps,),
            in_specs=[
                block,
                whole_block((1, width)),
                whole_block((width, 3 * width)),
                far_block,
                far_block,
            ]
            + kept_specs,
            out_specs=[block] * 4 + [probs_block],
        ),
        out_shape=[low] * 4
        + [jax.ShapeDtypeStruct((images * local_rows, HEADS, columns + far, columns), HALF)],
        input_output_aliases=aliases,
        compiler_params=pltpu.CompilerParams(vmem_limit_bytes=VMEM_BYTES),
        cost_estimate=pl.CostEstimate(
            flops=part * width * (6 * width + 8 * (columns + far)),
            bytes_accessed=part * width * 12 + part * HEADS * (columns + far) * 2,
            transcendentals=part * HEADS * (columns + far),
        ),
        name="attention_forward",
    )(first_row, *inputs, *kept)


GELU_OUTER = math.sqrt(2.0 / math.pi)
GELU_CUBE = 0.044715


def gelu_and_slope(value):
    square = value * value
    gate = 0.5 * jnp.tanh(value * (GELU_OUTER * GELU_CUBE * square + GELU_OUTER)) + 0.5
    activated = value * gate
    slope = gate + activated * (1.0 - gate) * (6.0 * GELU_OUTER * GELU_CUBE * square + 2.0 * GELU_OUTER)
    return (activated, slope)


def start_pieces(plan, flat_ref, outs, sems, index):
    copies = []
    for i, (out, place, offset, rows) in enumerate(plan):
        source = flat_ref.at[pl.ds(pl.multiple_of(offset(index), TAIL), rows)]
        target = outs[out].at[place] if place else outs[out]
        copies.append(pltpu.make_async_copy(source, target, sems.at[i]))
    for copy in copies:
        copy.start()
    return copies


def feed_forward_kernel(
    chunk,
    plan,
    masks,
    block,
    index_ref,
    block_ref,
    mixed_ref,
    cotangent_ref,
    gain_ref,
    *rest,
):
    given, rest = rest[: max(1, 3 * len(masks))], rest[max(1, 3 * len(masks)) :]
    out_ref, middle_grad_ref, mixed_grad_ref, grad_gain_ref, *rest = rest
    *pieces, grad_out_ref, grad_inner_ref, grad_outer_ref, w_inner_ref, flat_ref, sems = rest
    width, hidden = w_inner_ref.shape
    groups = hidden // width
    per = 256 // groups
    inner_start = TAIL + width
    outer_start = inner_start + hidden
    w_out_ref = flat_ref.at[TAIL:inner_start]
    w_outer_ref = flat_ref.at[outer_start:]

    @pl.when(pl.program_id(0) == 0)
    def _():
        for ref in (grad_out_ref, grad_inner_ref, grad_outer_ref, grad_gain_ref):
            ref[...] = jnp.zeros_like(ref)
        if block is None:
            flat_ref[...] = given[0][...]
        else:
            plane = 8 * block
            here, z = lax.rem(index_ref[0], 8), lax.div(index_ref[0], 8)
            own, first, last = (
                list(zip(given[i * len(masks) : (i + 1) * len(masks)], masks)) for i in range(3)
            )
            clear_seams(flat_ref, block, 3)

            @pl.when(z == 0)
            def _():
                assemble(flat_ref, first, here, block, 0)

            @pl.when(z > 0)
            def _():
                assemble(flat_ref, own, here, block, (z - 1) * plane)

            for i, slot in enumerate(second_slots(z)):
                pieces_here = [(ref.at[i], mask) for ref, mask in last]
                assemble(flat_ref, pieces_here, here, block, (slot - 1) * plane)
        mix = weave(groups, per)
        for c in range(width // per):
            start = inner_start + c * groups * per
            parted = dot_outer(mix, flat_ref[start : start + groups * per]).astype(HALF)
            for g in range(groups):
                w_inner_ref[c * per : (c + 1) * per, g * width : (g + 1) * width] = parted[
                    g * per : (g + 1) * per
                ]

    mixed = mixed_ref[...]
    cotangent = cotangent_ref[...]
    middle = block_ref[...].astype(SINGLE) + dot(mixed, w_out_ref[...])
    normed, inverse = normalize(middle)
    ff_in = (normed * gain_ref[...]).astype(HALF)
    out = middle
    ff_grad = jnp.zeros_like(middle)
    cotangent_turned = cotangent.T
    ff_turned = ff_in.T
    count = hidden // chunk
    spans = [slice(j * chunk, (j + 1) * chunk) for j in range(count)]

    def products(j):
        return (dot(ff_in, w_inner_ref[:, spans[j]]), dot_rows(cotangent, w_outer_ref[spans[j], :]))

    ready = products(0)
    for j in range(count):
        inner, act_grad = ready
        if j + 1 < count:
            ready = products(j + 1)
        activated, slope = gelu_and_slope(inner)
        activated = activated.astype(HALF)
        inner_grad = (slope * act_grad).astype(HALF)
        out = out + dot(activated, w_outer_ref[spans[j], :])
        ff_grad = ff_grad + dot_rows(inner_grad, w_inner_ref[:, spans[j]])
        grad_inner_ref[:, spans[j]] += dot(ff_turned, inner_grad)
        grad_outer_ref[:, spans[j]] += dot(cotangent_turned, activated)
    out_ref[...] = out.astype(HALF)
    grad_gain_ref[...] += jnp.sum(ff_grad * normed, axis=0, keepdims=True)
    middle_grad = cotangent.astype(SINGLE) + norm_back(ff_grad * gain_ref[...], normed, inverse)
    middle_grad_ref[...] = middle_grad
    branch_grad = middle_grad.astype(HALF)
    mixed_grad_ref[...] = dot_rows(branch_grad, w_out_ref[...]).astype(HALF)
    grad_out_ref[...] += dot_outer(mixed, branch_grad)

    @pl.when(pl.program_id(0) == pl.num_programs(0) - 1)
    def _():
        flat_ref[:TAIL] = jnp.zeros((TAIL, width), HALF)
        flat_ref[TAIL : TAIL + width] = grad_out_ref[...].astype(HALF)
        mix = weave(groups, per)
        for c in range(width // per):
            parts = [
                grad_inner_ref[c * per : (c + 1) * per, g * width : (g + 1) * width].astype(HALF)
                for g in range(groups)
            ]
            start = TAIL + width + c * groups * per
            woven = dot(mix, jnp.concatenate(parts, axis=0))
            flat_ref[start : start + groups * per] = woven.astype(HALF)
        start = TAIL + width + hidden
        for j in range(hidden // width):
            turned = grad_outer_ref[:, j * width : (j + 1) * width].astype(HALF).T
            flat_ref[start + j * width : start + (j + 1) * width] = turned
        for copy in start_pieces(plan, flat_ref, pieces, sems, index_ref[0]):
            copy.wait()


def weave(groups, per):
    size = groups * per
    row = lax.broadcasted_iota(jnp.int32, (size, size), 0)
    column = lax.broadcasted_iota(jnp.int32, (size, size), 1)
    wanted = lax.rem(row, groups) * per + lax.div(row, groups)
    return (wanted == column).astype(SINGLE).astype(HALF)


def piece_outputs(shapes):
    return (
        [pl.BlockSpec(memory_space=pl.ANY)] * len(shapes),
        [jax.ShapeDtypeStruct(shape, HALF) for shape in shapes],
    )


def feed_forward(index, block_in, mixed, cotangent, gain, given, block, hidden, size, plan, shapes):
    tokens, width = block_in.shape
    tile = pl.BlockSpec((size, width), lambda i, _: (i, 0))
    piece_specs, piece_shapes = piece_outputs(shapes)
    masks = [] if block is None else [mask for _, mask in given[: len(given) // 3]]
    arrays = [given] if block is None else [array for array, _ in given]
    return pl.pallas_call(
        functools.partial(feed_forward_kernel, 256, plan, masks, block),
        grid_spec=pltpu.PrefetchScalarGridSpec(
            num_scalar_prefetch=1,
            grid=(tokens // size,),
            in_specs=[tile, tile, tile, whole_block((1, width))] + vmem_specs(len(arrays)),
            out_specs=[tile, tile, tile, whole_block((1, width))] + piece_specs,
            scratch_shapes=[
                pltpu.VMEM((width, width), SINGLE),
                pltpu.VMEM((width, hidden), SINGLE),
                pltpu.VMEM((width, hidden), SINGLE),
                pltpu.VMEM((width, hidden), HALF),
                pltpu.VMEM((TAIL + width + 2 * hidden, width), HALF),
                pltpu.SemaphoreType.DMA((len(plan),)),
            ],
        ),
        out_shape=[
            jax.ShapeDtypeStruct((tokens, width), HALF),
            jax.ShapeDtypeStruct((tokens, width), SINGLE),
            jax.ShapeDtypeStruct((tokens, width), HALF),
            jax.ShapeDtypeStruct((1, width), SINGLE),
        ]
        + piece_shapes,
        compiler_params=pltpu.CompilerParams(vmem_limit_bytes=VMEM_BYTES),
        cost_estimate=pl.CostEstimate(
            flops=tokens * width * (6 * width + 12 * hidden),
            bytes_accessed=tokens * width * 14 + width * hidden * 8,
            transcendentals=tokens * hidden,
        ),
        name="feed_forward",
    )(index, block_in, mixed, cotangent, gain, *arrays)


def attention_backward_kernel(
    scaling,
    rows_per_step,
    per_image,
    first_step,
    plan,
    ends,
    index_ref,
    block_ref,
    query_ref,
    key_ref,
    value_ref,
    key_far_ref,
    value_far_ref,
    probs_ref,
    mixed_grad_ref,
    *rest,
):
    rest = list(rest)
    earlier = None
    if first_step > 0:
        earlier, rest = rest[:3], rest[6:]
    if ends:
        fixed, rest = rest[:6], rest[6:]
    query_grad_ref, key_grad_ref, value_grad_ref, *rest = rest
    if ends:
        shared_ref, *rest = rest
        small_ref = shared_ref.at[shared_ref.shape[0] - 8 - TAIL :]
        *pieces, total_ref, key_far_grad_ref, value_far_grad_ref, flat_ref, sems = rest
    else:
        total_ref, key_far_grad_ref, value_far_grad_ref = rest
    width = query_ref.shape[1]
    head_width = width // HEADS
    far = key_far_ref.shape[0]
    columns = query_ref.shape[0] // rows_per_step
    image = lax.div(first_step + pl.program_id(0), per_image)

    @pl.when(pl.program_id(0) == 0)
    def _():
        for i, ref in enumerate((total_ref, key_far_grad_ref, value_far_grad_ref)):
            ref[...] = jnp.zeros_like(ref) if earlier is None else earlier[i][...]

    first_half = lax.broadcasted_iota(jnp.int32, (columns + far, LANES), 1) < head_width
    keys = head_keys(rows_per_step, width)
    for start in range(0, len(keys), 2 * HEADS):
        group = keys[start : start + 2 * HEADS]
        prob_grad, score_grad, value_grad, key_grad, query_grad = {}, {}, {}, {}, {}
        for row, pair, half in group:
            tokens = slice(row * columns, (row + 1) * columns)
            lanes = slice(pair * LANES, (pair + 1) * LANES)
            all_values = jnp.concatenate([value_ref[tokens, lanes], value_far_ref[:, lanes]], axis=0)
            one_head = jnp.where(
                first_half if half == 0 else ~first_half, all_values, jnp.zeros_like(all_values)
            )
            prob_grad[row, pair, half] = dot_rows(one_head, mixed_grad_ref[tokens, lanes])
        for row, pair, half in group:
            tokens = slice(row * columns, (row + 1) * columns)
            lanes = slice(pair * LANES, (pair + 1) * LANES)
            value_grad[row, pair, half] = dot(
                probs_ref[row, 2 * pair + half], mixed_grad_ref[tokens, lanes]
            )
        for row, pair, half in group:
            probs = probs_ref[row, 2 * pair + half].astype(SINGLE)
            grad = prob_grad.pop((row, pair, half))
            total = jnp.sum(probs * grad, axis=0, keepdims=True)
            score_grad[row, pair, half] = (probs * (grad - total)).astype(HALF)
        for row, pair, half in group:
            tokens = slice(row * columns, (row + 1) * columns)
            lanes = slice(pair * LANES, (pair + 1) * LANES)
            key_grad[row, pair, half] = dot(score_grad[row, pair, half], query_ref[tokens, lanes])
            all_keys = jnp.concatenate([key_ref[tokens, lanes], key_far_ref[:, lanes]], axis=0)
            turned = all_keys.T[half * head_width : (half + 1) * head_width]
            query_grad[row, pair, half] = dot(turned, score_grad[row, pair, half])
        for row, pair, half in group:
            if half == 0:
                tokens = slice(row * columns, (row + 1) * columns)
                lanes = slice(pair * LANES, (pair + 1) * LANES)
                first, second = (row, pair, 0), (row, pair, 1)
                value_both = jnp.where(first_half, value_grad[first], value_grad[second])
                key_both = jnp.where(first_half, key_grad[first], key_grad[second]) * scaling
                value_grad_ref[tokens, lanes] = value_both[:columns].astype(HALF)
                key_grad_ref[tokens, lanes] = key_both[:columns].astype(HALF)
                value_far_grad_ref[image, :, lanes] += value_both[columns:]
                key_far_grad_ref[image, :, lanes] += key_both[columns:]
                query_both = jnp.concatenate([query_grad[first], query_grad[second]], axis=0) * scaling
                query_grad_ref[tokens, lanes] = query_both.T.astype(HALF)
    normed, _ = normalize(block_ref[...].astype(SINGLE))
    turned = normed.astype(HALF).T
    for i, ref in enumerate((query_grad_ref, key_grad_ref, value_grad_ref)):
        total_ref[:, i * width : (i + 1) * width] += dot(turned, ref[...])
    if not ends:
        return

    @pl.when(pl.program_id(0) == pl.num_programs(0) - 1)
    def _():
        gain_ref, gain_two_grad_ref, w_ref, summary_ref, standard_ref, gain_sum_ref = fixed

        key_low = key_far_grad_ref[...].reshape(-1, width).astype(HALF)
        value_low = value_far_grad_ref[...].reshape(-1, width).astype(HALF)
        gain = jnp.broadcast_to(gain_ref[...], (8, width)).T[:, :1]
        matched = jnp.zeros((width, width), SINGLE)
        flat_ref[:TAIL] = jnp.zeros((TAIL, width), HALF)
        for i in range(3):
            total = total_ref[:, i * width : (i + 1) * width]
            matched = matched + total * w_ref[:, i * width : (i + 1) * width].astype(SINGLE)
            grad = total * gain
            if i > 0:
                grad = grad + dot_outer(summary_ref[...], key_low if i == 1 else value_low)
            flat_ref[TAIL + i * width : TAIL + (i + 1) * width] = grad.astype(HALF)
            if i == 2:
                small_ref[8:] = grad[width - TAIL :]
        copies = start_pieces(plan, flat_ref, pieces, sems, index_ref[0])
        summary_grad = dot_rows(key_low, w_ref[:, width : 2 * width]) + dot_rows(
            value_low, w_ref[:, 2 * width :]
        )
        standard = standard_ref[...]
        standard_grad = summary_grad * gain_sum_ref[...]
        shared_ref[: standard.shape[0]] = standard_grad

        def fold(value):
            return jnp.sum(value, axis=0, keepdims=True)

        small_ref[0:1] = fold(standard_grad)
        small_ref[1:2] = fold(standard_grad * standard)
        small_ref[2:3] = fold(matched.T)
        small_ref[3:4] = fold(summary_grad * standard)
        small_ref[4:5] = fold(summary_grad)
        small_ref[5:6] = gain_two_grad_ref[...]
        small_ref[6:8] = jnp.zeros((2, width), SINGLE)
        for copy in copies:
            copy.wait()


def attention_backward(
    group,
    previous,
    index,
    block_in,
    query,
    key,
    value,
    key_far,
    value_far,
    probs,
    mixed_grad,
    last,
    local_rows,
    columns,
    plan,
    shapes,
):
    tokens, width = query.shape
    images, far, _ = key_far.shape
    first_step, count = group
    rows_per_step = math.gcd(local_rows, 4)
    per_image = local_rows // rows_per_step
    ends = first_step + count == images * per_image
    size = rows_per_step * columns
    part = count * size
    block = pl.BlockSpec((size, width), lambda i, _: (first_step + i, 0))
    far_block = pl.BlockSpec((None, far, width), lambda i, _: ((first_step + i) // per_image, 0, 0))
    probs_block = pl.BlockSpec(
        (rows_per_step, HEADS, columns + far, columns), lambda i, _: (first_step + i, 0, 0, 0)
    )
    inputs = [block_in, query, key, value, key_far, value_far, probs, mixed_grad]
    in_specs = [block] * 4 + [far_block] * 2 + [probs_block, block]
    aliases = {}
    total_shape = (width, 3 * width)
    far_shape = (images, far, width)
    if previous is not None:
        sums = list(previous[3:])
        inputs = inputs + sums
        in_specs = in_specs + [whole_block(array.shape) for array in sums]
        kept, kept_specs, aliases = kept_arrays(previous[:3], 1 + len(inputs))
        inputs, in_specs = inputs + kept, in_specs + kept_specs
    out_specs = [block] * 3
    out_shape = [jax.ShapeDtypeStruct((tokens, width), HALF)] * 3
    scratch = []
    if ends:
        inputs = inputs + list(last)
        in_specs = in_specs + [whole_block(array.shape) for array in last]
        piece_specs, piece_shapes = piece_outputs(shapes)
        summaries = images * far
        shared_shape = (summaries + 8 + TAIL, width)
        out_specs += [whole_block(shared_shape)] + piece_specs
        out_shape += [jax.ShapeDtypeStruct(shared_shape, SINGLE)] + piece_shapes
        scratch = [
            pltpu.VMEM(total_shape, SINGLE),
            pltpu.VMEM(far_shape, SINGLE),
            pltpu.VMEM(far_shape, SINGLE),
            pltpu.VMEM((TAIL + 3 * width, width), HALF),
            pltpu.SemaphoreType.DMA((len(plan),)),
        ]
    else:
        out_specs += [whole_block(total_shape), whole_block(far_shape), whole_block(far_shape)]
        out_shape += [
            jax.ShapeDtypeStruct(total_shape, SINGLE),
            jax.ShapeDtypeStruct(far_shape, SINGLE),
            jax.ShapeDtypeStruct(far_shape, SINGLE),
        ]
    return pl.pallas_call(
        functools.partial(
            attention_backward_kernel,
            1.0 / math.sqrt(width // HEADS),
            rows_per_step,
            per_image,
            first_step,
            plan,
            ends,
        ),
        grid_spec=pltpu.PrefetchScalarGridSpec(
            num_scalar_prefetch=1,
            grid=(count,),
            in_specs=in_specs,
            out_specs=out_specs,
            scratch_shapes=scratch,
        ),
        out_shape=out_shape,
        input_output_aliases=aliases,
        compiler_params=pltpu.CompilerParams(vmem_limit_bytes=VMEM_BYTES),
        cost_estimate=pl.CostEstimate(
            flops=part * width * (6 * width + 16 * (columns + far)),
            bytes_accessed=part * width * 16 + part * HEADS * (columns + far) * 2,
            transcendentals=0,
        ),
        name="attention_backward",
    )(index, *inputs)


def input_grad_kernel(
    block_ref,
    gain_ref,
    query_grad_ref,
    key_grad_ref,
    value_grad_ref,
    w_ref,
    middle_grad_ref,
    out_ref,
):
    width = block_ref.shape[1]
    attn_grad = (
        dot_rows(query_grad_ref[...], w_ref[:, :width])
        + dot_rows(key_grad_ref[...], w_ref[:, width : 2 * width])
        + dot_rows(value_grad_ref[...], w_ref[:, 2 * width :])
    )
    normed, inverse = normalize(block_ref[...].astype(SINGLE))
    out_ref[...] = middle_grad_ref[...] + norm_back(attn_grad * gain_ref[...], normed, inverse)


def input_grads(
    block_in, gain, query_grad, key_grad, value_grad, w_qkv, middle_grad, local_rows, columns
):
    tokens, width = block_in.shape
    size = math.gcd(local_rows, 2) * columns
    block = pl.BlockSpec((size, width), lambda i: (i, 0))
    return pl.pallas_call(
        input_grad_kernel,
        grid=(tokens // size,),
        in_specs=[block, whole_block((1, width))]
        + [block] * 3
        + [whole_block((width, 3 * width)), block],
        out_specs=block,
        out_shape=jax.ShapeDtypeStruct((tokens, width), SINGLE),
        compiler_params=pltpu.CompilerParams(vmem_limit_bytes=VMEM_BYTES),
        cost_estimate=pl.CostEstimate(
            flops=tokens * width * 6 * width, bytes_accessed=tokens * width * 16, transcendentals=0
        ),
        name="input_grads",
    )(block_in, gain, query_grad, key_grad, value_grad, w_qkv, middle_grad)


def clear_seams(flat_ref, block, count):
    for at in range(0, count * 8 * block + 1, block):
        flat_ref[at : at + TAIL] = jnp.zeros((TAIL, flat_ref.shape[1]), HALF)


def assemble(flat_ref, pieces, index, block, base):
    for ref, mask in pieces:
        spot = pl.multiple_of(base + (index ^ mask) * block, TAIL)
        for low, high in ((0, TAIL), (TAIL, block), (block, block + TAIL)):
            rows = pl.ds(spot + low, high - low)
            value = ref[low:high]
            if low != TAIL:
                value = flat_ref[rows] + value
            flat_ref[rows] = value


def second_slots(z):
    return [jnp.where(z < 2, 2, 1), jnp.where(z < 3, 3, 2)]


def parts_of(value):
    high = lax.reduce_precision(value, 8, 7)
    middle = lax.reduce_precision(value - high, 8, 7)
    low = value - high - middle
    return [part.astype(HALF) for part in (high, middle, low)]


def whole_of(parts):
    rows = parts.shape[0] // 3
    parts = parts.astype(SINGLE)
    return (parts[:rows] + parts[rows : 2 * rows]) + parts[2 * rows :]


def projection_weights_kernel(
    masks,
    block,
    images,
    local_rows,
    summary_count,
    index_ref,
    *refs,
):
    count = len(masks)
    own_refs, piece_refs, refs = refs[:count], refs[count : 2 * count], refs[2 * count :]
    w_ref, key_far_ref, value_far_ref, standard_ref, summary_ref, *refs = refs
    *stat_refs, flat_ref, shown_ref, means_ref = refs
    width = flat_ref.shape[1]
    rows = block + TAIL
    here = lax.rem(index_ref[0], 8)
    clear_seams(flat_ref, block, 1)

    @pl.when(index_ref[0] < 8)
    def _():
        assemble(flat_ref, list(zip(own_refs, masks)), here, block, 0)

    @pl.when(index_ref[0] >= 8)
    def _():
        assemble(flat_ref, list(zip(piece_refs, masks)), here, block, 0)

    for own_ref, ref, mask in zip(own_refs, piece_refs, masks):
        shown_ref[here ^ mask, : 2 * TAIL] = ref[rows:]
        shown_ref[here ^ mask, 2 * TAIL :] = own_ref[rows:]
    flat_ref[3 * width :] += shown_ref[0, :TAIL]
    for i in range(3):
        w_ref[:, i * width : (i + 1) * width] = flat_ref[TAIL + i * width : TAIL + (i + 1) * width]
    total = jnp.zeros((2, width), SINGLE)
    for j in range(8):
        total = total + whole_of(shown_ref[j, TAIL : 2 * TAIL].astype(SINGLE)[:6])
    for j in range(4):
        means = whole_of(shown_ref[lax.div(here, 4) * 4 + j, 2 * TAIL :])
        for image in range(images):
            start = (image * 4 + j) * local_rows
            means_ref[start : start + local_rows] = means[image * local_rows : (image + 1) * local_rows]
    vectors = flat_ref[:TAIL].astype(SINGLE)[TAIL - 4 :]
    mean = total[:1] / summary_count
    variance = total[1:] / summary_count - mean * mean
    inverse = lax.rsqrt(variance + EPS)
    standard = (means_ref[...] - mean) * inverse
    summary = (standard * vectors[1:2] + vectors[2:3]).astype(HALF)
    standard_ref[...] = standard
    summary_ref[...] = summary
    vector_rows = [vectors[i : i + 1] for i in range(4)]
    for ref, value in zip(stat_refs, [mean, variance, inverse] + vector_rows):
        ref[...] = value
    key_far_ref[...] = dot(summary, w_ref[:, width : 2 * width]).astype(HALF)
    value_far_ref[...] = dot(summary, w_ref[:, 2 * width :]).astype(HALF)


def vmem_specs(count):
    return [pl.BlockSpec(memory_space=pltpu.VMEM)] * count


def projection_weights(index, own_pieces, pieces, block, images, local_rows, summary_count):
    arrays, masks = [p[0] for p in own_pieces + pieces], [p[1] for p in pieces]
    width = arrays[0].shape[1]
    far = 4 * images * local_rows
    return pl.pallas_call(
        functools.partial(
            projection_weights_kernel, masks, block, images, local_rows, summary_count
        ),
        in_specs=[pl.BlockSpec(memory_space=pltpu.SMEM)] + vmem_specs(len(arrays)),
        out_specs=vmem_specs(12),
        out_shape=[
            jax.ShapeDtypeStruct((width, 3 * width), HALF),
            jax.ShapeDtypeStruct((far, width), HALF),
            jax.ShapeDtypeStruct((far, width), HALF),
            jax.ShapeDtypeStruct((far, width), SINGLE),
            jax.ShapeDtypeStruct((far, width), HALF),
        ]
        + [jax.ShapeDtypeStruct((1, width), SINGLE)] * 7,
        scratch_shapes=[
            pltpu.VMEM((TAIL + 3 * width, width), HALF),
            pltpu.VMEM((8, 5 * TAIL, width), HALF),
            pltpu.VMEM((far, width), SINGLE),
        ],
        compiler_params=pltpu.CompilerParams(vmem_limit_bytes=VMEM_BYTES),
        name="projection_weights",
    )(index, *arrays)


def with_sums(value, small):
    high = lax.reduce_precision(small[:8], 8, 7)
    return jnp.concatenate(
        [value, high.astype(HALF), (small[:8] - high).astype(HALF), small[8:].astype(HALF)]
    )


def sums_of(rows):
    rows = rows.astype(SINGLE)
    return jnp.concatenate([rows[:8] + rows[8:16], rows[16:]])


def swap_core(value):
    return swap(value, "row", 1)


def swap_x(value):
    return swap(value, "row", 2)


def swap_y(value):
    return swap(value, "img", 1)


def swap_both(value):
    size = lax.axis_size("img") * lax.axis_size("row")
    return lax.ppermute(value, ("img", "row"), [(i, i ^ 6) for i in range(size)])


def swap_near(value):
    return swap(value, "img", 2)


def swap_far(value):
    return swap(value, "img", 4)


def send_far(value):
    return lax.ppermute(value, "img", [(i, i ^ 4) for i in range(lax.axis_size("img")) if i // 2 != 2])


def piece_plan(block, slots):
    plan, shapes = [], []
    rows = block + TAIL
    for out, (side, masks) in enumerate(((0, (0,)), (0, (2,)), (0, (4,)), (0, (6,)), (1, (0, 2, 4, 6)))):
        shapes.append((len(masks), slots, rows))
        for place, mask in enumerate(masks):
            for slot in range(slots):

                def offset(index, mask=mask | side, slot=slot):
                    return (slot * 8 + (lax.rem(index, 8) ^ mask)) * block

                plan.append((out, (place, slot), offset, rows))
    return plan, shapes


def sum_core(kept, over_x, over_y, over_both, other):
    other = swap_core(other)
    own = kept[0].astype(SINGLE) + other[0].astype(SINGLE)
    sent = [
        (piece[0].astype(SINGLE) + other[i + 1].astype(SINGLE)).astype(HALF)
        for i, piece in enumerate((over_x, over_y, over_both))
    ]
    return (own, sent)


def send_down(value):
    return lax.ppermute(value, "img", [(i, i ^ 4) for i in range(lax.axis_size("img")) if i // 2 == 2])


def plane_pieces(own, near):
    pieces = [(array, 2 * i) for i, array in enumerate([own] + list(near))]
    return pieces + [(swap_core(array), mask | 1) for array, mask in pieces]


def across_plane(sent):
    return (swap_x(sent[0]), swap_y(sent[1]), swap_both(sent[2]))


def sum_plane(kept, over_x, over_y, over_both):
    return (kept + over_x.astype(SINGLE)) + (over_y.astype(SINGLE) + over_both.astype(SINGLE))


def together(*values):
    return lax.optimization_barrier(values)


def fits_planes(width, block):
    return lax.axis_size("row") == 4 and lax.axis_size("img") == 8 and 8 * block == 3 * width


def own_rows(weights, width):
    length = weights.shape[0]
    block, rest = length // width, length % width
    start = TAIL * width + rest * device_index() - 4 * width
    own = lax.dynamic_update_slice(jnp.zeros(((block + TAIL) * width,), HALF), weights, (start,))
    return own.reshape(block + TAIL, width), start


def per_device(activations, cotangent, weights):
    images, local_rows, columns, width = activations.shape
    tokens = images * local_rows * columns
    size = tokens // images
    rows_all = local_rows * lax.axis_size("row")
    far = images * rows_all
    first_row = lax.axis_index("row") * local_rows
    summary_count = float(images * lax.axis_size("img") * rows_all)
    block = weights.shape[0] // width
    planes = fits_planes(width, block)
    split = block // 2 // TAIL * TAIL
    me = device_index()
    index = me[None]
    z = lax.axis_index("img") // 2
    block_in = activations.reshape(tokens, width)

    row_means = jnp.mean(activations.astype(SINGLE), axis=2)
    sums = jnp.stack([jnp.sum(row_means, axis=(0, 1)), jnp.sum(row_means * row_means, axis=(0, 1))])
    if planes:
        weights, sums, row_means = together(weights, sums, row_means)
        own, start = own_rows(weights, width)
        piece_rows = block + TAIL
        own = jnp.concatenate([own] + parts_of(sums) + [jnp.zeros((TAIL - 6, width), HALF)])
        over_far = swap_far(own)
        means = row_means.reshape(-1, width)
        spare = jnp.zeros((TAIL - means.shape[0], width), SINGLE)
        own_shown = jnp.concatenate([own[:piece_rows]] + parts_of(jnp.concatenate([means, spare])))
        own_near = across_plane([own_shown] * 3)
        over_near = swap_near(jnp.stack([own, over_far]))
        over_near, own_near = together(over_near, own_near)
        own_pieces = plane_pieces(own_shown, own_near)
        held = [own, over_near[0], over_far, over_near[1]]
        sums = [whole_of(array[piece_rows : piece_rows + 6]) for array in held]
        sums = (sums[0] + sums[1]) + (sums[2] + sums[3])
        held = jnp.stack([array[:piece_rows] for array in held])

        def slot(i):
            return lax.dynamic_index_in_dim(held, z ^ i, 0, keepdims=False)

        known = parts_of(sums) + [jnp.zeros((TAIL - 6, width), HALF)]
        first_slot = jnp.concatenate([slot(jnp.where(z == 0, 1, 0)), slot(1)[:TAIL]] + known)
        last_slots = jnp.stack([slot(i) for i in second_slots(z)])
        first_near, last_slots = together(across_plane([first_slot] * 3), last_slots)
        first_pieces = plane_pieces(first_slot, first_near)
        last_near = across_plane([last_slots] * 3)
        w_qkv, key_far, value_far, standard, summary_low, *stats = projection_weights(
            index, own_pieces, first_pieces, block, images, local_rows, summary_count
        )
        summary_mean, summary_var, summary_inv = (row.reshape(width) for row in stats[:3])
        gain_one, gain_sum, bias_sum, gain_two = stats[3:]
        standard = standard.reshape(images, rows_all, width)
    else:
        vectors, matrix_rows = gather_weights(weights, width)
        gain_one, gain_sum, bias_sum, gain_two = (
            vectors[i : i + 1].astype(SINGLE) for i in range(4)
        )
        all_means = gather_rows(row_means)
        for axis, distance, _ in row_hops() + image_hops():
            sums = sums + swap(sums, axis, distance)
        summary_mean = sums[0] / summary_count
        summary_var = sums[1] / summary_count - summary_mean * summary_mean
        summary_inv = lax.rsqrt(summary_var + EPS)
        standard = (all_means - summary_mean) * summary_inv
        summary_low = (standard * gain_sum + bias_sum).astype(HALF).reshape(far, width)
        w_qkv = jnp.concatenate([matrix_rows[i * width : (i + 1) * width] for i in range(3)], axis=1)
        key_far = dot(summary_low, w_qkv[:, width : 2 * width]).astype(HALF)
        value_far = dot(summary_low, w_qkv[:, 2 * width :]).astype(HALF)
    key_far = key_far.reshape(images, rows_all, width)
    value_far = value_far.reshape(images, rows_all, width)

    forward = attention_forward(
        (0, images),
        None,
        block_in,
        gain_one,
        w_qkv,
        key_far,
        value_far,
        first_row[None],
        local_rows,
        columns,
    )
    if planes:
        last_near, forward = together(last_near, forward)
        given = own_pieces + first_pieces + plane_pieces(last_slots, last_near)
    query, key, value, mixed, probs = forward

    if planes:
        late_plan, late_shapes = piece_plan(block, 1)
        early_plan, early_shapes = piece_plan(block, 3)
        early_shapes = [shape + (width,) for shape in early_shapes]
        late_shapes = [shape + (width,) for shape in late_shapes]
    else:
        early_shapes = [(TAIL + width + 2 * FF, width)]
        late_shapes = [(TAIL + 3 * width, width)]
        early_plan = [(0, (), lambda i: i * 0, early_shapes[0][0])]
        late_plan = [(0, (), lambda i: i * 0, late_shapes[0][0])]
        given = jnp.pad(matrix_rows[3 * width :], ((TAIL, 0), (0, 0)))

    out, middle_grad, mixed_grad, gain_two_grad, *early = feed_forward(
        index,
        block_in,
        mixed,
        cotangent.reshape(tokens, width),
        gain_two,
        given,
        block if planes else None,
        FF,
        size,
        early_plan,
        early_shapes,
    )
    standard_flat = standard.reshape(far, width)
    last = [gain_one, gain_two_grad, w_qkv, summary_low, standard_flat, gain_sum]
    if planes:
        (early_kept, early_sent), mixed_grad = together(sum_core(*early), mixed_grad)
        early_in = across_plane(early_sent)
    steps = images * local_rows // math.gcd(local_rows, 4)
    backward = attention_backward(
        (0, steps),
        None,
        index,
        block_in,
        query,
        key,
        value,
        key_far,
        value_far,
        probs,
        mixed_grad,
        last,
        local_rows,
        columns,
        late_plan,
        late_shapes,
    )
    query_grad, key_grad, value_grad, shared, *late = backward
    if planes:
        (late_kept, late_sent), shared, early = together(
            sum_core(*late), shared + swap_core(shared), sum_plane(early_kept, *early_in)
        )
        small = shared[far:]
        late_sent = [with_sums(sent[0], small) for sent in late_sent]
        late_sent[0] = jnp.concatenate([late_sent[0], shared[:far].astype(HALF)])
        late_in = across_plane(late_sent)
        by_mask = [
            jnp.where(z == i, 0.0, lax.dynamic_index_in_dim(early, (z ^ i) - 1, 0, keepdims=False))
            for i in range(4)
        ]
        early_in = swap_near(jnp.stack([by_mask[1], by_mask[3]]).astype(HALF))
        late_in, early_in = together(late_in, early_in)
        rows = late_kept.shape[1]
        both = rows + small.shape[0] + 8
        late = sum_plane(late_kept[0], *[array[:rows] for array in late_in])
        over_x, over_y, over_both = (sums_of(array[rows:both]) for array in late_in)
        shared = shared[:far] + late_in[0][both:].astype(SINGLE)
        small = (small + over_x) + (over_y + over_both)
        early_far = send_far((by_mask[2] + early_in[1].astype(SINGLE)).astype(HALF))
        near_in = swap_near(with_sums(late.astype(HALF), small))
    else:
        for axis, distance, _ in row_hops():
            shared = shared + swap(shared, axis, distance)
        small = shared[far:]
        for axis, distance, _ in image_hops():
            small = small + swap(small, axis, distance)
    input_grad = input_grads(
        block_in, gain_one, query_grad, key_grad, value_grad, w_qkv, middle_grad, local_rows, columns
    )
    if planes:
        near_in, early_far, input_grad = together(near_in, early_far, input_grad)
        late = late + near_in[:rows].astype(SINGLE)
        small = small + sums_of(near_in[rows:])
        late_own = late + send_down(late.astype(HALF)).astype(SINGLE)
        small = small + swap_far(small)
    own_grad = lax.dynamic_slice_in_dim(
        shared[:far].reshape(images, rows_all, width), first_row, local_rows, axis=1
    )
    own_standard = lax.dynamic_slice_in_dim(standard, first_row, local_rows, axis=1)
    mean_grad = summary_inv * (
        own_grad - small[0] / summary_count - own_standard * (small[1] / summary_count)
    )
    input_grad = input_grad.reshape(activations.shape) + (mean_grad / columns)[:, :, None, :]
    if planes:
        early_own = by_mask[0] + early_in[0].astype(SINGLE) + early_far.astype(SINGLE)
        head = jnp.where(
            me == 0,
            jnp.concatenate([jnp.zeros((TAIL - 4, width), SINGLE), small[2:6]]),
            jnp.where(me == 8, small[8:], 0.0),
        )
        mine = jnp.where(z == 0, late_own, early_own)
        mine = jnp.concatenate([mine[:TAIL] + head, mine[TAIL:]])
        weight_grad = lax.dynamic_slice(mine.reshape(-1), (start,), weights.shape)
    else:
        grad_rows = jnp.concatenate([late[0][TAIL:], early[0][TAIL:]]).astype(SINGLE)
        weight_grad = scatter_grads(small[2:6], grad_rows, weights.shape[0])
    return (
        out.reshape(activations.shape),
        input_grad,
        weight_grad,
        summary_mean,
        summary_var,
    )


def solution(mesh):
    placed = (P("img", "row", None, None), P("img", "row", None, None), P(("img", "row")))
    return jax.shard_map(
        per_device,
        mesh=mesh,
        in_specs=placed,
        out_specs=(
            P("img", "row", None, None),
            P("img", "row", None, None),
            P(("img", "row")),
            P(),
            P(),
        ),
        check_vma=False,
    )
```

```python
import functools
import math

import jax
import jax.numpy as jnp
from jax import lax
from jax.experimental import pallas as pl
from jax.experimental.pallas import tpu as pltpu
from jax.sharding import PartitionSpec as P

FF = 2048
HEADS = 8
LANES = 128


EPS = 1e-05
NEGATIVE = -1e30
HALF = jnp.bfloat16
SINGLE = jnp.float32
VMEM_BYTES = 56 * 1024 * 1024

TAIL = 16


def swap(value, axis, distance):
    size = lax.axis_size(axis)
    return lax.ppermute(value, axis, [(i, i ^ distance) for i in range(size)])


def hops():
    rows, images = lax.axis_size("row"), lax.axis_size("img")
    inner = ("row", 1, 1)
    across = ("row", 2, 2)
    along = ("img", 1, rows)
    outer = []
    distance = images // 2
    while distance > 1:
        outer.append(("img", distance, distance * rows))
        distance //= 2
    distance = rows // 2
    while distance > 2:
        outer.append(("row", distance, distance))
        distance //= 2
    return inner, across, along, outer


def piece_order():
    inner, across, along, outer = hops()
    masks = [0]
    for _, _, mask in outer:
        masks = masks + [m ^ mask for m in masks]
    near = (
        masks
        + [m ^ across[2] for m in masks]
        + [m ^ along[2] for m in masks]
        + [m ^ across[2] ^ along[2] for m in masks]
    )
    return near + [m ^ inner[2] for m in near]


def device_index():
    return lax.axis_index("img") * lax.axis_size("row") + lax.axis_index("row")


def gather_pieces(own):
    inner, across, along, outer = hops()
    held = own[None]
    for axis, distance, _ in outer:
        held = jnp.concatenate([held, swap(held, axis, distance)])
    half = held.shape[0] // 2
    held_x = swap(held, across[0], across[1])
    held_y = swap(held, along[0], along[1])
    corner_first = swap(held_x[:half], along[0], along[1])
    corner_second = swap(held_y[half:], across[0], across[1])
    near = [held, held_x, held_y, corner_first, corner_second]
    far = [swap(part, inner[0], inner[1]) for part in near]
    return jnp.concatenate(near + far)


def scatter_pieces(pieces):
    inner, across, along, outer = hops()

    def add(kept, sent, axis, distance):
        return kept + swap(sent.astype(HALF), axis, distance).astype(SINGLE)

    count = pieces.shape[0] // 2
    near = add(pieces[:count], pieces[count:], inner[0], inner[1])
    quarter = count // 4
    half = quarter // 2
    held, held_x, held_y, corner = (near[i * quarter : (i + 1) * quarter] for i in range(4))
    first = add(
        jnp.concatenate([held[:half], held_x[:half]]),
        jnp.concatenate([held_y[:half], corner[:half]]),
        along[0],
        along[1],
    )
    second = add(
        jnp.concatenate([held[half:], held_y[half:]]),
        jnp.concatenate([held_x[half:], corner[half:]]),
        across[0],
        across[1],
    )
    first = add(first[:half], first[half:], across[0], across[1])
    second = add(second[:half], second[half:], along[0], along[1])
    held = jnp.concatenate([first, second])
    for axis, distance, _ in reversed(outer):
        half = held.shape[0] // 2
        held = add(held[:half], held[half:], axis, distance)
    return held[0]


def row_hops():
    inner, across, _, outer = hops()
    return [inner, across] + [hop for hop in outer if hop[0] == "row"]


def image_hops():
    _, _, along, outer = hops()
    return [along] + [hop for hop in outer if hop[0] == "img"]


def gather_rows(own):
    held, masks = own[None], [0]
    for axis, distance, mask in row_hops():
        held = jnp.concatenate([held, swap(held, axis, distance)])
        masks = masks + [m ^ mask for m in masks]
    place = [0] * len(masks)
    for at, mask in enumerate(masks):
        place[mask] = at
    order = jnp.asarray(place, jnp.int32)[jnp.arange(len(masks)) ^ lax.axis_index("row")]
    held = jnp.moveaxis(jnp.take(held, order, axis=0, mode="clip"), 0, 1)
    return held.reshape(own.shape[0], -1, own.shape[-1])


def gather_weights(weights, model_width):
    length = weights.shape[0]
    me = device_index()
    devices = lax.axis_size("img") * lax.axis_size("row")
    block = length // model_width
    rest = length % model_width
    start = TAIL * model_width + rest * me - 4 * model_width
    own = lax.dynamic_update_slice(jnp.zeros(((block + TAIL) * model_width,), HALF), weights, (start,))
    own = own.reshape(block + TAIL, model_width)
    pieces = gather_pieces(own)
    place = [0] * devices
    for at, mask in enumerate(piece_order()):
        place[mask] = at
    order = jnp.asarray(place, jnp.int32)[jnp.arange(devices) ^ me]
    pieces = jnp.take(pieces, order, axis=0, mode="clip")
    tails = jnp.concatenate([pieces[1:, :TAIL], jnp.zeros((1, TAIL, model_width), HALF)])
    body = jnp.concatenate([pieces[:, TAIL:block], pieces[:, block:] + tails], axis=1)
    return pieces[0, TAIL - 4 : TAIL], body.reshape(devices * block, model_width)


def scatter_grads(vectors, rows, length):
    model_width = rows.shape[1]
    me = device_index()
    devices = lax.axis_size("img") * lax.axis_size("row")
    block = length // model_width
    rest = length % model_width
    whole = jnp.concatenate([jnp.zeros((TAIL - 4, model_width), SINGLE), vectors, rows])
    place = jnp.asarray(piece_order(), jnp.int32)
    pieces = jnp.stack([whole[block * s : block * s + block + TAIL] for s in range(devices)])
    pieces = jnp.take(pieces, place ^ me, axis=0, mode="clip")
    mine = scatter_pieces(pieces)
    start = TAIL * model_width + rest * me - 4 * model_width
    return lax.dynamic_slice(mine.reshape(-1), (start,), (length,))


def dot(left, right):
    return jnp.dot(left, right, preferred_element_type=SINGLE)


def dot_rows(left, right):
    return lax.dot_general(left, right, (((1,), (1,)), ((), ())), preferred_element_type=SINGLE)


def dot_outer(left, right):
    return lax.dot_general(left, right, (((0,), (0,)), ((), ())), preferred_element_type=SINGLE)


def normalize(values):
    centred = values - jnp.mean(values, axis=-1, keepdims=True)
    inverse = lax.rsqrt(jnp.mean(centred * centred, axis=-1, keepdims=True) + EPS)
    return (centred * inverse, inverse)


def norm_back(grad_norm, normed, inverse):
    return inverse * (
        grad_norm
        - jnp.mean(grad_norm, axis=-1, keepdims=True)
        - normed * jnp.mean(grad_norm * normed, axis=-1, keepdims=True)
    )


def whole_block(shape):
    return pl.BlockSpec(shape, lambda *_: (0,) * len(shape), pipeline_mode=pl.Buffered(1))


def head_keys(rows_per_step, model_width):
    return [
        (row, pair, half)
        for row in range(rows_per_step)
        for pair in range(model_width // LANES)
        for half in range(2)
    ]


def attention_forward_kernel(
    scaling,
    rows_per_step,
    local_rows,
    first_row_ref,
    block_ref,
    gain_ref,
    w_ref,
    key_far_ref,
    value_far_ref,
    query_ref,
    key_ref,
    value_ref,
    mixed_ref,
    probs_ref,
):
    columns = block_ref.shape[0] // rows_per_step
    far = key_far_ref.shape[0]
    width = block_ref.shape[1]
    head_width = width // HEADS
    step = pl.program_id(0)
    normed, _ = normalize(block_ref[...].astype(SINGLE))
    attn_in = (normed * gain_ref[...]).astype(HALF)
    for i, ref in enumerate((query_ref, key_ref, value_ref)):
        ref[...] = dot(attn_in, w_ref[:, i * width : (i + 1) * width]).astype(HALF)
    first_half = lax.broadcasted_iota(jnp.int32, (columns + far, LANES), 1) < head_width
    far_index = lax.broadcasted_iota(jnp.int32, (far, columns), 0)
    key_index = lax.broadcasted_iota(jnp.int32, (columns, columns), 0)
    query_index = lax.broadcasted_iota(jnp.int32, (columns, columns), 1)
    causal = jnp.where(key_index <= query_index, 0.0, NEGATIVE)
    keys = head_keys(rows_per_step, width)
    for start in range(0, len(keys), 4 * HEADS):
        group = keys[start : start + 4 * HEADS]
        scores, low, mixed = {}, {}, {}
        for row, pair, half in group:
            global_row = first_row_ref[0] + lax.rem(step * rows_per_step + row, local_rows)
            far_bias = jnp.where(far_index < global_row, 0.0, NEGATIVE)
            tokens = slice(row * columns, (row + 1) * columns)
            lanes = slice(pair * LANES, (pair + 1) * LANES)
            all_keys = jnp.concatenate([key_ref[tokens, lanes], key_far_ref[:, lanes]], axis=0)
            one_head = jnp.where(
                first_half if half == 0 else ~first_half, all_keys, jnp.zeros_like(all_keys)
            )
            found = dot_rows(one_head, query_ref[tokens, lanes])
            scores[row, pair, half] = jnp.concatenate(
                [found[:columns] + causal, found[columns:] + far_bias], axis=0
            )
        for row, pair, half in group:
            found = scores.pop((row, pair, half))
            top = jnp.max(found, axis=0, keepdims=True)
            powers = jnp.exp2((found - top) * (scaling * math.log2(math.e)))
            inverse = 1.0 / jnp.sum(powers, axis=0, keepdims=True)
            low[row, pair, half] = (powers * inverse).astype(HALF)
            probs_ref[row, 2 * pair + half] = low[row, pair, half]
        for row, pair, half in group:
            tokens = slice(row * columns, (row + 1) * columns)
            lanes = slice(pair * LANES, (pair + 1) * LANES)
            all_values = jnp.concatenate([value_ref[tokens, lanes], value_far_ref[:, lanes]], axis=0)
            turned = all_values.T[half * head_width : (half + 1) * head_width]
            mixed[row, pair, half] = dot(turned, low[row, pair, half])
        for row, pair, half in group:
            if half == 0:
                tokens = slice(row * columns, (row + 1) * columns)
                lanes = slice(pair * LANES, (pair + 1) * LANES)
                both = jnp.concatenate([mixed[row, pair, 0], mixed[row, pair, 1]], axis=0)
                mixed_ref[tokens, lanes] = both.T.astype(HALF)


def image_groups(images):
    return [(0, 1), (1, images - 1)] if images > 1 else [(0, images)]


def step_groups(steps):
    if steps < 4:
        return [(0, steps)]
    first, last = steps // 3, max(1, steps // 6)
    return [(0, first), (first, steps - first - last), (steps - last, last)]


def kept_arrays(previous, start):
    if previous is None:
        return ([], [], {})
    specs = [pl.BlockSpec(memory_space=pl.ANY)] * len(previous)
    return (list(previous), specs, {start + i: i for i in range(len(previous))})


def attention_forward(
    group, previous, block_in, gain, w_qkv, key_far, value_far, first_row, local_rows, columns
):
    tokens, width = block_in.shape
    images, far, _ = key_far.shape
    first_image, count = group
    rows_per_step = math.gcd(local_rows, 4)
    steps = local_rows // rows_per_step
    first_step = first_image * steps
    size = rows_per_step * columns
    block = pl.BlockSpec((size, width), lambda i, _: (first_step + i, 0))
    far_block = pl.BlockSpec((None, far, width), lambda i, _: (first_image + i // steps, 0, 0))
    probs_block = pl.BlockSpec(
        (rows_per_step, HEADS, columns + far, columns), lambda i, _: (first_step + i, 0, 0, 0)
    )
    inputs = [block_in, gain, w_qkv, key_far, value_far]
    kept, kept_specs, aliases = kept_arrays(previous, 1 + len(inputs))
    low = jax.ShapeDtypeStruct((tokens, width), HALF)
    part = count * tokens // images
    kernel = functools.partial(
        attention_forward_kernel, 1.0 / math.sqrt(width // HEADS), rows_per_step, local_rows
    )

    def body(*refs):
        kernel(*refs[: 1 + len(inputs)], *refs[1 + len(inputs) + len(kept) :])

    return pl.pallas_call(
        body,
        grid_spec=pltpu.PrefetchScalarGridSpec(
            num_scalar_prefetch=1,
            grid=(count * steps,),
            in_specs=[
                block,
                whole_block((1, width)),
                whole_block((width, 3 * width)),
                far_block,
                far_block,
            ]
            + kept_specs,
            out_specs=[block] * 4 + [probs_block],
        ),
        out_shape=[low] * 4
        + [jax.ShapeDtypeStruct((images * local_rows, HEADS, columns + far, columns), HALF)],
        input_output_aliases=aliases,
        compiler_params=pltpu.CompilerParams(vmem_limit_bytes=VMEM_BYTES),
        cost_estimate=pl.CostEstimate(
            flops=part * width * (6 * width + 8 * (columns + far)),
            bytes_accessed=part * width * 12 + part * HEADS * (columns + far) * 2,
            transcendentals=part * HEADS * (columns + far),
        ),
        name="attention_forward",
    )(first_row, *inputs, *kept)


GELU_OUTER = math.sqrt(2.0 / math.pi)
GELU_CUBE = 0.044715


def gelu_and_slope(value):
    square = value * value
    gate = 0.5 * jnp.tanh(value * (GELU_OUTER * GELU_CUBE * square + GELU_OUTER)) + 0.5
    activated = value * gate
    slope = gate + activated * (1.0 - gate) * (6.0 * GELU_OUTER * GELU_CUBE * square + 2.0 * GELU_OUTER)
    return (activated, slope)


def start_pieces(plan, flat_ref, outs, sems, index, wanted=lambda place: True):
    copies = []
    for i, (out, place, offset, rows) in enumerate(plan):
        if not wanted(place):
            continue
        source = flat_ref.at[pl.ds(pl.multiple_of(offset(index), TAIL), rows)]
        target = outs[out].at[place] if place else outs[out]
        copies.append(pltpu.make_async_copy(source, target, sems.at[i]))
    for copy in copies:
        copy.start()
    return copies


def feed_forward_kernel(
    chunk,
    plan,
    masks,
    block,
    index_ref,
    block_ref,
    mixed_ref,
    cotangent_ref,
    gain_ref,
    *rest,
):
    given, rest = rest[: max(1, 3 * len(masks))], rest[max(1, 3 * len(masks)) :]
    out_ref, middle_grad_ref, mixed_grad_ref, grad_gain_ref, *rest = rest
    *pieces, grad_out_ref, grad_inner_ref, grad_outer_ref, w_inner_ref, flat_ref, sems = rest
    width, hidden = w_inner_ref.shape
    groups = hidden // width
    per = 256 // groups
    inner_start = TAIL + width
    outer_start = inner_start + hidden
    w_out_ref = flat_ref.at[TAIL:inner_start]
    w_outer_ref = flat_ref.at[outer_start:]

    @pl.when(pl.program_id(0) == 0)
    def _():
        for ref in (grad_out_ref, grad_inner_ref, grad_outer_ref, grad_gain_ref):
            ref[...] = jnp.zeros_like(ref)
        if block is None:
            flat_ref[...] = given[0][...]
        else:
            plane = 8 * block
            here, z = lax.rem(index_ref[0], 8), lax.div(index_ref[0], 8)
            own, first, last = (
                list(zip(given[i * len(masks) : (i + 1) * len(masks)], masks)) for i in range(3)
            )
            clear_seams(flat_ref, block, 3)

            @pl.when(z == 0)
            def _():
                assemble(flat_ref, first, here, block, 0)

            @pl.when(z > 0)
            def _():
                assemble(flat_ref, own, here, block, (z - 1) * plane)

            for i, slot in enumerate(second_slots(z)):
                pieces_here = [(ref.at[i], mask) for ref, mask in last]
                assemble(flat_ref, pieces_here, here, block, (slot - 1) * plane)
        mix = weave(groups, per)
        for c in range(width // per):
            start = inner_start + c * groups * per
            parted = dot_outer(mix, flat_ref[start : start + groups * per]).astype(HALF)
            for g in range(groups):
                w_inner_ref[c * per : (c + 1) * per, g * width : (g + 1) * width] = parted[
                    g * per : (g + 1) * per
                ]

    mixed = mixed_ref[...]
    cotangent = cotangent_ref[...]
    middle = block_ref[...].astype(SINGLE) + dot(mixed, w_out_ref[...])
    normed, inverse = normalize(middle)
    ff_in = (normed * gain_ref[...]).astype(HALF)
    out = middle
    ff_grad = jnp.zeros_like(middle)
    cotangent_turned = cotangent.T
    ff_turned = ff_in.T
    count = hidden // chunk
    spans = [slice(j * chunk, (j + 1) * chunk) for j in range(count)]

    def products(j):
        return (dot(ff_in, w_inner_ref[:, spans[j]]), dot_rows(cotangent, w_outer_ref[spans[j], :]))

    ready = products(0)
    for j in range(count):
        inner, act_grad = ready
        if j + 1 < count:
            ready = products(j + 1)
        activated, slope = gelu_and_slope(inner)
        activated = activated.astype(HALF)
        inner_grad = (slope * act_grad).astype(HALF)
        out = out + dot(activated, w_outer_ref[spans[j], :])
        ff_grad = ff_grad + dot_rows(inner_grad, w_inner_ref[:, spans[j]])
        grad_inner_ref[:, spans[j]] += dot(ff_turned, inner_grad)
        grad_outer_ref[:, spans[j]] += dot(cotangent_turned, activated)
    out_ref[...] = out.astype(HALF)
    grad_gain_ref[...] += jnp.sum(ff_grad * normed, axis=0, keepdims=True)
    middle_grad = cotangent.astype(SINGLE) + norm_back(ff_grad * gain_ref[...], normed, inverse)
    middle_grad_ref[...] = middle_grad
    branch_grad = middle_grad.astype(HALF)
    mixed_grad_ref[...] = dot_rows(branch_grad, w_out_ref[...]).astype(HALF)
    grad_out_ref[...] += dot_outer(mixed, branch_grad)

    @pl.when(pl.program_id(0) == pl.num_programs(0) - 1)
    def _():
        start = TAIL + width + hidden
        for j in range(hidden // width):
            turned = grad_outer_ref[:, j * width : (j + 1) * width].astype(HALF).T
            flat_ref[start + j * width : start + (j + 1) * width] = turned

        def behind(place):
            return place != () and place[1] == 2

        copies = start_pieces(plan, flat_ref, pieces, sems, index_ref[0], behind)
        flat_ref[:TAIL] = jnp.zeros((TAIL, width), HALF)
        flat_ref[TAIL : TAIL + width] = grad_out_ref[...].astype(HALF)
        mix = weave(groups, per)
        for c in range(width // per):
            parts = [
                grad_inner_ref[c * per : (c + 1) * per, g * width : (g + 1) * width].astype(HALF)
                for g in range(groups)
            ]
            start = TAIL + width + c * groups * per
            woven = dot(mix, jnp.concatenate(parts, axis=0))
            flat_ref[start : start + groups * per] = woven.astype(HALF)
        copies += start_pieces(
            plan, flat_ref, pieces, sems, index_ref[0], lambda place: not behind(place)
        )
        for copy in copies:
            copy.wait()


def weave(groups, per):
    size = groups * per
    row = lax.broadcasted_iota(jnp.int32, (size, size), 0)
    column = lax.broadcasted_iota(jnp.int32, (size, size), 1)
    wanted = lax.rem(row, groups) * per + lax.div(row, groups)
    return (wanted == column).astype(SINGLE).astype(HALF)


def piece_outputs(shapes):
    return (
        [pl.BlockSpec(memory_space=pl.ANY)] * len(shapes),
        [jax.ShapeDtypeStruct(shape, HALF) for shape in shapes],
    )


def feed_forward(index, block_in, mixed, cotangent, gain, given, block, hidden, size, plan, shapes):
    tokens, width = block_in.shape
    tile = pl.BlockSpec((size, width), lambda i, _: (i, 0))
    piece_specs, piece_shapes = piece_outputs(shapes)
    masks = [] if block is None else [mask for _, mask in given[: len(given) // 3]]
    arrays = [given] if block is None else [array for array, _ in given]
    return pl.pallas_call(
        functools.partial(feed_forward_kernel, 256, plan, masks, block),
        grid_spec=pltpu.PrefetchScalarGridSpec(
            num_scalar_prefetch=1,
            grid=(tokens // size,),
            in_specs=[tile, tile, tile, whole_block((1, width))] + vmem_specs(len(arrays)),
            out_specs=[tile, tile, tile, whole_block((1, width))] + piece_specs,
            scratch_shapes=[
                pltpu.VMEM((width, width), SINGLE),
                pltpu.VMEM((width, hidden), SINGLE),
                pltpu.VMEM((width, hidden), SINGLE),
                pltpu.VMEM((width, hidden), HALF),
                pltpu.VMEM((TAIL + width + 2 * hidden, width), HALF),
                pltpu.SemaphoreType.DMA((len(plan),)),
            ],
        ),
        out_shape=[
            jax.ShapeDtypeStruct((tokens, width), HALF),
            jax.ShapeDtypeStruct((tokens, width), SINGLE),
            jax.ShapeDtypeStruct((tokens, width), HALF),
            jax.ShapeDtypeStruct((1, width), SINGLE),
        ]
        + piece_shapes,
        compiler_params=pltpu.CompilerParams(vmem_limit_bytes=VMEM_BYTES),
        cost_estimate=pl.CostEstimate(
            flops=tokens * width * (6 * width + 12 * hidden),
            bytes_accessed=tokens * width * 14 + width * hidden * 8,
            transcendentals=tokens * hidden,
        ),
        name="feed_forward",
    )(index, block_in, mixed, cotangent, gain, *arrays)


def attention_backward_kernel(
    scaling,
    rows_per_step,
    per_image,
    first_step,
    plan,
    ends,
    index_ref,
    block_ref,
    query_ref,
    key_ref,
    value_ref,
    key_far_ref,
    value_far_ref,
    probs_ref,
    mixed_grad_ref,
    *rest,
):
    rest = list(rest)
    earlier = None
    if first_step > 0:
        earlier, rest = rest[:3], rest[6:]
    if ends:
        fixed, rest = rest[:6], rest[6:]
    query_grad_ref, key_grad_ref, value_grad_ref, *rest = rest
    if ends:
        shared_ref, *rest = rest
        small_ref = shared_ref.at[shared_ref.shape[0] - 8 - TAIL :]
        *pieces, total_ref, key_far_grad_ref, value_far_grad_ref, flat_ref, sems = rest
    else:
        total_ref, key_far_grad_ref, value_far_grad_ref = rest
    width = query_ref.shape[1]
    head_width = width // HEADS
    far = key_far_ref.shape[0]
    columns = query_ref.shape[0] // rows_per_step
    image = lax.div(first_step + pl.program_id(0), per_image)

    @pl.when(pl.program_id(0) == 0)
    def _():
        for i, ref in enumerate((total_ref, key_far_grad_ref, value_far_grad_ref)):
            ref[...] = jnp.zeros_like(ref) if earlier is None else earlier[i][...]

    first_half = lax.broadcasted_iota(jnp.int32, (columns + far, LANES), 1) < head_width
    keys = head_keys(rows_per_step, width)
    for start in range(0, len(keys), 2 * HEADS):
        group = keys[start : start + 2 * HEADS]
        prob_grad, score_grad, value_grad, key_grad, query_grad = {}, {}, {}, {}, {}
        for row, pair, half in group:
            tokens = slice(row * columns, (row + 1) * columns)
            lanes = slice(pair * LANES, (pair + 1) * LANES)
            all_values = jnp.concatenate([value_ref[tokens, lanes], value_far_ref[:, lanes]], axis=0)
            one_head = jnp.where(
                first_half if half == 0 else ~first_half, all_values, jnp.zeros_like(all_values)
            )
            prob_grad[row, pair, half] = dot_rows(one_head, mixed_grad_ref[tokens, lanes])
        for row, pair, half in group:
            tokens = slice(row * columns, (row + 1) * columns)
            lanes = slice(pair * LANES, (pair + 1) * LANES)
            value_grad[row, pair, half] = dot(
                probs_ref[row, 2 * pair + half], mixed_grad_ref[tokens, lanes]
            )
        for row, pair, half in group:
            probs = probs_ref[row, 2 * pair + half].astype(SINGLE)
            grad = prob_grad.pop((row, pair, half))
            total = jnp.sum(probs * grad, axis=0, keepdims=True)
            score_grad[row, pair, half] = (probs * (grad - total)).astype(HALF)
        for row, pair, half in group:
            tokens = slice(row * columns, (row + 1) * columns)
            lanes = slice(pair * LANES, (pair + 1) * LANES)
            key_grad[row, pair, half] = dot(score_grad[row, pair, half], query_ref[tokens, lanes])
            all_keys = jnp.concatenate([key_ref[tokens, lanes], key_far_ref[:, lanes]], axis=0)
            turned = all_keys.T[half * head_width : (half + 1) * head_width]
            query_grad[row, pair, half] = dot(turned, score_grad[row, pair, half])
        for row, pair, half in group:
            if half == 0:
                tokens = slice(row * columns, (row + 1) * columns)
                lanes = slice(pair * LANES, (pair + 1) * LANES)
                first, second = (row, pair, 0), (row, pair, 1)
                value_both = jnp.where(first_half, value_grad[first], value_grad[second])
                key_both = jnp.where(first_half, key_grad[first], key_grad[second]) * scaling
                value_grad_ref[tokens, lanes] = value_both[:columns].astype(HALF)
                key_grad_ref[tokens, lanes] = key_both[:columns].astype(HALF)
                value_far_grad_ref[image, :, lanes] += value_both[columns:]
                key_far_grad_ref[image, :, lanes] += key_both[columns:]
                query_both = jnp.concatenate([query_grad[first], query_grad[second]], axis=0) * scaling
                query_grad_ref[tokens, lanes] = query_both.T.astype(HALF)
    normed, _ = normalize(block_ref[...].astype(SINGLE))
    turned = normed.astype(HALF).T
    for i, ref in enumerate((query_grad_ref, key_grad_ref, value_grad_ref)):
        total_ref[:, i * width : (i + 1) * width] += dot(turned, ref[...])
    if not ends:
        return

    @pl.when(pl.program_id(0) == pl.num_programs(0) - 1)
    def _():
        gain_ref, gain_two_grad_ref, w_ref, summary_ref, standard_ref, gain_sum_ref = fixed

        key_low = key_far_grad_ref[...].reshape(-1, width).astype(HALF)
        value_low = value_far_grad_ref[...].reshape(-1, width).astype(HALF)
        gain = jnp.broadcast_to(gain_ref[...], (8, width)).T[:, :1]
        matched = jnp.zeros((width, width), SINGLE)
        flat_ref[:TAIL] = jnp.zeros((TAIL, width), HALF)
        for i in range(3):
            total = total_ref[:, i * width : (i + 1) * width]
            matched = matched + total * w_ref[:, i * width : (i + 1) * width].astype(SINGLE)
            grad = total * gain
            if i > 0:
                grad = grad + dot_outer(summary_ref[...], key_low if i == 1 else value_low)
            flat_ref[TAIL + i * width : TAIL + (i + 1) * width] = grad.astype(HALF)
            if i == 2:
                small_ref[8:] = grad[width - TAIL :]
        copies = start_pieces(plan, flat_ref, pieces, sems, index_ref[0])
        summary_grad = dot_rows(key_low, w_ref[:, width : 2 * width]) + dot_rows(
            value_low, w_ref[:, 2 * width :]
        )
        standard = standard_ref[...]
        standard_grad = summary_grad * gain_sum_ref[...]
        shared_ref[: standard.shape[0]] = standard_grad

        def fold(value):
            return jnp.sum(value, axis=0, keepdims=True)

        small_ref[0:1] = fold(standard_grad)
        small_ref[1:2] = fold(standard_grad * standard)
        small_ref[2:3] = fold(matched.T)
        small_ref[3:4] = fold(summary_grad * standard)
        small_ref[4:5] = fold(summary_grad)
        small_ref[5:6] = gain_two_grad_ref[...]
        small_ref[6:8] = jnp.zeros((2, width), SINGLE)
        for copy in copies:
            copy.wait()


def attention_backward(
    group,
    previous,
    index,
    block_in,
    query,
    key,
    value,
    key_far,
    value_far,
    probs,
    mixed_grad,
    last,
    local_rows,
    columns,
    plan,
    shapes,
):
    tokens, width = query.shape
    images, far, _ = key_far.shape
    first_step, count = group
    rows_per_step = math.gcd(local_rows, 4)
    per_image = local_rows // rows_per_step
    ends = first_step + count == images * per_image
    size = rows_per_step * columns
    part = count * size
    block = pl.BlockSpec((size, width), lambda i, _: (first_step + i, 0))
    far_block = pl.BlockSpec((None, far, width), lambda i, _: ((first_step + i) // per_image, 0, 0))
    probs_block = pl.BlockSpec(
        (rows_per_step, HEADS, columns + far, columns), lambda i, _: (first_step + i, 0, 0, 0)
    )
    inputs = [block_in, query, key, value, key_far, value_far, probs, mixed_grad]
    in_specs = [block] * 4 + [far_block] * 2 + [probs_block, block]
    aliases = {}
    total_shape = (width, 3 * width)
    far_shape = (images, far, width)
    if previous is not None:
        sums = list(previous[3:])
        inputs = inputs + sums
        in_specs = in_specs + [whole_block(array.shape) for array in sums]
        kept, kept_specs, aliases = kept_arrays(previous[:3], 1 + len(inputs))
        inputs, in_specs = inputs + kept, in_specs + kept_specs
    out_specs = [block] * 3
    out_shape = [jax.ShapeDtypeStruct((tokens, width), HALF)] * 3
    scratch = []
    if ends:
        inputs = inputs + list(last)
        in_specs = in_specs + [whole_block(array.shape) for array in last]
        piece_specs, piece_shapes = piece_outputs(shapes)
        summaries = images * far
        shared_shape = (summaries + 8 + TAIL, width)
        out_specs += [whole_block(shared_shape)] + piece_specs
        out_shape += [jax.ShapeDtypeStruct(shared_shape, SINGLE)] + piece_shapes
        scratch = [
            pltpu.VMEM(total_shape, SINGLE),
            pltpu.VMEM(far_shape, SINGLE),
            pltpu.VMEM(far_shape, SINGLE),
            pltpu.VMEM((TAIL + 3 * width, width), HALF),
            pltpu.SemaphoreType.DMA((len(plan),)),
        ]
    else:
        out_specs += [whole_block(total_shape), whole_block(far_shape), whole_block(far_shape)]
        out_shape += [
            jax.ShapeDtypeStruct(total_shape, SINGLE),
            jax.ShapeDtypeStruct(far_shape, SINGLE),
            jax.ShapeDtypeStruct(far_shape, SINGLE),
        ]
    return pl.pallas_call(
        functools.partial(
            attention_backward_kernel,
            1.0 / math.sqrt(width // HEADS),
            rows_per_step,
            per_image,
            first_step,
            plan,
            ends,
        ),
        grid_spec=pltpu.PrefetchScalarGridSpec(
            num_scalar_prefetch=1,
            grid=(count,),
            in_specs=in_specs,
            out_specs=out_specs,
            scratch_shapes=scratch,
        ),
        out_shape=out_shape,
        input_output_aliases=aliases,
        compiler_params=pltpu.CompilerParams(vmem_limit_bytes=VMEM_BYTES),
        cost_estimate=pl.CostEstimate(
            flops=part * width * (6 * width + 16 * (columns + far)),
            bytes_accessed=part * width * 16 + part * HEADS * (columns + far) * 2,
            transcendentals=0,
        ),
        name="attention_backward",
    )(index, *inputs)


def input_grad_kernel(
    block_ref,
    gain_ref,
    query_grad_ref,
    key_grad_ref,
    value_grad_ref,
    w_ref,
    middle_grad_ref,
    out_ref,
):
    width = block_ref.shape[1]
    attn_grad = (
        dot_rows(query_grad_ref[...], w_ref[:, :width])
        + dot_rows(key_grad_ref[...], w_ref[:, width : 2 * width])
        + dot_rows(value_grad_ref[...], w_ref[:, 2 * width :])
    )
    normed, inverse = normalize(block_ref[...].astype(SINGLE))
    out_ref[...] = middle_grad_ref[...] + norm_back(attn_grad * gain_ref[...], normed, inverse)


def input_grads(
    block_in, gain, query_grad, key_grad, value_grad, w_qkv, middle_grad, local_rows, columns
):
    tokens, width = block_in.shape
    size = math.gcd(local_rows, 2) * columns
    block = pl.BlockSpec((size, width), lambda i: (i, 0))
    return pl.pallas_call(
        input_grad_kernel,
        grid=(tokens // size,),
        in_specs=[block, whole_block((1, width))]
        + [block] * 3
        + [whole_block((width, 3 * width)), block],
        out_specs=block,
        out_shape=jax.ShapeDtypeStruct((tokens, width), SINGLE),
        compiler_params=pltpu.CompilerParams(vmem_limit_bytes=VMEM_BYTES),
        cost_estimate=pl.CostEstimate(
            flops=tokens * width * 6 * width, bytes_accessed=tokens * width * 16, transcendentals=0
        ),
        name="input_grads",
    )(block_in, gain, query_grad, key_grad, value_grad, w_qkv, middle_grad)


def clear_seams(flat_ref, block, count):
    for at in range(0, count * 8 * block + 1, block):
        flat_ref[at : at + TAIL] = jnp.zeros((TAIL, flat_ref.shape[1]), HALF)


def assemble(flat_ref, pieces, index, block, base):
    for ref, mask in pieces:
        spot = pl.multiple_of(base + (index ^ mask) * block, TAIL)
        for low, high in ((0, TAIL), (TAIL, block), (block, block + TAIL)):
            rows = pl.ds(spot + low, high - low)
            value = ref[low:high]
            if low != TAIL:
                value = flat_ref[rows] + value
            flat_ref[rows] = value


def second_slots(z):
    return [jnp.where(z < 2, 2, 1), jnp.where(z < 3, 3, 2)]


def parts_of(value):
    high = lax.reduce_precision(value, 8, 7)
    middle = lax.reduce_precision(value - high, 8, 7)
    low = value - high - middle
    return [part.astype(HALF) for part in (high, middle, low)]


def whole_of(parts):
    rows = parts.shape[0] // 3
    parts = parts.astype(SINGLE)
    return (parts[:rows] + parts[rows : 2 * rows]) + parts[2 * rows :]


def projection_weights_kernel(
    masks,
    block,
    images,
    local_rows,
    summary_count,
    index_ref,
    *refs,
):
    count = len(masks)
    own_refs, piece_refs, refs = refs[:count], refs[count : 2 * count], refs[2 * count :]
    w_ref, key_far_ref, value_far_ref, standard_ref, summary_ref, *refs = refs
    *stat_refs, flat_ref, shown_ref, means_ref = refs
    width = flat_ref.shape[1]
    rows = block + TAIL
    here = lax.rem(index_ref[0], 8)
    clear_seams(flat_ref, block, 1)

    @pl.when(index_ref[0] < 8)
    def _():
        assemble(flat_ref, list(zip(own_refs, masks)), here, block, 0)

    @pl.when(index_ref[0] >= 8)
    def _():
        assemble(flat_ref, list(zip(piece_refs, masks)), here, block, 0)

    for own_ref, ref, mask in zip(own_refs, piece_refs, masks):
        shown_ref[here ^ mask, : 2 * TAIL] = ref[rows:]
        shown_ref[here ^ mask, 2 * TAIL :] = own_ref[rows:]
    flat_ref[3 * width :] += shown_ref[0, :TAIL]
    for i in range(3):
        w_ref[:, i * width : (i + 1) * width] = flat_ref[TAIL + i * width : TAIL + (i + 1) * width]
    total = jnp.zeros((2, width), SINGLE)
    for j in range(8):
        total = total + whole_of(shown_ref[j, TAIL : 2 * TAIL].astype(SINGLE)[:6])
    for j in range(4):
        means = whole_of(shown_ref[lax.div(here, 4) * 4 + j, 2 * TAIL :])
        for image in range(images):
            start = (image * 4 + j) * local_rows
            means_ref[start : start + local_rows] = means[image * local_rows : (image + 1) * local_rows]
    vectors = flat_ref[:TAIL].astype(SINGLE)[TAIL - 4 :]
    mean = total[:1] / summary_count
    variance = total[1:] / summary_count - mean * mean
    inverse = lax.rsqrt(variance + EPS)
    standard = (means_ref[...] - mean) * inverse
    summary = (standard * vectors[1:2] + vectors[2:3]).astype(HALF)
    standard_ref[...] = standard
    summary_ref[...] = summary
    vector_rows = [vectors[i : i + 1] for i in range(4)]
    for ref, value in zip(stat_refs, [mean, variance, inverse] + vector_rows):
        ref[...] = value
    key_far_ref[...] = dot(summary, w_ref[:, width : 2 * width]).astype(HALF)
    value_far_ref[...] = dot(summary, w_ref[:, 2 * width :]).astype(HALF)


def vmem_specs(count):
    return [pl.BlockSpec(memory_space=pltpu.VMEM)] * count


def projection_weights(index, own_pieces, pieces, block, images, local_rows, summary_count):
    arrays, masks = [p[0] for p in own_pieces + pieces], [p[1] for p in pieces]
    width = arrays[0].shape[1]
    far = 4 * images * local_rows
    return pl.pallas_call(
        functools.partial(
            projection_weights_kernel, masks, block, images, local_rows, summary_count
        ),
        in_specs=[pl.BlockSpec(memory_space=pltpu.SMEM)] + vmem_specs(len(arrays)),
        out_specs=vmem_specs(12),
        out_shape=[
            jax.ShapeDtypeStruct((width, 3 * width), HALF),
            jax.ShapeDtypeStruct((far, width), HALF),
            jax.ShapeDtypeStruct((far, width), HALF),
            jax.ShapeDtypeStruct((far, width), SINGLE),
            jax.ShapeDtypeStruct((far, width), HALF),
        ]
        + [jax.ShapeDtypeStruct((1, width), SINGLE)] * 7,
        scratch_shapes=[
            pltpu.VMEM((TAIL + 3 * width, width), HALF),
            pltpu.VMEM((8, 5 * TAIL, width), HALF),
            pltpu.VMEM((far, width), SINGLE),
        ],
        compiler_params=pltpu.CompilerParams(vmem_limit_bytes=VMEM_BYTES),
        name="projection_weights",
    )(index, *arrays)


def with_sums(value, small):
    high = lax.reduce_precision(small[:8], 8, 7)
    return jnp.concatenate(
        [value, high.astype(HALF), (small[:8] - high).astype(HALF), small[8:].astype(HALF)]
    )


def sums_of(rows):
    rows = rows.astype(SINGLE)
    return jnp.concatenate([rows[:8] + rows[8:16], rows[16:]])


def swap_core(value):
    return swap(value, "row", 1)


def swap_x(value):
    return swap(value, "row", 2)


def swap_y(value):
    return swap(value, "img", 1)


def swap_both(value):
    size = lax.axis_size("img") * lax.axis_size("row")
    return lax.ppermute(value, ("img", "row"), [(i, i ^ 6) for i in range(size)])


def swap_near(value):
    return swap(value, "img", 2)


def swap_far(value):
    return swap(value, "img", 4)


def send_far(value):
    return lax.ppermute(value, "img", [(i, i ^ 4) for i in range(lax.axis_size("img")) if i // 2 != 2])


def piece_plan(block, slots):
    plan, shapes = [], []
    rows = block + TAIL
    for out, (side, masks) in enumerate(((0, (0,)), (0, (2,)), (0, (4,)), (0, (6,)), (1, (0, 2, 4, 6)))):
        shapes.append((len(masks), slots, rows))
        for place, mask in enumerate(masks):
            for slot in range(slots):

                def offset(index, mask=mask | side, slot=slot):
                    return (slot * 8 + (lax.rem(index, 8) ^ mask)) * block

                plan.append((out, (place, slot), offset, rows))
    return plan, shapes


def sum_core(kept, over_x, over_y, over_both, other):
    other = swap_core(other)
    own = kept[0].astype(SINGLE) + other[0].astype(SINGLE)
    sent = [
        (piece[0].astype(SINGLE) + other[i + 1].astype(SINGLE)).astype(HALF)
        for i, piece in enumerate((over_x, over_y, over_both))
    ]
    return (own, sent)


def send_down(value):
    return lax.ppermute(value, "img", [(i, i ^ 4) for i in range(lax.axis_size("img")) if i // 2 == 2])


def plane_pieces(own, near):
    pieces = [(array, 2 * i) for i, array in enumerate([own] + list(near))]
    return pieces + [(swap_core(array), mask | 1) for array, mask in pieces]


def across_plane(sent):
    return (swap_x(sent[0]), swap_y(sent[1]), swap_both(sent[2]))


def sum_plane(kept, over_x, over_y, over_both):
    return (kept + over_x.astype(SINGLE)) + (over_y.astype(SINGLE) + over_both.astype(SINGLE))


def together(*values):
    return lax.optimization_barrier(values)


def fits_planes(width, block):
    return lax.axis_size("row") == 4 and lax.axis_size("img") == 8 and 8 * block == 3 * width


def own_rows(weights, width):
    length = weights.shape[0]
    block, rest = length // width, length % width
    start = TAIL * width + rest * device_index() - 4 * width
    own = lax.dynamic_update_slice(jnp.zeros(((block + TAIL) * width,), HALF), weights, (start,))
    return own.reshape(block + TAIL, width), start


def per_device(activations, cotangent, weights):
    images, local_rows, columns, width = activations.shape
    tokens = images * local_rows * columns
    size = tokens // images
    rows_all = local_rows * lax.axis_size("row")
    far = images * rows_all
    first_row = lax.axis_index("row") * local_rows
    summary_count = float(images * lax.axis_size("img") * rows_all)
    block = weights.shape[0] // width
    planes = fits_planes(width, block)
    split = block // 2 // TAIL * TAIL
    me = device_index()
    index = me[None]
    z = lax.axis_index("img") // 2
    block_in = activations.reshape(tokens, width)

    row_means = jnp.mean(activations.astype(SINGLE), axis=2)
    sums = jnp.stack([jnp.sum(row_means, axis=(0, 1)), jnp.sum(row_means * row_means, axis=(0, 1))])
    if planes:
        weights, sums, row_means = together(weights, sums, row_means)
        own, start = own_rows(weights, width)
        piece_rows = block + TAIL
        own = jnp.concatenate([own] + parts_of(sums) + [jnp.zeros((TAIL - 6, width), HALF)])
        over_far = swap_far(own)
        means = row_means.reshape(-1, width)
        spare = jnp.zeros((TAIL - means.shape[0], width), SINGLE)
        own_shown = jnp.concatenate([own[:piece_rows]] + parts_of(jnp.concatenate([means, spare])))
        own_near = across_plane([own_shown] * 3)
        over_near = swap_near(jnp.stack([own, over_far]))
        over_near, own_near = together(over_near, own_near)
        own_pieces = plane_pieces(own_shown, own_near)
        held = [own, over_near[0], over_far, over_near[1]]
        sums = [whole_of(array[piece_rows : piece_rows + 6]) for array in held]
        sums = (sums[0] + sums[1]) + (sums[2] + sums[3])
        held = jnp.stack([array[:piece_rows] for array in held])

        def slot(i):
            return lax.dynamic_index_in_dim(held, z ^ i, 0, keepdims=False)

        known = parts_of(sums) + [jnp.zeros((TAIL - 6, width), HALF)]
        first_slot = jnp.concatenate([slot(jnp.where(z == 0, 1, 0)), slot(1)[:TAIL]] + known)
        last_slots = jnp.stack([slot(i) for i in second_slots(z)])
        first_near, last_slots = together(across_plane([first_slot] * 3), last_slots)
        first_pieces = plane_pieces(first_slot, first_near)
        last_near = across_plane([last_slots] * 3)
        w_qkv, key_far, value_far, standard, summary_low, *stats = projection_weights(
            index, own_pieces, first_pieces, block, images, local_rows, summary_count
        )
        summary_mean, summary_var, summary_inv = (row.reshape(width) for row in stats[:3])
        gain_one, gain_sum, bias_sum, gain_two = stats[3:]
        standard = standard.reshape(images, rows_all, width)
    else:
        vectors, matrix_rows = gather_weights(weights, width)
        gain_one, gain_sum, bias_sum, gain_two = (
            vectors[i : i + 1].astype(SINGLE) for i in range(4)
        )
        all_means = gather_rows(row_means)
        for axis, distance, _ in row_hops() + image_hops():
            sums = sums + swap(sums, axis, distance)
        summary_mean = sums[0] / summary_count
        summary_var = sums[1] / summary_count - summary_mean * summary_mean
        summary_inv = lax.rsqrt(summary_var + EPS)
        standard = (all_means - summary_mean) * summary_inv
        summary_low = (standard * gain_sum + bias_sum).astype(HALF).reshape(far, width)
        w_qkv = jnp.concatenate([matrix_rows[i * width : (i + 1) * width] for i in range(3)], axis=1)
        key_far = dot(summary_low, w_qkv[:, width : 2 * width]).astype(HALF)
        value_far = dot(summary_low, w_qkv[:, 2 * width :]).astype(HALF)
    key_far = key_far.reshape(images, rows_all, width)
    value_far = value_far.reshape(images, rows_all, width)

    forward = attention_forward(
        (0, images),
        None,
        block_in,
        gain_one,
        w_qkv,
        key_far,
        value_far,
        first_row[None],
        local_rows,
        columns,
    )
    if planes:
        last_near, forward = together(last_near, forward)
        given = own_pieces + first_pieces + plane_pieces(last_slots, last_near)
    query, key, value, mixed, probs = forward

    if planes:
        late_plan, late_shapes = piece_plan(block, 1)
        early_plan, early_shapes = piece_plan(block, 3)
        early_shapes = [shape + (width,) for shape in early_shapes]
        late_shapes = [shape + (width,) for shape in late_shapes]
    else:
        early_shapes = [(TAIL + width + 2 * FF, width)]
        late_shapes = [(TAIL + 3 * width, width)]
        early_plan = [(0, (), lambda i: i * 0, early_shapes[0][0])]
        late_plan = [(0, (), lambda i: i * 0, late_shapes[0][0])]
        given = jnp.pad(matrix_rows[3 * width :], ((TAIL, 0), (0, 0)))

    out, middle_grad, mixed_grad, gain_two_grad, *early = feed_forward(
        index,
        block_in,
        mixed,
        cotangent.reshape(tokens, width),
        gain_two,
        given,
        block if planes else None,
        FF,
        size,
        early_plan,
        early_shapes,
    )
    standard_flat = standard.reshape(far, width)
    last = [gain_one, gain_two_grad, w_qkv, summary_low, standard_flat, gain_sum]
    if planes:
        (early_kept, early_sent), mixed_grad = together(sum_core(*early), mixed_grad)
        early_in = across_plane(early_sent)
    steps = images * local_rows // math.gcd(local_rows, 4)
    backward = attention_backward(
        (0, steps),
        None,
        index,
        block_in,
        query,
        key,
        value,
        key_far,
        value_far,
        probs,
        mixed_grad,
        last,
        local_rows,
        columns,
        late_plan,
        late_shapes,
    )
    query_grad, key_grad, value_grad, shared, *late = backward
    if planes:
        (late_kept, late_sent), shared, early = together(
            sum_core(*late), shared + swap_core(shared), sum_plane(early_kept, *early_in)
        )
        small = shared[far:]
        late_sent = [with_sums(sent[0], small) for sent in late_sent]
        late_sent[0] = jnp.concatenate([late_sent[0], shared[:far].astype(HALF)])
        late_in = across_plane(late_sent)
        by_mask = [
            jnp.where(z == i, 0.0, lax.dynamic_index_in_dim(early, (z ^ i) - 1, 0, keepdims=False))
            for i in range(4)
        ]
        early_in = swap_near(jnp.stack([by_mask[1], by_mask[3]]).astype(HALF))
        late_in, early_in = together(late_in, early_in)
        rows = late_kept.shape[1]
        both = rows + small.shape[0] + 8
        late = sum_plane(late_kept[0], *[array[:rows] for array in late_in])
        over_x, over_y, over_both = (sums_of(array[rows:both]) for array in late_in)
        shared = shared[:far] + late_in[0][both:].astype(SINGLE)
        small = (small + over_x) + (over_y + over_both)
        early_far = send_far((by_mask[2] + early_in[1].astype(SINGLE)).astype(HALF))
        near_in = swap_near(with_sums(late.astype(HALF), small))
    else:
        for axis, distance, _ in row_hops():
            shared = shared + swap(shared, axis, distance)
        small = shared[far:]
        for axis, distance, _ in image_hops():
            small = small + swap(small, axis, distance)
    input_grad = input_grads(
        block_in, gain_one, query_grad, key_grad, value_grad, w_qkv, middle_grad, local_rows, columns
    )
    if planes:
        near_in, early_far, input_grad = together(near_in, early_far, input_grad)
        late = late + near_in[:rows].astype(SINGLE)
        small = small + sums_of(near_in[rows:])
        late_own = late + send_down(late.astype(HALF)).astype(SINGLE)
        small = small + swap_far(small)
    own_grad = lax.dynamic_slice_in_dim(
        shared[:far].reshape(images, rows_all, width), first_row, local_rows, axis=1
    )
    own_standard = lax.dynamic_slice_in_dim(standard, first_row, local_rows, axis=1)
    mean_grad = summary_inv * (
        own_grad - small[0] / summary_count - own_standard * (small[1] / summary_count)
    )
    input_grad = input_grad.reshape(activations.shape) + (mean_grad / columns)[:, :, None, :]
    if planes:
        early_own = by_mask[0] + early_in[0].astype(SINGLE) + early_far.astype(SINGLE)
        head = jnp.where(
            me == 0,
            jnp.concatenate([jnp.zeros((TAIL - 4, width), SINGLE), small[2:6]]),
            jnp.where(me == 8, small[8:], 0.0),
        )
        mine = jnp.where(z == 0, late_own, early_own)
        mine = jnp.concatenate([mine[:TAIL] + head, mine[TAIL:]])
        weight_grad = lax.dynamic_slice(mine.reshape(-1), (start,), weights.shape)
    else:
        grad_rows = jnp.concatenate([late[0][TAIL:], early[0][TAIL:]]).astype(SINGLE)
        weight_grad = scatter_grads(small[2:6], grad_rows, weights.shape[0])
    return (
        out.reshape(activations.shape),
        input_grad,
        weight_grad,
        summary_mean,
        summary_var,
    )


def solution(mesh):
    placed = (P("img", "row", None, None), P("img", "row", None, None), P(("img", "row")))
    return jax.shard_map(
        per_device,
        mesh=mesh,
        in_specs=placed,
        out_specs=(
            P("img", "row", None, None),
            P("img", "row", None, None),
            P(("img", "row")),
            P(),
            P(),
        ),
        check_vma=False,
    )
```
